32 devices in a mesh: dp: 4 (over y, x), tensor: 8 (over z, core).
Axes of the slice: x: 2, y: 2, z: 4, core: 2. Of those that a mesh axis runs over, the one named last changes fastest.
Arguments:
- tokens: bfloat16 [1024, 2048], P('dp'), may hold values from -6 to 6
- gate_weight: bfloat16 [8, 2048, 2816], P(None, 'dp', 'tensor'), may hold values from -0.25 to 0.25
- up_weight: bfloat16 [8, 2048, 2816], P(None, 'dp', 'tensor'), may hold values from -0.25 to 0.25
- down_weight: bfloat16 [8, 2816, 2048], P(None, 'tensor', 'dp'), may hold values from -0.3125 to 0.3125
- router_weight: float32 [2048, 8], replicated, may hold values from -6 to 6
- carry_mean: float32 [2048], replicated, may hold values from -0.375 to 0.375
Outputs:
- mixed: bfloat16 [1024, 2048], P(('dp', 'tensor'))
The draws below stay inside these ranges and needn't reach their ends.
All inputs are finite; a program needn't handle non-finite values.
Results may differ from the reference program's by a relative error of at most 0.028.
Values may be sent and summed in bfloat16 or wider, within the bound.
No kernel may reach another device: no remote copies, remote signals or barrier semaphores. Data moves between devices by JAX's collectives and lax.ppermute only.
A program may use at most 64 MiB of HBM per device.

```python
import jax
import jax.numpy as jnp
from jax import lax

D = 2048
FF = 2816
EXPERTS = 8
SEG = 256
SEGMENTS = 4
TOKENS = 1024
N_DP = 4
N_TENSOR = 8


def steps_of(key, dims, shards, least, top_value):
    def one(position, shards_of):
        heights = jax.random.uniform(jax.random.fold_in(jax.random.fold_in(key, 6), position), (shards_of,), jnp.float32, least / len(shards), top_value / len(shards))
        return jnp.repeat(jnp.exp(heights), dims[position] // shards_of).reshape((-1,) + (1,) * (len(dims) - position - 1))

    level = one(*shards[0])
    for cut in shards[1:]:
        level = level * one(*cut)
    return level


def scatter_about(key, shape, width, reach, pieces=(), held_as=jnp.bfloat16):
    values = jax.random.normal(key, shape, jnp.float32) * width
    if len(pieces) > 0:
        values = steps_of(key, shape, pieces, -0.22, 0.18) * values
    return jnp.clip(values, min=-reach, max=reach).astype(held_as)


def setup_inputs(seed: int = 0) -> dict:
    key_of = jax.random.split(jax.random.key(seed), 7)
    tokens = scatter_about(key_of[0], (TOKENS, D), 1.0, 6.0, ((0, 4),))
    gate_weight = scatter_about(key_of[1], (EXPERTS, D, FF), (D // 4) ** -0.5, 0.25, ((1, 4), (2, 8)))
    up_weight = scatter_about(key_of[2], (EXPERTS, D, FF), (D // 4) ** -0.5, 0.25, ((1, 4), (2, 8)))
    down_weight = scatter_about(key_of[3], (EXPERTS, FF, D), (FF // 8) ** -0.5, 0.3125, ((1, 8), (2, 4)))
    router_weight = scatter_about(key_of[4], (D, EXPERTS), 1.0, 6.0, (), jnp.float32)
    carry_mean = scatter_about(key_of[5], (D,), 0.0625, 0.375, (), jnp.float32)
    return {"tokens": tokens, "gate_weight": gate_weight, "up_weight": up_weight, "down_weight": down_weight, "router_weight": router_weight, "carry_mean": carry_mean}


soft_cap = 8.0


def merge_rows(probs_row, weight):
    flat = weight.reshape(weight.shape[0], -1)
    merged = jnp.dot(probs_row[None, :], flat, preferred_element_type=jnp.float32)
    return merged.reshape(weight.shape[1:]).astype(jnp.bfloat16)


def blocked_product(left, right, blocks):
    rows, inner = left.shape
    outer = right.shape[1]
    left_blocks = left.astype(jnp.float32).reshape(rows, blocks, inner // blocks)
    right_blocks = right.astype(jnp.float32).reshape(blocks, inner // blocks, outer)
    parts = jnp.einsum('tkr,krf->ktf', left_blocks, right_blocks)
    rounded = lax.optimization_barrier(parts.astype(jnp.bfloat16))
    return jnp.sum(rounded.astype(jnp.float32), axis=0)


def reference(tokens, gate_weight, up_weight, down_weight, router_weight, carry_mean):
    segment_rows = tokens.reshape(SEGMENTS, SEG, D)
    segment_means = jnp.sum(segment_rows.astype(jnp.float32), axis=1) / SEG
    prior_means = jnp.concatenate([carry_mean[None, :], segment_means[:-1]], axis=0)
    raw_logits = jnp.dot(prior_means, router_weight, precision=lax.Precision.HIGHEST, preferred_element_type=jnp.float32)
    logits = soft_cap * jnp.tanh(raw_logits / soft_cap)
    scores = jnp.exp(logits)
    probs = scores / jnp.sum(scores, axis=1, keepdims=True)
    probs_bf = probs.astype(jnp.bfloat16)

    def one_segment(inputs):
        rows, probs_row = inputs
        merged_gate = merge_rows(probs_row, gate_weight)
        merged_up = merge_rows(probs_row, up_weight)
        merged_down = merge_rows(probs_row, down_weight)
        gate = blocked_product(rows, merged_gate, N_DP)
        up = blocked_product(rows, merged_up, N_DP)
        hidden = (jax.nn.silu(gate) * up).astype(jnp.bfloat16)
        mixed = blocked_product(hidden, merged_down, N_TENSOR)
        return mixed.astype(jnp.bfloat16)

    outputs = lax.map(one_segment, (segment_rows, probs_bf))
    return outputs.reshape(TOKENS, D)
```

```python
import functools

import jax
import jax.numpy as jnp
from jax import lax
from jax.experimental import pallas as pl
from jax.experimental.pallas import tpu as pltpu
from jax.sharding import PartitionSpec as P

SEG = 256
SOFT_CAP = 8.0
VMEM = pl.BlockSpec(memory_space=pltpu.VMEM)


def swap(value, axis, step):
    count = lax.axis_size(axis)
    return lax.ppermute(value, axis, [(i, i ^ step) for i in range(count)])


def merge_kernel(block, probs_ref, *refs):
    weights, merged_ref = refs[:-1], refs[-1]
    segs, experts = probs_ref.shape
    cols = weights[0].shape[2]
    spread_row = lax.broadcasted_iota(jnp.int32, (experts, experts * block), 0)
    spread_col = lax.broadcasted_iota(jnp.int32, (experts, experts * block), 1)
    spread = jnp.where(spread_col // block == spread_row, 1.0, 0.0)
    wide = jnp.dot(probs_ref[...], spread, preferred_element_type=jnp.float32)
    place = lax.broadcasted_iota(jnp.int32, (block, experts * block), 1) % block
    row = lax.broadcasted_iota(jnp.int32, (block, experts * block), 0)
    mix = jnp.concatenate(
        [jnp.where(place == row, wide[s : s + 1, :], 0.0) for s in range(segs)], axis=0
    ).astype(jnp.bfloat16)
    at = 0
    for weight in weights:
        for start in range(0, weight.shape[1], block):
            tile = weight[:, start : start + block, :].reshape(experts * block, cols)
            out = jnp.dot(mix, tile, preferred_element_type=jnp.float32).astype(jnp.bfloat16)
            merged_ref[:, at + start : at + start + block, :] = out.reshape(segs, block, cols)
        at += weight.shape[1]


def merge(probs, *weights):
    experts, rows, cols = weights[0].shape
    segs = probs.shape[0]
    block = 32 if rows % 32 == 0 else 16
    total = rows * len(weights)
    return pl.pallas_call(
        functools.partial(merge_kernel, block),
        out_shape=jax.ShapeDtypeStruct((segs, total, cols), jnp.bfloat16),
        in_specs=[VMEM] * (1 + len(weights)),
        out_specs=VMEM,
        compiler_params=pltpu.CompilerParams(vmem_limit_bytes=28 * 2**20),
        cost_estimate=pl.CostEstimate(
            flops=2 * segs * total * cols * experts * block,
            bytes_accessed=2 * total * cols * (experts + segs),
            transcendentals=0,
        ),
    )(probs, *weights)


def preact_kernel(merged_ref, tokens_ref, out_ref):
    for s in range(merged_ref.shape[0]):
        out_ref[s] = lax.dot_general(
            merged_ref[s],
            tokens_ref[s],
            (((1,), (1,)), ((), ())),
            preferred_element_type=jnp.float32,
        ).astype(jnp.bfloat16)


def preact(merged, tokens):
    segs, rows, depth = merged.shape
    cols = tokens.shape[1]
    return pl.pallas_call(
        preact_kernel,
        out_shape=jax.ShapeDtypeStruct((segs, rows, cols), jnp.bfloat16),
        in_specs=[VMEM, VMEM],
        out_specs=VMEM,
        compiler_params=pltpu.CompilerParams(vmem_limit_bytes=28 * 2**20),
        cost_estimate=pl.CostEstimate(
            flops=2 * segs * rows * cols * depth,
            bytes_accessed=2 * segs * (rows * depth + cols * depth + rows * cols),
            transcendentals=0,
        ),
    )(merged, tokens)


def down_kernel(count, mine_ref, *refs):
    parts, downs, out_ref = refs[:count], refs[count : 2 * count], refs[-1]
    own_segs, both, seg = parts[0].shape
    half = both // 2
    cols = downs[0].shape[2]
    for j in range(own_segs):
        total = parts[0][j].astype(jnp.float32)
        for part in parts[1:]:
            total += part[j].astype(jnp.float32)
        gate, up = total[:half], total[half:]
        hidden = (gate / (1.0 + jnp.exp(-gate)) * up).astype(jnp.bfloat16)
        for k in range(count):
            out = lax.dot_general(
                hidden, downs[k][j], (((0,), (0,)), ((), ())), preferred_element_type=jnp.float32
            )
            start = pl.multiple_of((mine_ref[0] ^ k) * cols, 128)
            out_ref[j * seg : (j + 1) * seg, pl.ds(start, cols)] = out.astype(jnp.bfloat16)


def down_product(mine, parts, downs):
    count = len(parts)
    own_segs, both, seg = parts[0].shape
    cols = downs[0].shape[2]
    return pl.pallas_call(
        functools.partial(down_kernel, count),
        out_shape=jax.ShapeDtypeStruct((own_segs * seg, count * cols), jnp.bfloat16),
        in_specs=[pl.BlockSpec(memory_space=pltpu.SMEM)] + [VMEM] * (2 * count),
        out_specs=VMEM,
        compiler_params=pltpu.CompilerParams(vmem_limit_bytes=28 * 2**20),
        cost_estimate=pl.CostEstimate(
            flops=own_segs * seg * both * cols * count,
            bytes_accessed=2 * count * own_segs * (both * seg + both * cols // 2 + seg * cols),
            transcendentals=own_segs * seg * both // 2,
        ),
    )(mine, *parts, *downs)


def on_device(tokens, gate_weight, up_weight, down_weight, router_weight, carry_mean):
    dp = lax.axis_size("dp")
    tensor = lax.axis_size("tensor")
    my_dp = lax.axis_index("dp")
    my_tensor = lax.axis_index("tensor")
    core = my_tensor % 2
    own_rows, width = tokens.shape
    own_segs = own_rows // SEG
    segs = own_segs * dp
    experts, depth, hidden = gate_weight.shape
    gate_t = jnp.swapaxes(gate_weight, 1, 2)
    up_t = jnp.swapaxes(up_weight, 1, 2)

    own_means = jnp.sum(tokens.reshape(own_segs, SEG, width), axis=1, dtype=jnp.float32) / SEG
    own_logits = jnp.dot(
        own_means,
        router_weight,
        precision=lax.Precision.HIGHEST,
        preferred_element_type=jnp.float32,
    )
    carry_logits = jnp.dot(
        carry_mean[None, :],
        router_weight,
        precision=lax.Precision.HIGHEST,
        preferred_element_type=jnp.float32,
    )
    table = jnp.concatenate(
        [own_logits] + [swap(own_logits, "dp", k) for k in range(1, dp)] + [carry_logits], axis=0
    )
    order = jnp.arange(segs, dtype=jnp.int32)
    seg_index = ((order // own_segs) ^ my_dp) * own_segs + order % own_segs
    prior = seg_index - 1
    row = jnp.where(
        seg_index == 0, segs, ((prior // own_segs) ^ my_dp) * own_segs + prior % own_segs
    )
    pick = row[:, None, None] == jnp.arange(segs + 1, dtype=jnp.int32)[None, :, None]
    raw_logits = jnp.sum(jnp.where(pick, table[None], 0.0), axis=1)
    scores = jnp.exp(SOFT_CAP * jnp.tanh(raw_logits / SOFT_CAP))
    probs = (scores / jnp.sum(scores, axis=1, keepdims=True)).astype(jnp.bfloat16)
    probs = probs.astype(jnp.float32)

    half = own_rows // 2
    brought = jnp.stack(
        [
            swap(
                lax.dynamic_slice(tokens, (core * half, (my_dp ^ k) * depth), (half, depth)),
                "dp",
                k,
            )
            for k in range(1, dp)
        ]
    )
    other = swap(brought, "tensor", 1)
    rest = jnp.where(
        core == 0,
        jnp.concatenate([brought, other], axis=1),
        jnp.concatenate([other, brought], axis=1),
    )
    own_block = lax.dynamic_slice(tokens, (0, my_dp * depth), (own_rows, depth))
    rows_in = jnp.concatenate([own_block[None], rest], axis=0).reshape(segs, SEG, depth)

    merged_down = merge(probs, down_weight)
    merged_down = merged_down.reshape(dp, own_segs, hidden, down_weight.shape[2])
    downs = [merged_down[0]] + [swap(merged_down[k], "dp", k) for k in range(1, dp)]

    partial_pre = preact(merge(probs, gate_t, up_t), rows_in)
    partial_pre = partial_pre.reshape(dp, own_segs, 2 * hidden, SEG)
    parts = [partial_pre[0]] + [swap(partial_pre[k], "dp", k) for k in range(1, dp)]

    mixed = down_product(my_dp.reshape(1), parts, downs)

    lines = tensor // 2
    my_line = my_tensor // 2
    mixed = mixed.reshape(lines, 2, own_rows // tensor, width)
    mine = lax.dynamic_index_in_dim(mixed, core, 1, keepdims=False)
    theirs = lax.dynamic_index_in_dim(mixed, 1 - core, 1, keepdims=False)
    pair = mine.astype(jnp.float32) + swap(theirs, "tensor", 1).astype(jnp.float32)
    pair = pair.astype(jnp.bfloat16)
    out = lax.dynamic_index_in_dim(pair, my_line, 0, keepdims=False).astype(jnp.float32)
    for k in range(1, lines):
        piece = lax.dynamic_index_in_dim(pair, my_line ^ k, 0, keepdims=False)
        out = out + swap(piece, "tensor", 2 * k).astype(jnp.float32)
    return out.astype(jnp.bfloat16)


def solution(mesh):
    placed = (
        P("dp", None),
        P(None, "dp", "tensor"),
        P(None, "dp", "tensor"),
        P(None, "tensor", "dp"),
        P(),
        P(),
    )
    return jax.shard_map(
        on_device, mesh=mesh, in_specs=placed, out_specs=P(("dp", "tensor"), None), check_vma=False
    )
```

```python
import functools

import jax
import jax.numpy as jnp
from jax import lax
from jax.experimental import pallas as pl
from jax.experimental.pallas import tpu as pltpu
from jax.sharding import PartitionSpec as P

SEG = 256
SOFT_CAP = 8.0
VMEM = pl.BlockSpec(memory_space=pltpu.VMEM)
SMEM = pl.BlockSpec(memory_space=pltpu.SMEM)
F32 = jnp.float32
BF16 = jnp.bfloat16


def swap(value, axis, step):
    count = lax.axis_size(axis)
    return lax.ppermute(value, axis, [(i, i ^ step) for i in range(count)])


def call(kernel, outs, in_specs, args, flops, moved, scratch=()):
    return pl.pallas_call(
        kernel,
        out_shape=[jax.ShapeDtypeStruct(shape, dtype) for shape, dtype in outs],
        in_specs=in_specs,
        out_specs=[VMEM] * len(outs),
        scratch_shapes=list(scratch),
        compiler_params=pltpu.CompilerParams(vmem_limit_bytes=20 * 2**20),
        cost_estimate=pl.CostEstimate(flops=flops, bytes_accessed=moved, transcendentals=0),
    )(*args)


def prepare_kernel(dp, own_segs, my_dp, core, tokens, router, carry, logits, own, *sends):
    rows, width = tokens.shape
    half, depth = rows // 2, own.shape[1]
    shape = (logits.shape[0], rows)
    member = lax.broadcasted_iota(jnp.int32, shape, 1) // SEG
    ones = jnp.where(member == lax.broadcasted_iota(jnp.int32, shape, 0), 1.0, 0.0).astype(BF16)
    means = jnp.dot(ones, tokens[...], preferred_element_type=F32) / SEG
    place = lax.broadcasted_iota(jnp.int32, means.shape, 0)
    means = jnp.where(place == own_segs, carry[...], means)
    logits[...] = lax.dot_general(
        means,
        router[...],
        (((1,), (1,)), ((), ())),
        precision=lax.Precision.HIGHEST,
        preferred_element_type=F32,
    )
    start = pl.multiple_of(core[0] * half, half)
    for k in range(1, dp):
        column = pl.multiple_of((my_dp[0] ^ k) * depth, depth)
        sends[k - 1][...] = tokens[pl.ds(start, half), pl.ds(column, depth)]
    own[...] = tokens[:, pl.ds(pl.multiple_of(my_dp[0] * depth, depth), depth)]


def spread_probs(my_dp, tables, own_segs, steps, block):
    experts = tables[0].shape[1]
    raws = []
    for k in steps:
        for j in range(own_segs):
            prior = (my_dp ^ k) * own_segs + j - 1
            raw = tables[0][own_segs : own_segs + 1, :]
            for q, table in enumerate(tables):
                for i in range(own_segs):
                    here = (my_dp ^ q) * own_segs + i == prior
                    raw = jnp.where(here, table[i : i + 1, :], raw)
            raws.append(raw)
    logits = SOFT_CAP * jnp.tanh(jnp.concatenate(raws, axis=0) / SOFT_CAP)
    scores = jnp.exp(logits)
    probs = (scores / jnp.sum(scores, axis=1, keepdims=True)).astype(BF16).astype(F32)
    shape = (experts, experts * block)
    ahead = lax.broadcasted_iota(jnp.int32, shape, 1) // block
    spread = jnp.where(ahead == lax.broadcasted_iota(jnp.int32, shape, 0), 1.0, 0.0)
    wide = jnp.dot(probs, spread, preferred_element_type=F32)
    shape = (block, experts * block)
    diagonal = lax.broadcasted_iota(jnp.int32, shape, 1) % block == lax.broadcasted_iota(
        jnp.int32, shape, 0
    )
    return jnp.concatenate(
        [jnp.where(diagonal, wide[s : s + 1, :], 0.0) for s in range(len(raws))], axis=0
    ).astype(BF16)


def merge_kernel(dp, own_segs, steps, block, count, my_dp, *refs):
    tables, weights, outs = refs[:dp], refs[dp : dp + count], refs[-len(steps) :]
    tables = [table[...] for table in tables]
    mix = spread_probs(my_dp[0], tables, own_segs, steps, block)
    experts, rows, cols = weights[0].shape
    for w, weight in enumerate(weights):
        for start in range(0, rows, block):
            tile = weight[:, start : start + block, :].reshape(experts * block, cols)
            out = jnp.dot(mix, tile, preferred_element_type=F32).astype(BF16)
            out = out.reshape(len(steps), own_segs, block, cols)
            at = w * rows + start
            for k in range(len(steps)):
                outs[k][:, at : at + block, :] = out[k]


def merge(my_dp, tables, own_segs, steps, weights, after=()):
    experts, rows, cols = weights[0].shape
    block = 32 if rows % 32 == 0 else 16
    total = rows * len(weights)
    count = len(weights)
    dp = len(tables)

    def kernel(my_dp_ref, *refs):
        merge_kernel(
            dp, own_segs, steps, block, count, my_dp_ref, *refs[: dp + count], *refs[-len(steps) :]
        )

    segs = own_segs * len(steps)
    return call(
        kernel,
        [((own_segs, total, cols), BF16)] * len(steps),
        [SMEM] + [VMEM] * (dp + count) + [pl.BlockSpec(memory_space=pl.ANY)] * len(after),
        (my_dp, *tables, *weights, *after),
        2 * segs * total * cols * experts * block,
        2 * total * cols * (experts + segs),
    )


def preact_kernel(dp, core, own, *refs):
    brought, others, merged, outs = (
        refs[: dp - 1],
        refs[dp - 1 : 2 * dp - 2],
        refs[2 * dp - 2 : 3 * dp - 2],
        refs[3 * dp - 2 : 4 * dp - 2],
    )
    whole = refs[-1]
    half = own.shape[0] // 2
    near = pl.multiple_of(core[0] * half, half)
    far = pl.multiple_of((1 - core[0]) * half, half)
    for k in list(range(dp - 1, -1, -1)):
        if k > 0:
            whole[k - 1, pl.ds(near, half), :] = brought[k - 1][...]
            whole[k - 1, pl.ds(far, half), :] = others[k - 1][...]
        for j in range(merged[k].shape[0]):
            rows = slice(j * SEG, (j + 1) * SEG)
            outs[k][j] = lax.dot_general(
                merged[k][j],
                own[rows, :] if k == 0 else whole[k - 1, rows, :],
                (((1,), (1,)), ((), ())),
                preferred_element_type=F32,
            ).astype(BF16)


def preact(core, own, brought, others, merged):
    dp = len(merged)
    own_segs, total, depth = merged[0].shape
    segs = dp * own_segs
    return call(
        functools.partial(preact_kernel, dp),
        [((own_segs, total, SEG), BF16)] * dp,
        [SMEM] + [VMEM] * (3 * dp - 1),
        (core, own, *brought, *others, *merged),
        2 * segs * total * SEG * depth,
        2 * segs * (total * depth + SEG * depth + total * SEG),
        [pltpu.VMEM((dp - 1, own_segs * SEG, depth), BF16)],
    )


def down_columns(core, hidden, downs, mixed):
    own_segs, cols = downs[0].shape[0], downs[0].shape[2]
    rows = mixed.shape[2]
    for j in range(own_segs):
        for k, down in enumerate(downs):
            out = lax.dot_general(
                hidden[j], down[j], (((0,), (0,)), ((), ())), preferred_element_type=F32
            ).astype(BF16)
            for i in range(SEG // rows):
                at = j * (SEG // rows) + i
                mixed[(at % 2) ^ core, at // 2, :, k * cols : (k + 1) * cols] = out[
                    i * rows : (i + 1) * rows
                ]


def first_kernel(dp, core, *refs):
    parts, downs, (hidden, mixed) = refs[:dp], refs[dp:-2], refs[-2:]
    half = hidden.shape[1]
    kept = []
    for j in range(hidden.shape[0]):
        total = parts[0][j].astype(F32)
        for part in parts[1:]:
            total += part[j].astype(F32)
        gate, up = total[:half], total[half:]
        kept.append((gate / (1.0 + jnp.exp(-gate)) * up).astype(BF16))
        hidden[j] = kept[j]
    down_columns(core[0], kept, downs, mixed)


def second_kernel(core, hidden, *refs):
    down_columns(core[0], hidden, refs[:-1], refs[-1])


def finish_kernel(groups, lines, my_dp, *refs):
    out = refs[-1]
    for g, steps in enumerate(groups):
        pieces = refs[g * lines : (g + 1) * lines]
        cols = pieces[0].shape[1] // len(steps)
        total = pieces[0][...].astype(F32)
        for piece in pieces[1:]:
            total += piece[...].astype(F32)
        total = total.astype(BF16)
        for k, step in enumerate(steps):
            at = pl.multiple_of((my_dp[0] ^ step) * cols, cols)
            out[:, pl.ds(at, cols)] = total[:, k * cols : (k + 1) * cols]


def tensor_sum_pieces(mixed, lines):
    my_line = lax.axis_index("tensor") // 2
    pair = mixed[0].astype(F32) + swap(mixed[1], "tensor", 1).astype(F32)
    pair = pair.astype(BF16)
    pieces = [lax.dynamic_index_in_dim(pair, my_line ^ k, 0, keepdims=False) for k in range(lines)]
    return [pieces[0]] + [swap(pieces[k], "tensor", 2 * k) for k in range(1, lines)]


def on_device(tokens, gate_weight, up_weight, down_weight, router_weight, carry_mean):
    dp = lax.axis_size("dp")
    tensor = lax.axis_size("tensor")
    lines = tensor // 2
    my_dp = lax.axis_index("dp").reshape(1)
    core = (lax.axis_index("tensor") % 2).reshape(1)
    own_rows, width = tokens.shape
    own_segs = own_rows // SEG
    experts, depth, hidden_count = gate_weight.shape
    cols = down_weight.shape[2]
    steps = tuple(range(dp))
    late = tuple(k for k in steps if k.bit_count() == 1)
    early = tuple(k for k in steps if k not in late)

    table_rows = -(-(own_segs + 1) // 8) * 8
    logits, own, *sends = call(
        functools.partial(prepare_kernel, dp, own_segs),
        [((table_rows, experts), F32), ((own_rows, depth), BF16)]
        + [((own_rows // 2, depth), BF16)] * (dp - 1),
        [SMEM, SMEM, VMEM, VMEM, VMEM],
        (my_dp, core, tokens, router_weight.T, carry_mean.reshape(1, width)),
        2 * table_rows * own_rows * width,
        4 * own_rows * width,
    )
    tables = [logits] + [swap(logits, "dp", k) for k in range(1, dp)]
    brought = [swap(sends[k - 1], "dp", k) for k in range(1, dp)]
    others = [swap(piece, "tensor", 1) for piece in brought]

    merged_early = merge(my_dp, tables, own_segs, early, (down_weight,))
    downs = {k: block if k == 0 else swap(block, "dp", k) for k, block in zip(early, merged_early)}

    gate_up = (jnp.swapaxes(gate_weight, 1, 2), jnp.swapaxes(up_weight, 1, 2))
    merged = merge(my_dp, tables, own_segs, steps, gate_up)
    partial_pre = preact(core, own, brought, others, merged)
    parts = [partial_pre[0]] + [swap(partial_pre[k], "dp", k) for k in range(1, dp)]

    merged_late = merge(my_dp, tables, own_segs, late, (down_weight,), (partial_pre[0],))
    for k, block in zip(late, merged_late):
        downs[k] = swap(block, "dp", k)

    rows = own_rows // tensor
    half_flops = own_rows * hidden_count * cols
    hidden, mixed_early = call(
        functools.partial(first_kernel, dp),
        [
            ((own_segs, hidden_count, SEG), BF16),
            ((2, lines, rows, len(early) * cols), BF16),
        ],
        [SMEM] + [VMEM] * (dp + len(early)),
        (core, *parts, *[downs[k] for k in early]),
        2 * half_flops * len(early),
        2 * (own_rows * hidden_count * 3 + hidden_count * cols * len(early)),
    )
    early_pieces = tensor_sum_pieces(mixed_early, lines)
    (mixed_late,) = call(
        second_kernel,
        [((2, lines, rows, len(late) * cols), BF16)],
        [SMEM] + [VMEM] * (1 + len(late)),
        (core, hidden, *[downs[k] for k in late]),
        2 * half_flops * len(late),
        2 * (own_rows * hidden_count + hidden_count * cols * len(late)),
    )
    late_pieces = tensor_sum_pieces(mixed_late, lines)
    (out,) = call(
        functools.partial(finish_kernel, (early, late), lines),
        [((rows, width), BF16)],
        [SMEM] + [VMEM] * (2 * lines),
        (my_dp, *early_pieces, *late_pieces),
        rows * width * lines,
        2 * rows * width * (lines + 1),
    )
    return out


def solution(mesh):
    placed = (
        P("dp", None),
        P(None, "dp", "tensor"),
        P(None, "dp", "tensor"),
        P(None, "tensor", "dp"),
        P(),
        P(),
    )
    return jax.shard_map(
        on_device, mesh=mesh, in_specs=placed, out_specs=P(("dp", "tensor"), None), check_vma=False
    )
```

```python
import functools

import jax
import jax.numpy as jnp
from jax import lax
from jax.experimental import pallas as pl
from jax.experimental.pallas import tpu as pltpu
from jax.sharding import PartitionSpec as P

SEG = 256
SOFT_CAP = 8.0
VMEM = pl.BlockSpec(memory_space=pltpu.VMEM)
SMEM = pl.BlockSpec(memory_space=pltpu.SMEM)
F32 = jnp.float32
BF16 = jnp.bfloat16
LANES = 128
HBM = pl.BlockSpec(memory_space=pltpu.HBM)
ANY = pl.BlockSpec(memory_space=pl.ANY)


def swap(value, axis, step):
    count = lax.axis_size(axis)
    return lax.ppermute(value, axis, [(i, i ^ step) for i in range(count)])


def in_hbm(value):
    return pltpu.with_memory_space_constraint(value, pltpu.HBM)


def call(kernel, outs, in_specs, args, flops, moved, scratch=()):
    return pl.pallas_call(
        kernel,
        out_shape=[jax.ShapeDtypeStruct(shape, dtype) for shape, dtype in outs],
        in_specs=in_specs,
        out_specs=[VMEM] * len(outs),
        scratch_shapes=list(scratch),
        compiler_params=pltpu.CompilerParams(vmem_limit_bytes=24 * 2**20),
        cost_estimate=pl.CostEstimate(flops=flops, bytes_accessed=moved, transcendentals=0),
    )(*args)


def prepare_kernel(dp, own_segs, my_dp, core, tokens, router, carry, own, *refs):
    sends, (blocks, routers, carries, sems) = refs[: dp - 1], refs[dp - 1 :]
    rows, depth = own.shape
    half = rows // 2
    extra = sends[0].shape[0] - half
    experts = router.shape[0]
    columns = [pl.multiple_of((my_dp[0] ^ k) * depth, depth) for k in range(dp)]
    copies = [
        pltpu.make_async_copy(
            tokens.at[:, pl.ds(columns[k], depth)],
            own if k == 0 else blocks.at[k - 1],
            sems.at[k],
        )
        for k in range(dp)
    ]
    copies.append(pltpu.make_async_copy(router, routers, sems.at[dp]))
    copies.append(pltpu.make_async_copy(carry, carries, sems.at[dp + 1]))
    for copy in copies[dp:] + copies[:dp]:
        copy.start()
    member = lax.broadcasted_iota(jnp.int32, (extra, rows), 1) // SEG
    ones = member == lax.broadcasted_iota(jnp.int32, (extra, rows), 0)
    ones = jnp.where(ones, 1.0, 0.0).astype(BF16)
    start = pl.multiple_of(core[0] * half, half)
    copies[dp].wait()
    copies[dp + 1].wait()
    logits = jnp.zeros((extra, experts), F32)
    for k in range(dp):
        copies[k].wait()
        block = own[...] if k == 0 else blocks[k - 1]
        means = jnp.dot(ones, block, preferred_element_type=F32) / SEG
        place = lax.broadcasted_iota(jnp.int32, means.shape, 0)
        means = jnp.where(place == own_segs, carries[:, pl.ds(columns[k], depth)], means)
        logits += lax.dot_general(
            means,
            routers[:, pl.ds(columns[k], depth)],
            (((1,), (1,)), ((), ())),
            precision=lax.Precision.HIGHEST,
            preferred_element_type=F32,
        )
        if k > 0:
            sends[k - 1][:half] = blocks[k - 1, pl.ds(start, half), :]
    lane = lax.broadcasted_iota(jnp.int32, (experts, LANES), 1)
    copied = lane % experts == lax.broadcasted_iota(jnp.int32, (experts, LANES), 0)
    logits = jnp.dot(
        logits,
        jnp.where(copied, 1.0, 0.0),
        precision=lax.Precision.HIGHEST,
        preferred_element_type=F32,
    )
    high = logits.astype(BF16).astype(F32)
    middle = (logits - high).astype(BF16).astype(F32)
    low = logits - high - middle
    lane = lax.broadcasted_iota(jnp.int32, logits.shape, 1)
    terms = jnp.where(lane < experts, high, jnp.where(lane < 2 * experts, middle, low))
    terms = jnp.where(lane < 3 * experts, terms, 0.0).astype(BF16)
    for send in sends:
        send[half:] = jnp.zeros((extra, depth), BF16)
        send[half:, :LANES] = terms


def load_kernel(count, *refs):
    sources, targets, sems = refs[:count], refs[-count - 1 : -1], refs[-1]
    copies = [
        pltpu.make_async_copy(source, target, sems.at[i])
        for i, (source, target) in enumerate(zip(sources, targets))
    ]
    for copy in copies:
        copy.start()
    for copy in copies:
        copy.wait()


def read_table(piece, half, experts):
    lane = lax.broadcasted_iota(jnp.int32, (LANES, experts), 0)
    summed = lane % experts == lax.broadcasted_iota(jnp.int32, (LANES, experts), 1)
    summed = jnp.where(summed & (lane < 3 * experts), 1.0, 0.0).astype(BF16)
    return jnp.dot(piece[half:, :LANES], summed, preferred_element_type=F32)


def spread_probs(my_dp, tables, own_segs, steps, block):
    experts = tables[0].shape[1]
    raws = []
    for k in steps:
        for j in range(own_segs):
            prior = (my_dp ^ k) * own_segs + j - 1
            raw = tables[0][own_segs : own_segs + 1, :]
            for q, table in enumerate(tables):
                for i in range(own_segs):
                    here = (my_dp ^ q) * own_segs + i == prior
                    raw = jnp.where(here, table[i : i + 1, :], raw)
            raws.append(raw)
    logits = SOFT_CAP * jnp.tanh(jnp.concatenate(raws, axis=0) / SOFT_CAP)
    scores = jnp.exp(logits)
    probs = (scores / jnp.sum(scores, axis=1, keepdims=True)).astype(BF16).astype(F32)
    shape = (experts, experts * block)
    ahead = lax.broadcasted_iota(jnp.int32, shape, 1) // block
    spread = jnp.where(ahead == lax.broadcasted_iota(jnp.int32, shape, 0), 1.0, 0.0)
    wide = jnp.dot(probs, spread, preferred_element_type=F32)
    shape = (block, experts * block)
    diagonal = lax.broadcasted_iota(jnp.int32, shape, 1) % block == lax.broadcasted_iota(
        jnp.int32, shape, 0
    )
    return jnp.concatenate(
        [jnp.where(diagonal, wide[s : s + 1, :], 0.0) for s in range(len(raws))], axis=0
    ).astype(BF16)


def route_kernel(dp, own_segs, block, my_dp, sent, *refs):
    pieces, (stacked, mix) = refs[: dp - 1], refs[-2:]
    half = stacked.shape[1]
    for k, piece in enumerate(pieces):
        stacked[k] = piece[:half]
    experts = mix.shape[1] // block
    tables = [read_table(piece, half, experts) for piece in (sent, *pieces)]
    mix[...] = spread_probs(my_dp[0], tables, own_segs, tuple(range(dp)), block)


def merge_kernel(own_segs, mix, *refs):
    weights, outs = refs
    experts, rows, cols = weights[0].shape
    block = mix.shape[1] // experts
    for w, weight in enumerate(weights):
        for start in range(0, rows, block):
            tile = weight[:, start : start + block, :].reshape(experts * block, cols)
            out = jnp.dot(mix[...], tile, preferred_element_type=F32).astype(BF16)
            out = out.reshape(len(outs), own_segs, block, cols)
            at = w * rows + start
            for k in range(len(outs)):
                outs[k][:, at : at + block, :] = out[k]


def merge(mix, dp, own_segs, weights, after=()):
    experts, rows, cols = weights[0].shape
    total = rows * len(weights)
    count = len(weights)

    def kernel(mix_ref, *refs):
        merge_kernel(own_segs, mix_ref, refs[:count], refs[-dp:])

    return call(
        kernel,
        [((own_segs, total, cols), BF16)] * dp,
        [VMEM] * (1 + count) + [ANY] * len(after),
        (mix, *weights, *after),
        2 * mix.size * total * cols // rows,
        2 * total * cols * (experts + dp * own_segs),
    )


def preact_kernel(dp, core, own, *refs):
    brought, other = refs[: dp - 1], refs[dp - 1]
    merged, outs, whole = refs[dp : 2 * dp], refs[2 * dp : 3 * dp], refs[-1]
    half = own.shape[0] // 2
    near = pl.multiple_of(core[0] * half, half)
    far = pl.multiple_of((1 - core[0]) * half, half)
    for k in list(range(dp - 1, -1, -1)):
        if k > 0:
            whole[k - 1, pl.ds(near, half), :] = brought[k - 1][:half]
            whole[k - 1, pl.ds(far, half), :] = other[k - 1]
        for j in range(merged[k].shape[0]):
            rows = slice(j * SEG, (j + 1) * SEG)
            outs[k][j] = lax.dot_general(
                merged[k][j],
                own[rows, :] if k == 0 else whole[k - 1, rows, :],
                (((1,), (1,)), ((), ())),
                preferred_element_type=F32,
            ).astype(BF16)


def preact(core, own, brought, other, merged):
    dp = len(merged)
    own_segs, total, depth = merged[0].shape
    segs = dp * own_segs
    return call(
        functools.partial(preact_kernel, dp),
        [((own_segs, total, SEG), BF16)] * dp,
        [SMEM] + [VMEM] * (2 * dp + 1),
        (core, own, *brought, other, *merged),
        2 * segs * total * SEG * depth,
        2 * segs * (total * depth + SEG * depth + total * SEG),
        [pltpu.VMEM((dp - 1, own_segs * SEG, depth), BF16)],
    )


def down_columns(core, hidden, downs, mixed):
    own_segs, cols = downs[0].shape[0], downs[0].shape[2]
    rows = mixed.shape[2]
    for j in range(own_segs):
        for k, down in enumerate(downs):
            out = lax.dot_general(
                hidden[j], down[j], (((0,), (0,)), ((), ())), preferred_element_type=F32
            ).astype(BF16)
            for i in range(SEG // rows):
                at = j * (SEG // rows) + i
                mixed[(at % 2) ^ core, at // 2, :, k * cols : (k + 1) * cols] = out[
                    i * rows : (i + 1) * rows
                ]


def first_kernel(dp, core, *refs):
    parts, downs, (hidden, mixed) = refs[:dp], refs[dp:-2], refs[-2:]
    half = hidden.shape[1]
    kept = []
    for j in range(hidden.shape[0]):
        total = parts[0][j].astype(F32)
        for part in parts[1:]:
            total += part[j].astype(F32)
        gate, up = total[:half], total[half:]
        kept.append((gate / (1.0 + jnp.exp(-gate)) * up).astype(BF16))
        hidden[j] = kept[j]
    down_columns(core[0], kept, downs, mixed)


def second_kernel(count, core, hidden, *refs):
    down_columns(core[0], hidden, refs[:count], refs[-1])


def finish_kernel(groups, lines, my_dp, *refs):
    out = refs[-1]
    for g, steps in enumerate(groups):
        pieces = refs[g * lines : (g + 1) * lines]
        cols = pieces[0].shape[1] // len(steps)
        total = pieces[0][...].astype(F32)
        for piece in pieces[1:]:
            total += piece[...].astype(F32)
        total = total.astype(BF16)
        for k, step in enumerate(steps):
            at = pl.multiple_of((my_dp[0] ^ step) * cols, cols)
            out[:, pl.ds(at, cols)] = total[:, k * cols : (k + 1) * cols]


def tensor_sum_pieces(mixed, lines):
    my_line = lax.axis_index("tensor") // 2
    pair = mixed[0].astype(F32) + swap(mixed[1], "tensor", 1).astype(F32)
    pair = pair.astype(BF16)
    pieces = [lax.dynamic_index_in_dim(pair, my_line ^ k, 0, keepdims=False) for k in range(lines)]
    return [pieces[0]] + [swap(pieces[k], "tensor", 2 * k) for k in range(1, lines)]


def on_device(tokens, gate_weight, up_weight, down_weight, router_weight, carry_mean):
    dp = lax.axis_size("dp")
    tensor = lax.axis_size("tensor")
    lines = tensor // 2
    my_dp = lax.axis_index("dp").reshape(1)
    core = (lax.axis_index("tensor") % 2).reshape(1)
    own_rows, width = tokens.shape
    own_segs = own_rows // SEG
    experts, depth, hidden_count = gate_weight.shape
    cols = down_weight.shape[2]
    steps = tuple(range(dp))
    segs = dp * own_segs
    late = tuple(k for k in steps if k.bit_count() == 1)
    early = tuple(k for k in steps if k not in late)

    extra = -(-(own_segs + 1) // 16) * 16
    own, *sends = call(
        functools.partial(prepare_kernel, dp, own_segs),
        [((own_rows, depth), BF16)] + [((own_rows // 2 + extra, depth), BF16)] * (dp - 1),
        [SMEM, SMEM, HBM, HBM, HBM],
        (my_dp, core, *map(in_hbm, (tokens, router_weight.T, carry_mean.reshape(1, width)))),
        2 * extra * own_rows * width,
        4 * own_rows * width,
        [
            pltpu.VMEM((dp - 1, own_rows, depth), BF16),
            pltpu.VMEM((experts, width), F32),
            pltpu.VMEM((1, width), F32),
            pltpu.SemaphoreType.DMA((dp + 2,)),
        ],
    )
    brought = [swap(sends[k - 1], "dp", k) for k in range(1, dp)]
    weights = (jnp.swapaxes(gate_weight, 1, 2), jnp.swapaxes(up_weight, 1, 2), down_weight)
    gate_t, up_t, down = call(
        functools.partial(load_kernel, len(weights)),
        [(weight.shape, BF16) for weight in weights],
        [HBM] * len(weights) + [ANY],
        (*[in_hbm(weight) for weight in weights], own),
        0,
        12 * gate_weight.size,
        [pltpu.SemaphoreType.DMA((len(weights),))],
    )
    block = 32 if hidden_count % 32 == 0 else 16
    stacked, mix = call(
        functools.partial(route_kernel, dp, own_segs, block),
        [((dp - 1, own_rows // 2, depth), BF16), ((segs * block, experts * block), BF16)],
        [SMEM] + [VMEM] * dp + [ANY],
        (my_dp, sends[0], *brought, down),
        0,
        2 * own_rows * width,
    )
    other = swap(stacked, "tensor", 1)
    merged = merge(mix, dp, own_segs, (gate_t, up_t))
    partial_pre = preact(core, own, brought, other, merged)
    parts = [partial_pre[0]] + [swap(partial_pre[k], "dp", k) for k in range(1, dp)]

    merged_down = merge(mix, dp, own_segs, (down,), (partial_pre[0],))
    downs = [block if k == 0 else swap(block, "dp", k) for k, block in enumerate(merged_down)]

    rows = own_rows // tensor
    half_flops = own_rows * hidden_count * cols
    hidden, mixed_early = call(
        functools.partial(first_kernel, dp),
        [
            ((own_segs, hidden_count, SEG), BF16),
            ((2, lines, rows, len(early) * cols), BF16),
        ],
        [SMEM] + [VMEM] * (dp + len(early)),
        (core, *parts, *[downs[k] for k in early]),
        2 * half_flops * len(early),
        2 * (own_rows * hidden_count * 3 + hidden_count * cols * len(early)),
    )
    early_pieces = tensor_sum_pieces(mixed_early, lines)
    (mixed_late,) = call(
        functools.partial(second_kernel, len(late)),
        [((2, lines, rows, len(late) * cols), BF16)],
        [SMEM] + [VMEM] * (1 + len(late)) + [ANY],
        (core, hidden, *[downs[k] for k in late], early_pieces[0]),
        2 * half_flops * len(late),
        2 * (own_rows * hidden_count + hidden_count * cols * len(late)),
    )
    late_pieces = tensor_sum_pieces(mixed_late, lines)
    (out,) = call(
        functools.partial(finish_kernel, (early, late), lines),
        [((rows, width), BF16)],
        [SMEM] + [VMEM] * (2 * lines),
        (my_dp, *early_pieces, *late_pieces),
        rows * width * lines,
        2 * rows * width * (lines + 1),
    )
    return out


def solution(mesh):
    placed = (
        P("dp", None),
        P(None, "dp", "tensor"),
        P(None, "dp", "tensor"),
        P(None, "tensor", "dp"),
        P(),
        P(),
    )
    return jax.shard_map(
        on_device, mesh=mesh, in_specs=placed, out_specs=P(("dp", "tensor"), None), check_vma=False
    )
```

```python
import functools

import jax
import jax.numpy as jnp
from jax import lax
from jax.experimental import pallas as pl
from jax.experimental.pallas import tpu as pltpu
from jax.sharding import PartitionSpec as P

SEG = 256
SOFT_CAP = 8.0
VMEM = pl.BlockSpec(memory_space=pltpu.VMEM)
SMEM = pl.BlockSpec(memory_space=pltpu.SMEM)
F32 = jnp.float32
BF16 = jnp.bfloat16
LANES = 128
HBM = pl.BlockSpec(memory_space=pltpu.HBM)
ANY = pl.BlockSpec(memory_space=pl.ANY)


def swap(value, axis, step):
    count = lax.axis_size(axis)
    return lax.ppermute(value, axis, [(i, i ^ step) for i in range(count)])


def in_hbm(value):
    return pltpu.with_memory_space_constraint(value, pltpu.HBM)


def call(kernel, outs, in_specs, args, flops, moved, scratch=()):
    return pl.pallas_call(
        kernel,
        out_shape=[jax.ShapeDtypeStruct(shape, dtype) for shape, dtype in outs],
        in_specs=in_specs,
        out_specs=[VMEM] * len(outs),
        scratch_shapes=list(scratch),
        compiler_params=pltpu.CompilerParams(vmem_limit_bytes=24 * 2**20),
        cost_estimate=pl.CostEstimate(flops=flops, bytes_accessed=moved, transcendentals=0),
    )(*args)


def prepare_kernel(dp, own_segs, my_dp, core, tokens, router, carry, own, *refs):
    sends, (blocks, routers, carries, sems) = refs[: dp - 1], refs[dp - 1 :]
    rows, depth = own.shape
    half = rows // 2
    extra = sends[0].shape[0] - half
    experts = router.shape[0]
    columns = [pl.multiple_of((my_dp[0] ^ k) * depth, depth) for k in range(dp)]
    copies = [
        pltpu.make_async_copy(
            tokens.at[:, pl.ds(columns[k], depth)],
            own if k == 0 else blocks.at[k - 1],
            sems.at[k],
        )
        for k in range(dp)
    ]
    copies.append(pltpu.make_async_copy(router, routers, sems.at[dp]))
    copies.append(pltpu.make_async_copy(carry, carries, sems.at[dp + 1]))
    for copy in copies[dp:] + copies[:dp]:
        copy.start()
    member = lax.broadcasted_iota(jnp.int32, (extra, rows), 1) // SEG
    ones = member == lax.broadcasted_iota(jnp.int32, (extra, rows), 0)
    ones = jnp.where(ones, 1.0, 0.0).astype(BF16)
    start = pl.multiple_of(core[0] * half, half)
    copies[dp].wait()
    copies[dp + 1].wait()
    logits = jnp.zeros((extra, experts), F32)
    for k in range(dp):
        copies[k].wait()
        block = own[...] if k == 0 else blocks[k - 1]
        means = jnp.dot(ones, block, preferred_element_type=F32) / SEG
        place = lax.broadcasted_iota(jnp.int32, means.shape, 0)
        means = jnp.where(place == own_segs, carries[:, pl.ds(columns[k], depth)], means)
        logits += lax.dot_general(
            means,
            routers[:, pl.ds(columns[k], depth)],
            (((1,), (1,)), ((), ())),
            precision=lax.Precision.HIGHEST,
            preferred_element_type=F32,
        )
        if k > 0:
            sends[k - 1][:half] = blocks[k - 1, pl.ds(start, half), :]
    lane = lax.broadcasted_iota(jnp.int32, (experts, LANES), 1)
    copied = lane % experts == lax.broadcasted_iota(jnp.int32, (experts, LANES), 0)
    logits = jnp.dot(
        logits,
        jnp.where(copied, 1.0, 0.0),
        precision=lax.Precision.HIGHEST,
        preferred_element_type=F32,
    )
    high = logits.astype(BF16).astype(F32)
    middle = (logits - high).astype(BF16).astype(F32)
    low = logits - high - middle
    lane = lax.broadcasted_iota(jnp.int32, logits.shape, 1)
    terms = jnp.where(lane < experts, high, jnp.where(lane < 2 * experts, middle, low))
    terms = jnp.where(lane < 3 * experts, terms, 0.0).astype(BF16)
    for send in sends:
        send[half:] = jnp.zeros((extra, depth), BF16)
        send[half:, :LANES] = terms


def load_kernel(count, *refs):
    sources, targets, sems = refs[:count], refs[-count - 1 : -1], refs[-1]
    copies = [
        pltpu.make_async_copy(source, target, sems.at[i])
        for i, (source, target) in enumerate(zip(sources, targets))
    ]
    for copy in copies:
        copy.start()
    for copy in copies:
        copy.wait()


def read_table(piece, half, experts):
    lane = lax.broadcasted_iota(jnp.int32, (LANES, experts), 0)
    summed = lane % experts == lax.broadcasted_iota(jnp.int32, (LANES, experts), 1)
    summed = jnp.where(summed & (lane < 3 * experts), 1.0, 0.0).astype(BF16)
    return jnp.dot(piece[half:, :LANES], summed, preferred_element_type=F32)


def spread_probs(my_dp, tables, own_segs, steps, block):
    experts = tables[0].shape[1]
    raws = []
    for k in steps:
        for j in range(own_segs):
            prior = (my_dp ^ k) * own_segs + j - 1
            raw = tables[0][own_segs : own_segs + 1, :]
            for q, table in enumerate(tables):
                for i in range(own_segs):
                    here = (my_dp ^ q) * own_segs + i == prior
                    raw = jnp.where(here, table[i : i + 1, :], raw)
            raws.append(raw)
    logits = SOFT_CAP * jnp.tanh(jnp.concatenate(raws, axis=0) / SOFT_CAP)
    scores = jnp.exp(logits)
    probs = (scores / jnp.sum(scores, axis=1, keepdims=True)).astype(BF16).astype(F32)
    shape = (experts, experts * block)
    ahead = lax.broadcasted_iota(jnp.int32, shape, 1) // block
    spread = jnp.where(ahead == lax.broadcasted_iota(jnp.int32, shape, 0), 1.0, 0.0)
    wide = jnp.dot(probs, spread, preferred_element_type=F32)
    shape = (block, experts * block)
    diagonal = lax.broadcasted_iota(jnp.int32, shape, 1) % block == lax.broadcasted_iota(
        jnp.int32, shape, 0
    )
    return jnp.concatenate(
        [jnp.where(diagonal, wide[s : s + 1, :], 0.0) for s in range(len(raws))], axis=0
    ).astype(BF16)


def route_kernel(dp, own_segs, block, my_dp, sent, *refs):
    pieces, (stacked, mix) = refs[: dp - 1], refs[-2:]
    half = stacked.shape[1]
    for k, piece in enumerate(pieces):
        stacked[k] = piece[:half]
    experts = mix.shape[1] // block
    tables = [read_table(piece, half, experts) for piece in (sent, *pieces)]
    mix[...] = spread_probs(my_dp[0], tables, own_segs, tuple(range(dp)), block)


def merge_kernel(own_segs, mix, *refs):
    weights, outs = refs
    experts, rows, cols = weights[0].shape
    block = mix.shape[1] // experts
    for w, weight in enumerate(weights):
        for start in range(0, rows, block):
            tile = weight[:, start : start + block, :].reshape(experts * block, cols)
            out = jnp.dot(mix[...], tile, preferred_element_type=F32).astype(BF16)
            out = out.reshape(len(outs), own_segs, block, cols)
            at = w * rows + start
            for k in range(len(outs)):
                outs[k][:, at : at + block, :] = out[k]


def merge(mix, dp, own_segs, weights):
    experts, rows, cols = weights[0].shape
    total = rows * len(weights)
    count = len(weights)

    def kernel(mix_ref, *refs):
        merge_kernel(own_segs, mix_ref, refs[:count], refs[-dp:])

    return call(
        kernel,
        [((own_segs, total, cols), BF16)] * dp,
        [VMEM] * (1 + count),
        (mix, *weights),
        2 * mix.size * total * cols // rows,
        2 * total * cols * (experts + dp * own_segs),
    )


def preact_kernel(dp, core, own, *refs):
    brought, other = refs[: dp - 1], refs[dp - 1]
    merged, outs, whole = refs[dp : 2 * dp], refs[2 * dp : 3 * dp], refs[-1]
    half = own.shape[0] // 2
    near = pl.multiple_of(core[0] * half, half)
    far = pl.multiple_of((1 - core[0]) * half, half)
    for k in list(range(dp - 1, -1, -1)):
        if k > 0:
            whole[k - 1, pl.ds(near, half), :] = brought[k - 1][:half]
            whole[k - 1, pl.ds(far, half), :] = other[k - 1]
        for j in range(merged[k].shape[0]):
            rows = slice(j * SEG, (j + 1) * SEG)
            outs[k][j] = lax.dot_general(
                merged[k][j],
                own[rows, :] if k == 0 else whole[k - 1, rows, :],
                (((1,), (1,)), ((), ())),
                preferred_element_type=F32,
            ).astype(BF16)


def preact(core, own, brought, other, merged):
    dp = len(merged)
    own_segs, total, depth = merged[0].shape
    segs = dp * own_segs
    return call(
        functools.partial(preact_kernel, dp),
        [((own_segs, total, SEG), BF16)] * dp,
        [SMEM] + [VMEM] * (2 * dp + 1),
        (core, own, *brought, other, *merged),
        2 * segs * total * SEG * depth,
        2 * segs * (total * depth + SEG * depth + total * SEG),
        [pltpu.VMEM((dp - 1, own_segs * SEG, depth), BF16)],
    )


def down_kernel(dp, core, *refs):
    parts, downs, mixed = refs[:dp], refs[dp:-1], refs[-1]
    own_segs, half, cols = downs[0].shape
    rows = mixed.shape[2]
    for j in range(own_segs):
        total = parts[0][j].astype(F32)
        for part in parts[1:]:
            total += part[j].astype(F32)
        gate, up = total[:half], total[half:]
        hidden = (gate / (1.0 + jnp.exp(-gate)) * up).astype(BF16)
        for k, down in enumerate(downs):
            out = lax.dot_general(
                hidden, down[j], (((0,), (0,)), ((), ())), preferred_element_type=F32
            ).astype(BF16)
            for i in range(SEG // rows):
                at = j * (SEG // rows) + i
                mixed[(at % 2) ^ core[0], at // 2, :, k * cols : (k + 1) * cols] = out[
                    i * rows : (i + 1) * rows
                ]


def finish_kernel(dp, my_dp, *refs):
    pieces, out = refs[:-1], refs[-1]
    cols = out.shape[1] // dp
    total = pieces[0][...].astype(F32)
    for piece in pieces[1:]:
        total += piece[...].astype(F32)
    total = total.astype(BF16)
    for k in range(dp):
        at = pl.multiple_of((my_dp[0] ^ k) * cols, cols)
        out[:, pl.ds(at, cols)] = total[:, k * cols : (k + 1) * cols]


def tensor_sum_pieces(mixed, lines):
    my_line = lax.axis_index("tensor") // 2
    pair = mixed[0].astype(F32) + swap(mixed[1], "tensor", 1).astype(F32)
    pair = pair.astype(BF16)
    pieces = [lax.dynamic_index_in_dim(pair, my_line ^ k, 0, keepdims=False) for k in range(lines)]
    return [pieces[0]] + [swap(pieces[k], "tensor", 2 * k) for k in range(1, lines)]


def on_device(tokens, gate_weight, up_weight, down_weight, router_weight, carry_mean):
    dp = lax.axis_size("dp")
    tensor = lax.axis_size("tensor")
    lines = tensor // 2
    my_dp = lax.axis_index("dp").reshape(1)
    core = (lax.axis_index("tensor") % 2).reshape(1)
    own_rows, width = tokens.shape
    own_segs = own_rows // SEG
    experts, depth, hidden_count = gate_weight.shape
    cols = down_weight.shape[2]
    segs = dp * own_segs
    return call(
        functools.partial(preact_kernel, dp),
        [((own_segs, total, SEG), BF16)] * dp,
        [SMEM] + [VMEM] * (2 * dp + 1),
        (core, own, *brought, other, *merged),
        2 * segs * total * SEG * depth,
        2 * segs * (total * depth + SEG * depth + total * SEG),
        [pltpu.VMEM((dp - 1, own_segs * SEG, depth), BF16)],
    )


def down_kernel(dp, core, *refs):
    parts, downs, mixed = refs[:dp], refs[dp:-1], refs[-1]
    own_segs, half, cols = downs[0].shape
    rows = mixed.shape[2]
    for j in range(own_segs):
        total = parts[0][j].astype(F32)
        for part in parts[1:]:
            total += part[j].astype(F32)
        gate, up = total[:half], total[half:]
        hidden = (gate / (1.0 + jnp.exp(-gate)) * up).astype(BF16)
        for k, down in enumerate(downs):
            out = lax.dot_general(
                hidden, down[j], (((0,), (0,)), ((), ())), preferred_element_type=F32
            ).astype(BF16)
            for i in range(SEG // rows):
                at = j * (SEG // rows) + i
                mixed[(at % 2) ^ core[0], at // 2, :, k * cols : (k + 1) * cols] = out[
                    i * rows : (i + 1) * rows
                ]


def finish_kernel(dp, my_dp, *refs):
    pieces, out = refs[:-1], refs[-1]
    cols = out.shape[1] // dp
    total = pieces[0][...].astype(F32)
    for piece in pieces[1:]:
        total += piece[...].astype(F32)
    total = total.astype(BF16)
    for k in range(dp):
        at = pl.multiple_of((my_dp[0] ^ k) * cols, cols)
        out[:, pl.ds(at, cols)] = total[:, k * cols : (k + 1) * cols]


def tensor_sum_pieces(mixed, lines):
    my_line = lax.axis_index("tensor") // 2
    pair = mixed[0].astype(F32) + swap(mixed[1], "tensor", 1).astype(F32)
    pair = pair.astype(BF16)
    pieces = [lax.dynamic_index_in_dim(pair, my_line ^ k, 0, keepdims=False) for k in range(lines)]
    return [pieces[0]] + [swap(pieces[k], "tensor", 2 * k) for k in range(1, lines)]


def on_device(tokens, gate_weight, up_weight, down_weight, router_weight, carry_mean):
    dp = lax.axis_size("dp")
    tensor = lax.axis_size("tensor")
    lines = tensor // 2
    my_dp = lax.axis_index("dp").reshape(1)
    core = (lax.axis_index("tensor") % 2).reshape(1)
    own_rows, width = tokens.shape
    own_segs = own_rows // SEG
    experts, depth, hidden_count = gate_weight.shape
    cols = down_weight.shape[2]
    steps = tuple(range(dp))
    segs = dp * own_segs
    late = tuple(k for k in steps if k.bit_count() == 1)
    early = tuple(k for k in steps if k not in late)

    extra = -(-(own_segs + 1) // 16) * 16
    own, *sends = call(
        functools.partial(prepare_kernel, dp, own_segs),
        [((own_rows, depth), BF16)] + [((own_rows // 2 + extra, depth), BF16)] * (dp - 1),
        [SMEM, SMEM, HBM, HBM, HBM],
        (my_dp, core, *map(in_hbm, (tokens, router_weight.T, carry_mean.reshape(1, width)))),
        2 * extra * own_rows * width,
        4 * own_rows * width,
        [
            pltpu.VMEM((dp - 1, own_rows, depth), BF16),
            pltpu.VMEM((experts, width), F32),
            pltpu.VMEM((1, width), F32),
            pltpu.SemaphoreType.DMA((dp + 2,)),
        ],
    )
    brought = [swap(sends[k - 1], "dp", k) for k in range(1, dp)]
    weights = (jnp.swapaxes(gate_weight, 1, 2), jnp.swapaxes(up_weight, 1, 2), down_weight)
    gate_t, up_t, down = call(
        functools.partial(load_kernel, len(weights)),
        [(weight.shape, BF16) for weight in weights],
        [HBM] * len(weights) + [ANY],
        (*[in_hbm(weight) for weight in weights], own),
        0,
        12 * gate_weight.size,
        [pltpu.SemaphoreType.DMA((len(weights),))],
    )
    block = 32 if hidden_count % 32 == 0 else 16
    stacked, mix = call(
        functools.partial(route_kernel, dp, own_segs, block),
        [((dp - 1, own_rows // 2, depth), BF16), ((segs * block, experts * block), BF16)],
        [SMEM] + [VMEM] * dp + [ANY],
        (my_dp, sends[0], *brought, down),
        0,
        2 * own_rows * width,
    )
    other = swap(stacked, "tensor", 1)
    merged_down = merge(mix, dp, own_segs, (down,))
    downs = [block if k == 0 else swap(block, "dp", k) for k, block in enumerate(merged_down)]
    merged = merge(mix, dp, own_segs, (gate_t, up_t))
    partial_pre = preact(core, own, brought, other, merged)
    parts = [partial_pre[0]] + [swap(partial_pre[k], "dp", k) for k in range(1, dp)]


    rows = own_rows // tensor
    (mixed,) = call(
        functools.partial(down_kernel, dp),
        [((2, lines, rows, width), BF16)],
        [SMEM] + [VMEM] * (2 * dp),
        (core, *parts, *downs),
        2 * own_rows * hidden_count * width,
        2 * (own_rows * hidden_count * dp * 2 + hidden_count * width),
    )
    pieces = tensor_sum_pieces(mixed, lines)
    (out,) = call(
        functools.partial(finish_kernel, dp),
        [((rows, width), BF16)],
        [SMEM] + [VMEM] * lines,
        (my_dp, *pieces),
        rows * width * lines,
        2 * rows * width * (lines + 1),
    )
    return out


def solution(mesh):
    placed = (
        P("dp", None),
        P(None, "dp", "tensor"),
        P(None, "dp", "tensor"),
        P(None, "tensor", "dp"),
        P(),
        P(),
    )
    return jax.shard_map(
        on_device, mesh=mesh, in_specs=placed, out_specs=P(("dp", "tensor"), None), check_vma=False
    )
```

```python
import functools

import jax
import jax.numpy as jnp
from jax import lax
from jax.experimental import pallas as pl
from jax.experimental.pallas import tpu as pltpu
from jax.sharding import PartitionSpec as P

SEG = 256
SOFT_CAP = 8.0
VMEM = pl.BlockSpec(memory_space=pltpu.VMEM)
SMEM = pl.BlockSpec(memory_space=pltpu.SMEM)
F32 = jnp.float32
BF16 = jnp.bfloat16
LANES = 128
HBM = pl.BlockSpec(memory_space=pltpu.HBM)
ANY = pl.BlockSpec(memory_space=pl.ANY)


def swap(value, axis, step):
    count = lax.axis_size(axis)
    return lax.ppermute(value, axis, [(i, i ^ step) for i in range(count)])


def in_hbm(value):
    return pltpu.with_memory_space_constraint(value, pltpu.HBM)


def call(kernel, outs, in_specs, args, flops, moved, scratch=()):
    return pl.pallas_call(
        kernel,
        out_shape=[jax.ShapeDtypeStruct(shape, dtype) for shape, dtype in outs],
        in_specs=in_specs,
        out_specs=[VMEM] * len(outs),
        scratch_shapes=list(scratch),
        compiler_params=pltpu.CompilerParams(vmem_limit_bytes=24 * 2**20),
        cost_estimate=pl.CostEstimate(flops=flops, bytes_accessed=moved, transcendentals=0),
    )(*args)


def prepare_kernel(dp, own_segs, my_dp, core, tokens, router, carry, own, *refs):
    sends, (blocks, routers, carries, sems) = refs[: dp - 1], refs[dp - 1 :]
    rows, depth = own.shape
    half = rows // 2
    extra = sends[0].shape[0] - half
    experts = router.shape[0]
    columns = [pl.multiple_of((my_dp[0] ^ k) * depth, depth) for k in range(dp)]
    copies = [
        pltpu.make_async_copy(
            tokens.at[:, pl.ds(columns[k], depth)],
            own if k == 0 else blocks.at[k - 1],
            sems.at[k],
        )
        for k in range(dp)
    ]
    copies.append(pltpu.make_async_copy(router, routers, sems.at[dp]))
    copies.append(pltpu.make_async_copy(carry, carries, sems.at[dp + 1]))
    for copy in copies[dp:] + copies[:dp]:
        copy.start()
    member = lax.broadcasted_iota(jnp.int32, (extra, rows), 1) // SEG
    ones = member == lax.broadcasted_iota(jnp.int32, (extra, rows), 0)
    ones = jnp.where(ones, 1.0, 0.0).astype(BF16)
    start = pl.multiple_of(core[0] * half, half)
    for copy in copies:
        copy.wait()
    totals = [jnp.zeros((experts, depth), F32)] * (own_segs + 1)
    for k in range(dp):
        block = own[...] if k == 0 else blocks[k - 1]
        weight = routers[:, pl.ds(columns[k], depth)]
        means = jnp.dot(ones, block, preferred_element_type=F32) / SEG
        for j in range(own_segs):
            totals[j] += means[j : j + 1, :] * weight
        totals[own_segs] += carries[:, pl.ds(columns[k], depth)] * weight
        if k > 0:
            sends[k - 1][:half] = blocks[k - 1, pl.ds(start, half), :]
    lane = lax.broadcasted_iota(jnp.int32, (experts, LANES), 1)
    place = lane % experts == lax.broadcasted_iota(jnp.int32, (experts, LANES), 0)
    row = lax.broadcasted_iota(jnp.int32, (extra, LANES), 0)
    lane = lax.broadcasted_iota(jnp.int32, (extra, LANES), 1)
    logits = jnp.zeros((extra, LANES), F32)
    for j, total in enumerate(totals):
        column = jnp.sum(total, axis=1, keepdims=True)
        spread = jnp.sum(jnp.where(place, column, 0.0), axis=0, keepdims=True)
        logits = jnp.where(row == j, spread, logits)
    high = logits.astype(BF16).astype(F32)
    middle = (logits - high).astype(BF16).astype(F32)
    low = logits - high - middle
    terms = jnp.where(lane < experts, high, jnp.where(lane < 2 * experts, middle, low))
    terms = jnp.where(lane < 3 * experts, terms, 0.0).astype(BF16)
    for send in sends:
        send[half:] = jnp.zeros((extra, depth), BF16)
        send[half:, :LANES] = terms


def load_kernel(count, *refs):
    sources, targets, sems = refs[:count], refs[-count - 1 : -1], refs[-1]
    copies = [
        pltpu.make_async_copy(source, target, sems.at[i])
        for i, (source, target) in enumerate(zip(sources, targets))
    ]
    for copy in copies:
        copy.start()
    for copy in copies:
        copy.wait()


def read_table(piece, half, experts):
    lane = lax.broadcasted_iota(jnp.int32, (LANES, experts), 0)
    summed = lane % experts == lax.broadcasted_iota(jnp.int32, (LANES, experts), 1)
    summed = jnp.where(summed & (lane < 3 * experts), 1.0, 0.0).astype(BF16)
    return jnp.dot(piece[half:, :LANES], summed, preferred_element_type=F32)


def spread_probs(my_dp, tables, own_segs, steps, block):
    experts = tables[0].shape[1]
    raws = []
    for k in steps:
        for j in range(own_segs):
            prior = (my_dp ^ k) * own_segs + j - 1
            raw = tables[0][own_segs : own_segs + 1, :]
            for q, table in enumerate(tables):
                for i in range(own_segs):
                    here = (my_dp ^ q) * own_segs + i == prior
                    raw = jnp.where(here, table[i : i + 1, :], raw)
            raws.append(raw)
    logits = SOFT_CAP * jnp.tanh(jnp.concatenate(raws, axis=0) / SOFT_CAP)
    scores = jnp.exp(logits)
    probs = (scores / jnp.sum(scores, axis=1, keepdims=True)).astype(BF16).astype(F32)
    shape = (experts, experts * block)
    ahead = lax.broadcasted_iota(jnp.int32, shape, 1) // block
    spread = jnp.where(ahead == lax.broadcasted_iota(jnp.int32, shape, 0), 1.0, 0.0)
    wide = jnp.dot(probs, spread, preferred_element_type=F32)
    shape = (block, experts * block)
    diagonal = lax.broadcasted_iota(jnp.int32, shape, 1) % block == lax.broadcasted_iota(
        jnp.int32, shape, 0
    )
    return jnp.concatenate(
        [jnp.where(diagonal, wide[s : s + 1, :], 0.0) for s in range(len(raws))], axis=0
    ).astype(BF16)


def route_kernel(dp, own_segs, block, my_dp, sent, *refs):
    pieces, (stacked, mix) = refs[: dp - 1], refs[-2:]
    half = stacked.shape[1]
    for k, piece in enumerate(pieces):
        stacked[k] = piece[:half]
    experts = mix.shape[1] // block
    tables = [read_table(piece, half, experts) for piece in (sent, *pieces)]
    mix[...] = spread_probs(my_dp[0], tables, own_segs, tuple(range(dp)), block)


def merge_kernel(own_segs, mix, *refs):
    weights, outs = refs
    experts, rows, cols = weights[0].shape
    block = mix.shape[1] // experts
    for w, weight in enumerate(weights):
        for start in range(0, rows, block):
            tile = weight[:, start : start + block, :].reshape(experts * block, cols)
            out = jnp.dot(mix[...], tile, preferred_element_type=F32).astype(BF16)
            out = out.reshape(len(outs), own_segs, block, cols)
            at = w * rows + start
            for k in range(len(outs)):
                outs[k][:, at : at + block, :] = out[k]


def merge(mix, dp, own_segs, weights):
    experts, rows, cols = weights[0].shape
    total = rows * len(weights)
    count = len(weights)

    def kernel(mix_ref, *refs):
        merge_kernel(own_segs, mix_ref, refs[:count], refs[-dp:])

    return call(
        kernel,
        [((own_segs, total, cols), BF16)] * dp,
        [VMEM] * (1 + count),
        (mix, *weights),
        2 * mix.size * total * cols // rows,
        2 * total * cols * (experts + dp * own_segs),
    )


def preact_kernel(dp, core, own, *refs):
    brought, other = refs[: dp - 1], refs[dp - 1]
    merged, outs, whole = refs[dp : 2 * dp], refs[2 * dp : 3 * dp], refs[-1]
    half = own.shape[0] // 2
    near = pl.multiple_of(core[0] * half, half)
    far = pl.multiple_of((1 - core[0]) * half, half)
    for k in list(range(dp - 1, -1, -1)):
        if k > 0:
            whole[k - 1, pl.ds(near, half), :] = brought[k - 1][:half]
            whole[k - 1, pl.ds(far, half), :] = other[k - 1]
        for j in range(merged[k].shape[0]):
            rows = slice(j * SEG, (j + 1) * SEG)
            outs[k][j] = lax.dot_general(
                merged[k][j],
                own[rows, :] if k == 0 else whole[k - 1, rows, :],
                (((1,), (1,)), ((), ())),
                preferred_element_type=F32,
            ).astype(BF16)


def preact(core, own, brought, other, merged):
    dp = len(merged)
    own_segs, total, depth = merged[0].shape
    segs = dp * own_segs
    return call(
        functools.partial(preact_kernel, dp),
        [((own_segs, total, SEG), BF16)] * dp,
        [SMEM] + [VMEM] * (2 * dp + 1),
        (core, own, *brought, other, *merged),
        2 * segs * total * SEG * depth,
        2 * segs * (total * depth + SEG * depth + total * SEG),
        [pltpu.VMEM((dp - 1, own_segs * SEG, depth), BF16)],
    )


def down_kernel(dp, core, *refs):
    parts, downs, mixed = refs[:dp], refs[dp:-1], refs[-1]
    own_segs, half, cols = downs[0].shape
    rows = mixed.shape[2]
    for j in range(own_segs):
        total = parts[0][j].astype(F32)
        for part in parts[1:]:
            total += part[j].astype(F32)
        gate, up = total[:half], total[half:]
        hidden = (gate / (1.0 + jnp.exp(-gate)) * up).astype(BF16)
        for k, down in enumerate(downs):
            out = lax.dot_general(
                hidden, down[j], (((0,), (0,)), ((), ())), preferred_element_type=F32
            ).astype(BF16)
            for i in range(SEG // rows):
                at = j * (SEG // rows) + i
                mixed[(at % 2) ^ core[0], at // 2, :, k * cols : (k + 1) * cols] = out[
                    i * rows : (i + 1) * rows
                ]


def finish_kernel(dp, my_dp, *refs):
    pieces, out = refs[:-1], refs[-1]
    cols = out.shape[1] // dp
    total = pieces[0][...].astype(F32)
    for piece in pieces[1:]:
        total += piece[...].astype(F32)
    total = total.astype(BF16)
    for k in range(dp):
        at = pl.multiple_of((my_dp[0] ^ k) * cols, cols)
        out[:, pl.ds(at, cols)] = total[:, k * cols : (k + 1) * cols]


def tensor_sum_pieces(mixed, lines):
    my_line = lax.axis_index("tensor") // 2
    pair = mixed[0].astype(F32) + swap(mixed[1], "tensor", 1).astype(F32)
    pair = pair.astype(BF16)
    pieces = [lax.dynamic_index_in_dim(pair, my_line ^ k, 0, keepdims=False) for k in range(lines)]
    return [swap(pieces[k], "tensor", 2 * k) for k in range(lines - 1, 0, -1)] + [pieces[0]]


def on_device(tokens, gate_weight, up_weight, down_weight, router_weight, carry_mean):
    dp = lax.axis_size("dp")
    tensor = lax.axis_size("tensor")
    lines = tensor // 2
    my_dp = lax.axis_index("dp").reshape(1)
    core = (lax.axis_index("tensor") % 2).reshape(1)
    own_rows, width = tokens.shape
    own_segs = own_rows // SEG
    experts, depth, hidden_count = gate_weight.shape
    cols = down_weight.shape[2]
    segs = dp * own_segs

    extra = -(-(own_segs + 1) // 16) * 16
    own, *sends = call(
        functools.partial(prepare_kernel, dp, own_segs),
        [((own_rows, depth), BF16)] + [((own_rows // 2 + extra, depth), BF16)] * (dp - 1),
        [SMEM, SMEM, HBM, HBM, HBM],
        (my_dp, core, *map(in_hbm, (tokens, router_weight.T, carry_mean.reshape(1, width)))),
        2 * extra * own_rows * width,
        4 * own_rows * width,
        [
            pltpu.VMEM((dp - 1, own_rows, depth), BF16),
            pltpu.VMEM((experts, width), F32),
            pltpu.VMEM((1, width), F32),
            pltpu.SemaphoreType.DMA((dp + 2,)),
        ],
    )
    brought = [swap(sends[k - 1], "dp", k) for k in range(1, dp)]
    weights = (jnp.swapaxes(gate_weight, 1, 2), jnp.swapaxes(up_weight, 1, 2), down_weight)
    gate_t, up_t, down = call(
        functools.partial(load_kernel, len(weights)),
        [(weight.shape, BF16) for weight in weights],
        [HBM] * len(weights) + [ANY],
        (*[in_hbm(weight) for weight in weights], own),
        0,
        12 * gate_weight.size,
        [pltpu.SemaphoreType.DMA((len(weights),))],
    )
    block = 32 if hidden_count % 32 == 0 else 16
    stacked, mix = call(
        functools.partial(route_kernel, dp, own_segs, block),
        [((dp - 1, own_rows // 2, depth), BF16), ((segs * block, experts * block), BF16)],
        [SMEM] + [VMEM] * dp + [ANY],
        (my_dp, sends[0], *brought, down),
        0,
        2 * own_rows * width,
    )
    other = swap(stacked, "tensor", 1)
    merged_down = merge(mix, dp, own_segs, (down,))
    downs = [swap(merged_down[k], "dp", k) for k in range(dp - 1, 0, -1)]
    downs = [merged_down[0], *reversed(downs)]
    merged = merge(mix, dp, own_segs, (gate_t, up_t))
    partial_pre = preact(core, own, brought, other, merged)
    parts = [partial_pre[0]] + [swap(partial_pre[k], "dp", k) for k in range(1, dp)]

    rows = own_rows // tensor
    (mixed,) = call(
        functools.partial(down_kernel, dp),
        [((2, lines, rows, width), BF16)],
        [SMEM] + [VMEM] * (2 * dp),
        (core, *parts, *downs),
        2 * own_rows * hidden_count * width,
        2 * (own_rows * hidden_count * dp * 2 + hidden_count * width),
    )
    pieces = tensor_sum_pieces(mixed, lines)
    (out,) = call(
        functools.partial(finish_kernel, dp),
        [((rows, width), BF16)],
        [SMEM] + [VMEM] * lines,
        (my_dp, *pieces),
        rows * width * lines,
        2 * rows * width * (lines + 1),
    )
    return out


def solution(mesh):
    placed = (
        P("dp", None),
        P(None, "dp", "tensor"),
        P(None, "dp", "tensor"),
        P(None, "tensor", "dp"),
        P(),
        P(),
    )
    return jax.shard_map(
        on_device, mesh=mesh, in_specs=placed, out_specs=P(("dp", "tensor"), None), check_vma=False
    )
```

```python
import functools

import jax
import jax.numpy as jnp
from jax import lax
from jax.experimental import pallas as pl
from jax.experimental.pallas import tpu as pltpu
from jax.sharding import PartitionSpec as P

SEG = 256
SOFT_CAP = 8.0
VMEM = pl.BlockSpec(memory_space=pltpu.VMEM)
SMEM = pl.BlockSpec(memory_space=pltpu.SMEM)
F32 = jnp.float32
BF16 = jnp.bfloat16
LANES = 128
HBM = pl.BlockSpec(memory_space=pltpu.HBM)
ANY = pl.BlockSpec(memory_space=pl.ANY)


def swap(value, axis, step):
    count = lax.axis_size(axis)
    return lax.ppermute(value, axis, [(i, i ^ step) for i in range(count)])


def in_hbm(value):
    return pltpu.with_memory_space_constraint(value, pltpu.HBM)


def call(kernel, outs, in_specs, args, flops, moved, scratch=()):
    return pl.pallas_call(
        kernel,
        out_shape=[jax.ShapeDtypeStruct(shape, dtype) for shape, dtype in outs],
        in_specs=in_specs,
        out_specs=[VMEM] * len(outs),
        scratch_shapes=list(scratch),
        compiler_params=pltpu.CompilerParams(vmem_limit_bytes=24 * 2**20),
        cost_estimate=pl.CostEstimate(flops=flops, bytes_accessed=moved, transcendentals=0),
    )(*args)


def prepare_kernel(dp, own_segs, my_dp, core, tokens, router, carry, own, *refs):
    sends, (blocks, routers, carries, sems) = refs[: dp - 1], refs[dp - 1 :]
    rows, depth = own.shape
    half = rows // 2
    extra = sends[0].shape[0] - half
    experts = router.shape[0]
    columns = [pl.multiple_of((my_dp[0] ^ k) * depth, depth) for k in range(dp)]
    copies = [
        pltpu.make_async_copy(
            tokens.at[:, pl.ds(columns[k], depth)],
            own if k == 0 else blocks.at[k - 1],
            sems.at[k],
        )
        for k in range(dp)
    ]
    copies.append(pltpu.make_async_copy(router, routers, sems.at[dp]))
    copies.append(pltpu.make_async_copy(carry, carries, sems.at[dp + 1]))
    for copy in copies[dp:] + copies[:dp]:
        copy.start()
    member = lax.broadcasted_iota(jnp.int32, (extra, rows), 1) // SEG
    ones = member == lax.broadcasted_iota(jnp.int32, (extra, rows), 0)
    ones = jnp.where(ones, 1.0, 0.0).astype(BF16)
    start = pl.multiple_of(core[0] * half, half)
    for copy in copies:
        copy.wait()
    totals = [jnp.zeros((experts, depth), F32)] * (own_segs + 1)
    for k in range(dp):
        block = own[...] if k == 0 else blocks[k - 1]
        weight = routers[:, pl.ds(columns[k], depth)]
        means = jnp.dot(ones, block, preferred_element_type=F32) / SEG
        for j in range(own_segs):
            totals[j] += means[j : j + 1, :] * weight
        totals[own_segs] += carries[:, pl.ds(columns[k], depth)] * weight
        if k > 0:
            sends[k - 1][:half] = blocks[k - 1, pl.ds(start, half), :]
    lane = lax.broadcasted_iota(jnp.int32, (experts, LANES), 1)
    place = lane % experts == lax.broadcasted_iota(jnp.int32, (experts, LANES), 0)
    row = lax.broadcasted_iota(jnp.int32, (extra, LANES), 0)
    lane = lax.broadcasted_iota(jnp.int32, (extra, LANES), 1)
    logits = jnp.zeros((extra, LANES), F32)
    for j, total in enumerate(totals):
        column = jnp.sum(total, axis=1, keepdims=True)
        spread = jnp.sum(jnp.where(place, column, 0.0), axis=0, keepdims=True)
        logits = jnp.where(row == j, spread, logits)
    high = logits.astype(BF16).astype(F32)
    middle = (logits - high).astype(BF16).astype(F32)
    low = logits - high - middle
    terms = jnp.where(lane < experts, high, jnp.where(lane < 2 * experts, middle, low))
    terms = jnp.where(lane < 3 * experts, terms, 0.0).astype(BF16)
    for send in sends:
        send[half:] = jnp.zeros((extra, depth), BF16)
        send[half:, :LANES] = terms


def load_kernel(count, *refs):
    sources, targets, sems = refs[:count], refs[-count - 1 : -1], refs[-1]
    copies = [
        pltpu.make_async_copy(source, target, sems.at[i])
        for i, (source, target) in enumerate(zip(sources, targets))
    ]
    for copy in copies:
        copy.start()
    for copy in copies:
        copy.wait()


def read_table(piece, half, experts):
    lane = lax.broadcasted_iota(jnp.int32, (LANES, experts), 0)
    summed = lane % experts == lax.broadcasted_iota(jnp.int32, (LANES, experts), 1)
    summed = jnp.where(summed & (lane < 3 * experts), 1.0, 0.0).astype(BF16)
    return jnp.dot(piece[half:, :LANES], summed, preferred_element_type=F32)


def spread_probs(my_dp, tables, own_segs, steps, block):
    experts = tables[0].shape[1]
    raws = []
    for k in steps:
        for j in range(own_segs):
            prior = (my_dp ^ k) * own_segs + j - 1
            raw = tables[0][own_segs : own_segs + 1, :]
            for q, table in enumerate(tables):
                for i in range(own_segs):
                    here = (my_dp ^ q) * own_segs + i == prior
                    raw = jnp.where(here, table[i : i + 1, :], raw)
            raws.append(raw)
    logits = SOFT_CAP * jnp.tanh(jnp.concatenate(raws, axis=0) / SOFT_CAP)
    scores = jnp.exp(logits)
    probs = (scores / jnp.sum(scores, axis=1, keepdims=True)).astype(BF16).astype(F32)
    shape = (experts, experts * block)
    ahead = lax.broadcasted_iota(jnp.int32, shape, 1) // block
    spread = jnp.where(ahead == lax.broadcasted_iota(jnp.int32, shape, 0), 1.0, 0.0)
    wide = jnp.dot(probs, spread, preferred_element_type=F32)
    shape = (block, experts * block)
    diagonal = lax.broadcasted_iota(jnp.int32, shape, 1) % block == lax.broadcasted_iota(
        jnp.int32, shape, 0
    )
    return jnp.concatenate(
        [jnp.where(diagonal, wide[s : s + 1, :], 0.0) for s in range(len(raws))], axis=0
    ).astype(BF16)


def route_kernel(dp, own_segs, block, my_dp, sent, *refs):
    pieces, (stacked, mix) = refs[: dp - 1], refs[-2:]
    half = stacked.shape[1]
    for k, piece in enumerate(pieces):
        stacked[k] = piece[:half]
    experts = mix.shape[1] // block
    tables = [read_table(piece, half, experts) for piece in (sent, *pieces)]
    mix[...] = spread_probs(my_dp[0], tables, own_segs, tuple(range(dp)), block)


def merge_kernel(own_segs, mix, *refs):
    weights, outs = refs
    experts, rows, cols = weights[0].shape
    block = mix.shape[1] // experts
    for w, weight in enumerate(weights):
        for start in range(0, rows, block):
            tile = weight[:, start : start + block, :].reshape(experts * block, cols)
            out = jnp.dot(mix[...], tile, preferred_element_type=F32).astype(BF16)
            out = out.reshape(len(outs), own_segs, block, cols)
            at = w * rows + start
            for k in range(len(outs)):
                outs[k][:, at : at + block, :] = out[k]


def merge(mix, dp, own_segs, weights):
    experts, rows, cols = weights[0].shape
    total = rows * len(weights)
    count = len(weights)

    def kernel(mix_ref, *refs):
        merge_kernel(own_segs, mix_ref, refs[:count], refs[-dp:])

    return call(
        kernel,
        [((own_segs, total, cols), BF16)] * dp,
        [VMEM] * (1 + count),
        (mix, *weights),
        2 * mix.size * total * cols // rows,
        2 * total * cols * (experts + dp * own_segs),
    )


def preact_kernel(dp, core, own, *refs):
    brought, other = refs[: dp - 1], refs[dp - 1]
    merged, outs, whole = refs[dp : 2 * dp], refs[2 * dp : 3 * dp], refs[-1]
    half = own.shape[0] // 2
    near = pl.multiple_of(core[0] * half, half)
    far = pl.multiple_of((1 - core[0]) * half, half)
    for k in list(range(dp - 1, -1, -1)):
        if k > 0:
            whole[k - 1, pl.ds(near, half), :] = brought[k - 1][:half]
            whole[k - 1, pl.ds(far, half), :] = other[k - 1]
        for j in range(merged[k].shape[0]):
            rows = slice(j * SEG, (j + 1) * SEG)
            outs[k][j] = lax.dot_general(
                merged[k][j],
                own[rows, :] if k == 0 else whole[k - 1, rows, :],
                (((1,), (1,)), ((), ())),
                preferred_element_type=F32,
            ).astype(BF16)


def preact(core, own, brought, other, merged):
    dp = len(merged)
    own_segs, total, depth = merged[0].shape
    segs = dp * own_segs
    return call(
        functools.partial(preact_kernel, dp),
        [((own_segs, total, SEG), BF16)] * dp,
        [SMEM] + [VMEM] * (2 * dp + 1),
        (core, own, *brought, other, *merged),
        2 * segs * total * SEG * depth,
        2 * segs * (total * depth + SEG * depth + total * SEG),
        [pltpu.VMEM((dp - 1, own_segs * SEG, depth), BF16)],
    )


def down_columns(core, hidden, downs, mixed):
    cols = downs[0].shape[2]
    rows = mixed.shape[2]
    for j, part in enumerate(hidden):
        for k, down in enumerate(downs):
            out = lax.dot_general(
                part, down[j], (((0,), (0,)), ((), ())), preferred_element_type=F32
            ).astype(BF16)
            for i in range(SEG // rows):
                at = j * (SEG // rows) + i
                mixed[(at % 2) ^ core, at // 2, :, k * cols : (k + 1) * cols] = out[
                    i * rows : (i + 1) * rows
                ]


def first_kernel(dp, core, *refs):
    parts, downs, hidden, mixed = refs[:dp], refs[dp:-2], refs[-2], refs[-1]
    half = hidden.shape[1]
    kept = []
    for j in range(hidden.shape[0]):
        total = parts[0][j].astype(F32)
        for part in parts[1:]:
            total += part[j].astype(F32)
        gate, up = total[:half], total[half:]
        kept.append((gate / (1.0 + jnp.exp(-gate)) * up).astype(BF16))
        hidden[j] = kept[j]
    down_columns(core[0], kept, downs, mixed)


def second_kernel(count, core, hidden, *refs):
    kept = [hidden[j] for j in range(hidden.shape[0])]
    down_columns(core[0], kept, refs[:count], refs[-1])


def finish_kernel(groups, lines, my_dp, *refs):
    out = refs[-1]
    for g, steps in enumerate(groups):
        pieces = refs[g * lines : (g + 1) * lines]
        cols = pieces[0].shape[1] // len(steps)
        total = pieces[0][...].astype(F32)
        for piece in pieces[1:]:
            total += piece[...].astype(F32)
        total = total.astype(BF16)
        for k, step in enumerate(steps):
            at = pl.multiple_of((my_dp[0] ^ step) * cols, cols)
            out[:, pl.ds(at, cols)] = total[:, k * cols : (k + 1) * cols]


def tensor_sum_pieces(mixed, lines):
    my_line = lax.axis_index("tensor") // 2
    pair = mixed[0].astype(F32) + swap(mixed[1], "tensor", 1).astype(F32)
    pair = pair.astype(BF16)
    pieces = [lax.dynamic_index_in_dim(pair, my_line ^ k, 0, keepdims=False) for k in range(lines)]
    return [swap(pieces[k], "tensor", 2 * k) for k in range(lines - 1, 0, -1)] + [pieces[0]]


def on_device(tokens, gate_weight, up_weight, down_weight, router_weight, carry_mean):
    dp = lax.axis_size("dp")
    tensor = lax.axis_size("tensor")
    lines = tensor // 2
    my_dp = lax.axis_index("dp").reshape(1)
    core = (lax.axis_index("tensor") % 2).reshape(1)
    own_rows, width = tokens.shape
    own_segs = own_rows // SEG
    experts, depth, hidden_count = gate_weight.shape
    cols = down_weight.shape[2]
    segs = dp * own_segs

    extra = -(-(own_segs + 1) // 16) * 16
    own, *sends = call(
        functools.partial(prepare_kernel, dp, own_segs),
        [((own_rows, depth), BF16)] + [((own_rows // 2 + extra, depth), BF16)] * (dp - 1),
        [SMEM, SMEM, HBM, HBM, HBM],
        (my_dp, core, *map(in_hbm, (tokens, router_weight.T, carry_mean.reshape(1, width)))),
        2 * extra * own_rows * width,
        4 * own_rows * width,
        [
            pltpu.VMEM((dp - 1, own_rows, depth), BF16),
            pltpu.VMEM((experts, width), F32),
            pltpu.VMEM((1, width), F32),
            pltpu.SemaphoreType.DMA((dp + 2,)),
        ],
    )
    brought = [swap(sends[k - 1], "dp", k) for k in range(1, dp)]
    weights = (jnp.swapaxes(gate_weight, 1, 2), jnp.swapaxes(up_weight, 1, 2), down_weight)
    gate_t, up_t, down = call(
        functools.partial(load_kernel, len(weights)),
        [(weight.shape, BF16) for weight in weights],
        [HBM] * len(weights) + [ANY],
        (*[in_hbm(weight) for weight in weights], own),
        0,
        12 * gate_weight.size,
        [pltpu.SemaphoreType.DMA((len(weights),))],
    )
    block = 32 if hidden_count % 32 == 0 else 16
    stacked, mix = call(
        functools.partial(route_kernel, dp, own_segs, block),
        [((dp - 1, own_rows // 2, depth), BF16), ((segs * block, experts * block), BF16)],
        [SMEM] + [VMEM] * dp + [ANY],
        (my_dp, sends[0], *brought, down),
        0,
        2 * own_rows * width,
    )
    other = swap(stacked, "tensor", 1)
    merged_down = merge(mix, dp, own_segs, (down,))
    downs = [block if k == 0 else swap(block, "dp", k) for k, block in enumerate(merged_down)]
    merged = merge(mix, dp, own_segs, (gate_t, up_t))
    partial_pre = preact(core, own, brought, other, merged)
    parts = [partial_pre[0]] + [swap(partial_pre[k], "dp", k) for k in range(1, dp)]

    rows = own_rows // tensor
    early, late = tuple(range(dp - 1)), (dp - 1,)
    flops = 2 * own_rows * hidden_count * cols
    hidden, mixed = call(
        functools.partial(first_kernel, dp),
        [((own_segs, hidden_count, SEG), BF16), ((2, lines, rows, len(early) * cols), BF16)],
        [SMEM] + [VMEM] * (dp + len(early)),
        (core, *parts, *[downs[k] for k in early]),
        flops * len(early),
        2 * (own_rows * hidden_count * dp * 2 + hidden_count * cols * len(early)),
    )
    early_pieces = tensor_sum_pieces(mixed, lines)
    (mixed,) = call(
        functools.partial(second_kernel, len(late)),
        [((2, lines, rows, len(late) * cols), BF16)],
        [SMEM] + [VMEM] * (1 + len(late)) + [ANY] * lines,
        (core, hidden, *[downs[k] for k in late], *early_pieces),
        flops * len(late),
        2 * (own_rows * hidden_count + hidden_count * cols * len(late)),
    )
    late_pieces = tensor_sum_pieces(mixed, lines)
    (out,) = call(
        functools.partial(finish_kernel, (early, late), lines),
        [((rows, width), BF16)],
        [SMEM] + [VMEM] * (2 * lines),
        (my_dp, *early_pieces, *late_pieces),
        rows * width * lines,
        2 * rows * width * (lines + 1),
    )
    return out


def solution(mesh):
    placed = (
        P("dp", None),
        P(None, "dp", "tensor"),
        P(None, "dp", "tensor"),
        P(None, "tensor", "dp"),
        P(),
        P(),
    )
    return jax.shard_map(
        on_device, mesh=mesh, in_specs=placed, out_specs=P(("dp", "tensor"), None), check_vma=False
    )
```

```python
import functools

import jax
import jax.numpy as jnp
from jax import lax
from jax.experimental import pallas as pl
from jax.experimental.pallas import tpu as pltpu
from jax.sharding import PartitionSpec as P

SEG = 256
SOFT_CAP = 8.0
VMEM = pl.BlockSpec(memory_space=pltpu.VMEM)
SMEM = pl.BlockSpec(memory_space=pltpu.SMEM)
F32 = jnp.float32
BF16 = jnp.bfloat16
LANES = 128
HBM = pl.BlockSpec(memory_space=pltpu.HBM)
ANY = pl.BlockSpec(memory_space=pl.ANY)


def swap(value, axis, step):
    count = lax.axis_size(axis)
    return lax.ppermute(value, axis, [(i, i ^ step) for i in range(count)])


def in_hbm(value):
    return pltpu.with_memory_space_constraint(value, pltpu.HBM)


def call(kernel, outs, in_specs, args, flops, moved, scratch=()):
    return pl.pallas_call(
        kernel,
        out_shape=[jax.ShapeDtypeStruct(shape, dtype) for shape, dtype in outs],
        in_specs=in_specs,
        out_specs=[VMEM] * len(outs),
        scratch_shapes=list(scratch),
        compiler_params=pltpu.CompilerParams(vmem_limit_bytes=24 * 2**20),
        cost_estimate=pl.CostEstimate(flops=flops, bytes_accessed=moved, transcendentals=0),
    )(*args)


def prepare_kernel(dp, own_segs, my_dp, core, tokens, router, carry, own, *refs):
    firsts, seconds = refs[: dp - 1], refs[dp - 1 : 2 * dp - 2]
    blocks, routers, carries, sems = refs[2 * dp - 2 :]
    rows, depth = own.shape
    half = rows // 2
    quarter = half // 2
    extra = firsts[0].shape[0] - quarter
    experts = router.shape[0]
    columns = [pl.multiple_of((my_dp[0] ^ k) * depth, depth) for k in range(dp)]
    copies = [
        pltpu.make_async_copy(
            tokens.at[:, pl.ds(columns[k], depth)],
            own if k == 0 else blocks.at[k - 1],
            sems.at[k],
        )
        for k in range(dp)
    ]
    copies.append(pltpu.make_async_copy(router, routers, sems.at[dp]))
    copies.append(pltpu.make_async_copy(carry, carries, sems.at[dp + 1]))
    for copy in copies[dp:] + copies[:dp]:
        copy.start()
    member = lax.broadcasted_iota(jnp.int32, (extra, rows), 1) // SEG
    ones = member == lax.broadcasted_iota(jnp.int32, (extra, rows), 0)
    ones = jnp.where(ones, 1.0, 0.0).astype(BF16)
    start = pl.multiple_of(core[0] * half, quarter)
    for copy in copies:
        copy.wait()
    totals = [jnp.zeros((experts, depth), F32)] * (own_segs + 1)
    for k in range(dp):
        block = own[...] if k == 0 else blocks[k - 1]
        weight = routers[:, pl.ds(columns[k], depth)]
        means = jnp.dot(ones, block, preferred_element_type=F32) / SEG
        for j in range(own_segs):
            totals[j] += means[j : j + 1, :] * weight
        totals[own_segs] += carries[:, pl.ds(columns[k], depth)] * weight
        if k > 0:
            firsts[k - 1][:quarter] = blocks[k - 1, pl.ds(start, quarter), :]
            seconds[k - 1][...] = blocks[k - 1, pl.ds(start + quarter, quarter), :]
    lane = lax.broadcasted_iota(jnp.int32, (experts, LANES), 1)
    place = lane % experts == lax.broadcasted_iota(jnp.int32, (experts, LANES), 0)
    row = lax.broadcasted_iota(jnp.int32, (extra, LANES), 0)
    lane = lax.broadcasted_iota(jnp.int32, (extra, LANES), 1)
    logits = jnp.zeros((extra, LANES), F32)
    for j, total in enumerate(totals):
        column = jnp.sum(total, axis=1, keepdims=True)
        spread = jnp.sum(jnp.where(place, column, 0.0), axis=0, keepdims=True)
        logits = jnp.where(row == j, spread, logits)
    high = logits.astype(BF16).astype(F32)
    middle = (logits - high).astype(BF16).astype(F32)
    low = logits - high - middle
    terms = jnp.where(lane < experts, high, jnp.where(lane < 2 * experts, middle, low))
    terms = jnp.where(lane < 3 * experts, terms, 0.0).astype(BF16)
    for first in firsts:
        first[quarter:] = jnp.zeros((extra, depth), BF16)
        first[quarter:, :LANES] = terms


def load_kernel(count, *refs):
    sources, targets, sems = refs[:count], refs[-count - 1 : -1], refs[-1]
    copies = [
        pltpu.make_async_copy(source, target, sems.at[i])
        for i, (source, target) in enumerate(zip(sources, targets))
    ]
    for copy in copies:
        copy.start()
    for copy in copies:
        copy.wait()


def read_table(piece, tokens, experts):
    lane = lax.broadcasted_iota(jnp.int32, (LANES, experts), 0)
    summed = lane % experts == lax.broadcasted_iota(jnp.int32, (LANES, experts), 1)
    summed = jnp.where(summed & (lane < 3 * experts), 1.0, 0.0).astype(BF16)
    return jnp.dot(piece[tokens:, :LANES], summed, preferred_element_type=F32)


def load(weights, after):
    count = len(weights)
    return call(
        functools.partial(load_kernel, count),
        [(weight.shape, BF16) for weight in weights],
        [HBM] * count + [ANY],
        (*map(in_hbm, weights), after),
        0,
        4 * count * weights[0].size,
        [pltpu.SemaphoreType.DMA((count,))],
    )


def spread_probs(my_dp, tables, own_segs, experts, steps, block):
    raws = []
    for k in steps:
        for j in range(own_segs):
            prior = (my_dp ^ k) * own_segs + j - 1
            raw = tables[0][own_segs : own_segs + 1, :]
            for q, table in enumerate(tables):
                for i in range(own_segs):
                    here = (my_dp ^ q) * own_segs + i == prior
                    raw = jnp.where(here, table[i : i + 1, :], raw)
            raws.append(raw)
    logits = SOFT_CAP * jnp.tanh(jnp.concatenate(raws, axis=0) / SOFT_CAP)
    scores = jnp.exp(logits)
    probs = (scores / jnp.sum(scores, axis=1, keepdims=True)).astype(BF16).astype(F32)
    shape = (experts, experts * block)
    ahead = lax.broadcasted_iota(jnp.int32, shape, 1) // block
    spread = jnp.where(ahead == lax.broadcasted_iota(jnp.int32, shape, 0), 1.0, 0.0)
    wide = jnp.dot(probs, spread, preferred_element_type=F32)
    shape = (block, experts * block)
    diagonal = lax.broadcasted_iota(jnp.int32, shape, 1) % block == lax.broadcasted_iota(
        jnp.int32, shape, 0
    )
    return jnp.concatenate(
        [jnp.where(diagonal, wide[s : s + 1, :], 0.0) for s in range(len(raws))], axis=0
    ).astype(BF16)


def route_kernel(dp, own_segs, block, my_dp, *refs):
    pieces, mix = refs[:dp], refs[-1]
    experts = mix.shape[1] // block
    tables = [read_table(piece, own_segs * SEG // 4, experts) for piece in pieces]
    mix[...] = spread_probs(my_dp[0], tables, own_segs, experts, tuple(range(dp)), block)


def stack_kernel(dp, *refs):
    firsts, seconds, stacked = refs[: dp - 1], refs[dp - 1 : 2 * dp - 2], refs[-1]
    quarter = seconds[0].shape[0]
    for k in range(dp - 1):
        stacked[k, :quarter] = firsts[k][:quarter]
        stacked[k, quarter:] = seconds[k][...]


def merge_kernel(own_segs, mix, *refs):
    weights, outs = refs
    experts, rows, cols = weights[0].shape
    block = mix.shape[1] // experts
    for w, weight in enumerate(weights):
        for start in range(0, rows, block):
            tile = weight[:, start : start + block, :].reshape(experts * block, cols)
            out = jnp.dot(mix[...], tile, preferred_element_type=F32).astype(BF16)
            out = out.reshape(len(outs), own_segs, block, cols)
            at = w * rows + start
            for k in range(len(outs)):
                outs[k][:, at : at + block, :] = out[k]


def merge(mix, dp, own_segs, weights):
    experts, rows, cols = weights[0].shape
    total = rows * len(weights)
    count = len(weights)

    def kernel(mix_ref, *refs):
        merge_kernel(own_segs, mix_ref, refs[:count], refs[-dp:])

    return call(
        kernel,
        [((own_segs, total, cols), BF16)] * dp,
        [VMEM] * (1 + count),
        (mix, *weights),
        2 * mix.size * total * cols // rows,
        2 * total * cols * (experts + dp * own_segs),
    )


def preact_kernel(dp, core, own, brought, other, *refs):
    merged, outs, whole = refs[:dp], refs[dp : 2 * dp], refs[-1]
    half = own.shape[0] // 2
    near = pl.multiple_of(core[0] * half, half)
    far = pl.multiple_of((1 - core[0]) * half, half)
    for k in range(dp - 1, -1, -1):
        if k > 0:
            whole[k - 1, pl.ds(near, half), :] = brought[k - 1]
            whole[k - 1, pl.ds(far, half), :] = other[k - 1]
        for j in range(merged[k].shape[0]):
            rows = slice(j * SEG, (j + 1) * SEG)
            outs[k][j] = lax.dot_general(
                merged[k][j],
                own[rows, :] if k == 0 else whole[k - 1, rows, :],
                (((1,), (1,)), ((), ())),
                preferred_element_type=F32,
            ).astype(BF16)


def preact(core, own, brought, other, merged):
    dp = len(merged)
    own_segs, total, depth = merged[0].shape
    segs = dp * own_segs
    return call(
        functools.partial(preact_kernel, dp),
        [((own_segs, total, SEG), BF16)] * dp,
        [SMEM] + [VMEM] * (dp + 3),
        (core, own, brought, other, *merged),
        2 * segs * total * SEG * depth,
        2 * segs * (total * depth + SEG * depth + total * SEG),
        [pltpu.VMEM((dp - 1, own_segs * SEG, depth), BF16)],
    )


def down_columns(core, hidden, downs, mixed):
    cols = downs[0].shape[2]
    rows = mixed.shape[2]
    for j, part in enumerate(hidden):
        for k, down in enumerate(downs):
            out = lax.dot_general(
                part, down[j], (((0,), (0,)), ((), ())), preferred_element_type=F32
            ).astype(BF16)
            for i in range(SEG // rows):
                at = j * (SEG // rows) + i
                mixed[(at % 2) ^ core, at // 2, :, k * cols : (k + 1) * cols] = out[
                    i * rows : (i + 1) * rows
                ]


def first_kernel(dp, core, *refs):
    parts, downs, hidden, mixed = refs[:dp], refs[dp:-2], refs[-2], refs[-1]
    half = hidden.shape[1]
    kept = []
    for j in range(hidden.shape[0]):
        total = parts[0][j].astype(F32)
        for part in parts[1:]:
            total += part[j].astype(F32)
        gate, up = total[:half], total[half:]
        kept.append((gate / (1.0 + jnp.exp(-gate)) * up).astype(BF16))
        hidden[j] = kept[j]
    down_columns(core[0], kept, downs, mixed)


def second_kernel(count, core, hidden, *refs):
    kept = [hidden[j] for j in range(hidden.shape[0])]
    down_columns(core[0], kept, refs[:count], refs[-1])


def finish_kernel(groups, lines, my_dp, *refs):
    out = refs[-1]
    for g, steps in enumerate(groups):
        pieces = refs[g * lines : (g + 1) * lines]
        cols = pieces[0].shape[1] // len(steps)
        total = pieces[0][...].astype(F32)
        for piece in pieces[1:]:
            total += piece[...].astype(F32)
        total = total.astype(BF16)
        for k, step in enumerate(steps):
            at = pl.multiple_of((my_dp[0] ^ step) * cols, cols)
            out[:, pl.ds(at, cols)] = total[:, k * cols : (k + 1) * cols]


def tensor_sum_pieces(mixed, lines):
    my_line = lax.axis_index("tensor") // 2
    pair = mixed[0].astype(F32) + swap(mixed[1], "tensor", 1).astype(F32)
    pair = pair.astype(BF16)
    pieces = [lax.dynamic_index_in_dim(pair, my_line ^ k, 0, keepdims=False) for k in range(lines)]
    return [swap(pieces[k], "tensor", 2 * k) for k in range(lines - 1, 0, -1)] + [pieces[0]]


def on_device(tokens, gate_weight, up_weight, down_weight, router_weight, carry_mean):
    dp = lax.axis_size("dp")
    tensor = lax.axis_size("tensor")
    lines = tensor // 2
    my_dp = lax.axis_index("dp").reshape(1)
    core = (lax.axis_index("tensor") % 2).reshape(1)
    own_rows, width = tokens.shape
    own_segs = own_rows // SEG
    experts, depth, hidden_count = gate_weight.shape
    cols = down_weight.shape[2]
    segs = dp * own_segs

    extra = -(-(own_segs + 1) // 16) * 16
    quarter = own_rows // 4
    own, *sends = call(
        functools.partial(prepare_kernel, dp, own_segs),
        [((own_rows, depth), BF16)]
        + [((quarter + extra, depth), BF16)] * (dp - 1)
        + [((quarter, depth), BF16)] * (dp - 1),
        [SMEM, SMEM, HBM, HBM, HBM],
        (my_dp, core, *map(in_hbm, (tokens, router_weight.T, carry_mean.reshape(1, width)))),
        2 * extra * own_rows * width,
        4 * own_rows * width,
        [
            pltpu.VMEM((dp - 1, own_rows, depth), BF16),
            pltpu.VMEM((experts, width), F32),
            pltpu.VMEM((1, width), F32),
            pltpu.SemaphoreType.DMA((dp + 2,)),
        ],
    )
    firsts = [swap(sends[k - 1], "dp", k) for k in range(1, dp)]
    seconds = [swap(sends[dp + k - 2], "dp", k) for k in range(1, dp)]
    (down,) = load((down_weight,), own)
    block = 32 if hidden_count % 32 == 0 else 16
    (mix,) = call(
        functools.partial(route_kernel, dp, own_segs, block),
        [((segs * block, experts * block), BF16)],
        [SMEM] + [VMEM] * dp + [ANY],
        (my_dp, sends[0], *firsts, down),
        0,
        2 * own_rows * depth,
    )
    merged_down = merge(mix, dp, own_segs, (down,))
    downs = [block if k == 0 else swap(block, "dp", k) for k, block in enumerate(merged_down)]
    gate_t, up_t = load(
        (jnp.swapaxes(gate_weight, 1, 2), jnp.swapaxes(up_weight, 1, 2)), merged_down[0]
    )
    (stacked,) = call(
        functools.partial(stack_kernel, dp),
        [((dp - 1, own_rows // 2, depth), BF16)],
        [VMEM] * (2 * dp - 2) + [ANY],
        (*firsts, *seconds, up_t),
        0,
        2 * own_rows * width,
    )
    other = swap(stacked, "tensor", 1)
    merged = merge(mix, dp, own_segs, (gate_t, up_t))
    partial_pre = preact(core, own, stacked, other, merged)
    parts = [partial_pre[0]] + [swap(partial_pre[k], "dp", k) for k in range(1, dp)]

    rows = own_rows // tensor
    early, late = tuple(range(dp - 1)), (dp - 1,)
    flops = 2 * own_rows * hidden_count * cols
    hidden, mixed = call(
        functools.partial(first_kernel, dp),
        [((own_segs, hidden_count, SEG), BF16), ((2, lines, rows, len(early) * cols), BF16)],
        [SMEM] + [VMEM] * (dp + len(early)),
        (core, *parts, *[downs[k] for k in early]),
        flops * len(early),
        2 * (own_rows * hidden_count * dp * 2 + hidden_count * cols * len(early)),
    )
    early_pieces = tensor_sum_pieces(mixed, lines)
    (mixed,) = call(
        functools.partial(second_kernel, len(late)),
        [((2, lines, rows, len(late) * cols), BF16)],
        [SMEM] + [VMEM] * (1 + len(late)) + [ANY] * lines,
        (core, hidden, *[downs[k] for k in late], *early_pieces),
        flops * len(late),
        2 * (own_rows * hidden_count + hidden_count * cols * len(late)),
    )
    late_pieces = tensor_sum_pieces(mixed, lines)
    (out,) = call(
        functools.partial(finish_kernel, (early, late), lines),
        [((rows, width), BF16)],
        [SMEM] + [VMEM] * (2 * lines),
        (my_dp, *early_pieces, *late_pieces),
        rows * width * lines,
        2 * rows * width * (lines + 1),
    )
    return out


def solution(mesh):
    placed = (
        P("dp", None),
        P(None, "dp", "tensor"),
        P(None, "dp", "tensor"),
        P(None, "tensor", "dp"),
        P(),
        P(),
    )
    return jax.shard_map(
        on_device, mesh=mesh, in_specs=placed, out_specs=P(("dp", "tensor"), None), check_vma=False
    )
```

```python
import functools

import jax
import jax.numpy as jnp
from jax import lax
from jax.experimental import pallas as pl
from jax.experimental.pallas import tpu as pltpu
from jax.sharding import PartitionSpec as P

SEG = 256
SOFT_CAP = 8.0
VMEM = pl.BlockSpec(memory_space=pltpu.VMEM)
SMEM = pl.BlockSpec(memory_space=pltpu.SMEM)
F32 = jnp.float32
BF16 = jnp.bfloat16
LANES = 128
BESIDE = 10**10
HBM = pl.BlockSpec(memory_space=pltpu.HBM)
ANY = pl.BlockSpec(memory_space=pl.ANY)


def swap(value, axis, step):
    count = lax.axis_size(axis)
    return lax.ppermute(value, axis, [(i, i ^ step) for i in range(count)])


def in_hbm(value):
    return pltpu.with_memory_space_constraint(value, pltpu.HBM)


def call(kernel, outs, in_specs, args, flops, moved, scratch=()):
    return pl.pallas_call(
        kernel,
        out_shape=[jax.ShapeDtypeStruct(shape, dtype) for shape, dtype in outs],
        in_specs=in_specs,
        out_specs=[VMEM] * len(outs),
        scratch_shapes=list(scratch),
        compiler_params=pltpu.CompilerParams(vmem_limit_bytes=24 * 2**20),
        cost_estimate=pl.CostEstimate(flops=flops, bytes_accessed=moved, transcendentals=0),
    )(*args)


def prepare_kernel(dp, own_segs, block, my_dp, core, tokens, router, carry, own, *refs):
    firsts, seconds = refs[: dp - 1], refs[dp - 1 : 2 * dp - 2]
    blocks, routers, carries, sems = refs[2 * dp - 2 :]
    rows, depth = own.shape
    half = rows // 2
    quarter = half // 2
    extra = firsts[0].shape[0] - quarter
    experts = router.shape[0]
    columns = [pl.multiple_of((my_dp[0] ^ k) * depth, depth) for k in range(dp)]
    copies = [
        pltpu.make_async_copy(
            tokens.at[:, pl.ds(columns[k], depth)],
            blocks.at[k],
            sems.at[k],
        )
        for k in range(dp)
    ]
    copies.append(pltpu.make_async_copy(router, routers, sems.at[dp]))
    copies.append(pltpu.make_async_copy(carry, carries, sems.at[dp + 1]))
    for copy in copies[dp:] + copies[:dp]:
        copy.start()
    member = lax.broadcasted_iota(jnp.int32, (extra, rows), 1) // SEG
    ones = member == lax.broadcasted_iota(jnp.int32, (extra, rows), 0)
    ones = jnp.where(ones, 1.0, 0.0).astype(BF16)
    near = [pl.multiple_of((2 * i + core[0]) * block, block) for i in range(half // block)]
    far = [pl.multiple_of((2 * i + 1 - core[0]) * block, block) for i in range(half // block)]
    for copy in copies:
        copy.wait()
    totals = [jnp.zeros((experts, depth), F32)] * (own_segs + 1)
    for k in range(dp):
        weight = routers[:, pl.ds(columns[k], depth)]
        means = jnp.dot(ones, blocks[k], preferred_element_type=F32) / SEG
        for j in range(own_segs):
            totals[j] += means[j : j + 1, :] * weight
        totals[own_segs] += carries[:, pl.ds(columns[k], depth)] * weight
        for i, start in enumerate(near if k > 0 else near + far):
            at = i * block
            rows_in = blocks[k, pl.ds(start, block), :]
            if k == 0:
                own[at : at + block] = rows_in
            elif at < quarter:
                firsts[k - 1][at : at + block] = rows_in
            else:
                seconds[k - 1][at - quarter : at - quarter + block] = rows_in
    lane = lax.broadcasted_iota(jnp.int32, (experts, LANES), 1)
    place = lane % experts == lax.broadcasted_iota(jnp.int32, (experts, LANES), 0)
    row = lax.broadcasted_iota(jnp.int32, (extra, LANES), 0)
    lane = lax.broadcasted_iota(jnp.int32, (extra, LANES), 1)
    logits = jnp.zeros((extra, LANES), F32)
    for j, total in enumerate(totals):
        column = jnp.sum(total, axis=1, keepdims=True)
        spread = jnp.sum(jnp.where(place, column, 0.0), axis=0, keepdims=True)
        logits = jnp.where(row == j, spread, logits)
    high = logits.astype(BF16).astype(F32)
    middle = (logits - high).astype(BF16).astype(F32)
    low = logits - high - middle
    terms = jnp.where(lane < experts, high, jnp.where(lane < 2 * experts, middle, low))
    terms = jnp.where(lane < 3 * experts, terms, 0.0).astype(BF16)
    for first in firsts:
        first[quarter:] = jnp.zeros((extra, depth), BF16)
        first[quarter:, :LANES] = terms


def load_kernel(count, *refs):
    sources, targets, sems = refs[:count], refs[-count - 1 : -1], refs[-1]
    copies = [
        pltpu.make_async_copy(source, target, sems.at[i])
        for i, (source, target) in enumerate(zip(sources, targets))
    ]
    for copy in copies:
        copy.start()
    for copy in copies:
        copy.wait()


def read_table(piece, tokens, experts):
    lane = lax.broadcasted_iota(jnp.int32, (LANES, experts), 0)
    summed = lane % experts == lax.broadcasted_iota(jnp.int32, (LANES, experts), 1)
    summed = jnp.where(summed & (lane < 3 * experts), 1.0, 0.0).astype(BF16)
    return jnp.dot(piece[tokens:, :LANES], summed, preferred_element_type=F32)


def load(weights, after):
    count = len(weights)
    return call(
        functools.partial(load_kernel, count),
        [(weight.shape, BF16) for weight in weights],
        [HBM] * count + [ANY],
        (*map(in_hbm, weights), after),
        0,
        4 * count * weights[0].size,
        [pltpu.SemaphoreType.DMA((count,))],
    )


def spread_probs(my_dp, tables, own_segs, experts, steps, block):
    raws = []
    for k in steps:
        for j in range(own_segs):
            prior = (my_dp ^ k) * own_segs + j - 1
            raw = tables[0][own_segs : own_segs + 1, :]
            for q, table in enumerate(tables):
                for i in range(own_segs):
                    here = (my_dp ^ q) * own_segs + i == prior
                    raw = jnp.where(here, table[i : i + 1, :], raw)
            raws.append(raw)
    logits = SOFT_CAP * jnp.tanh(jnp.concatenate(raws, axis=0) / SOFT_CAP)
    scores = jnp.exp(logits)
    probs = (scores / jnp.sum(scores, axis=1, keepdims=True)).astype(BF16).astype(F32)
    shape = (experts, experts * block)
    ahead = lax.broadcasted_iota(jnp.int32, shape, 1) // block
    spread = jnp.where(ahead == lax.broadcasted_iota(jnp.int32, shape, 0), 1.0, 0.0)
    wide = jnp.dot(probs, spread, preferred_element_type=F32)
    shape = (block, experts * block)
    diagonal = lax.broadcasted_iota(jnp.int32, shape, 1) % block == lax.broadcasted_iota(
        jnp.int32, shape, 0
    )
    return jnp.concatenate(
        [jnp.where(diagonal, wide[s : s + 1, :], 0.0) for s in range(len(raws))], axis=0
    ).astype(BF16)


def route_kernel(dp, own_segs, block, my_dp, *refs):
    pieces, mix = refs[:dp], refs[-1]
    experts = mix.shape[1] // block
    tables = [read_table(piece, own_segs * SEG // 4, experts) for piece in pieces]
    mix[...] = spread_probs(my_dp[0], tables, own_segs, experts, tuple(range(dp)), block)


def stack_kernel(dp, *refs):
    firsts, seconds, stacked = refs[: dp - 1], refs[dp - 1 : 2 * dp - 2], refs[-1]
    quarter = seconds[0].shape[0]
    for k in range(dp - 1):
        stacked[k, :quarter] = firsts[k][:quarter]
        stacked[k, quarter:] = seconds[k][...]


def merge_kernel(own_segs, mix, *refs):
    weights, outs = refs
    experts, rows, cols = weights[0].shape
    block = mix.shape[1] // experts
    for w, weight in enumerate(weights):
        for start in range(0, rows, block):
            tile = weight[:, start : start + block, :].reshape(experts * block, cols)
            out = jnp.dot(mix[...], tile, preferred_element_type=F32).astype(BF16)
            out = out.reshape(len(outs), own_segs, block, cols)
            at = w * rows + start
            for k in range(len(outs)):
                outs[k][:, at : at + block, :] = out[k]


def merge(mix, dp, own_segs, weights, flops):
    experts, rows, cols = weights[0].shape
    total = rows * len(weights)
    count = len(weights)

    def kernel(mix_ref, *refs):
        merge_kernel(own_segs, mix_ref, refs[:count], refs[-dp:])

    return call(
        kernel,
        [((own_segs, total, cols), BF16)] * dp,
        [VMEM] * (1 + count),
        (mix, *weights),
        flops,
        2 * total * cols * (experts + dp * own_segs),
    )


def preact_kernel(dp, own, brought, other, *refs):
    merged, outs, whole = refs[:dp], refs[dp : 2 * dp], refs[-1]
    half = own.shape[0] // 2
    for k in range(dp - 1, -1, -1):
        if k > 0:
            whole[k - 1, :half] = brought[k - 1]
            whole[k - 1, half:] = other[k - 1]
        outs[k][0] = lax.dot_general(
            merged[k][0],
            own[...] if k == 0 else whole[k - 1],
            (((1,), (1,)), ((), ())),
            preferred_element_type=F32,
        ).astype(BF16)


def preact(own, brought, other, merged):
    dp = len(merged)
    own_segs, total, depth = merged[0].shape
    segs = dp * own_segs
    return call(
        functools.partial(preact_kernel, dp),
        [((own_segs, total, SEG), BF16)] * dp,
        [VMEM] * (dp + 3),
        (own, brought, other, *merged),
        2 * segs * total * SEG * depth,
        2 * segs * (total * depth + SEG * depth + total * SEG),
        [pltpu.VMEM((dp - 1, own_segs * SEG, depth), BF16)],
    )


def down_columns(hidden, downs, mixed):
    lines, rows, cols = mixed.shape
    cols //= len(downs)
    for k, down in enumerate(downs):
        out = lax.dot_general(
            hidden, down[0], (((0,), (0,)), ((), ())), preferred_element_type=F32
        ).astype(BF16)
        mixed[:, :, k * cols : (k + 1) * cols] = out.reshape(lines, rows, cols)


def hidden_kernel(dp, *refs):
    parts, downs, hidden, mixed = refs[:dp], refs[dp:-2], refs[-2], refs[-1]
    half = hidden.shape[0]
    total = parts[0][0].astype(F32)
    for part in parts[1:]:
        total += part[0].astype(F32)
    gate, up = total[:half], total[half:]
    value = (gate / (1.0 + jnp.exp(-gate)) * up).astype(BF16)
    hidden[...] = value
    down_columns(value[:, value.shape[1] // 2 :], downs, mixed)


def product_kernel(count, near, hidden, *refs):
    half = hidden.shape[1] // 2
    part = hidden[:, :half] if near else hidden[:, half:]
    down_columns(part, refs[:count], refs[-1])


def finish_kernel(groups, lines, my_dp, *refs):
    out = refs[-1]
    for g, steps in enumerate(groups):
        pieces = refs[g * lines : (g + 1) * lines]
        cols = pieces[0].shape[1] // len(steps)
        total = pieces[0][...].astype(F32)
        for piece in pieces[1:]:
            total += piece[...].astype(F32)
        total = total.astype(BF16)
        for k, step in enumerate(steps):
            at = pl.multiple_of((my_dp[0] ^ step) * cols, cols)
            out[:, pl.ds(at, cols)] = total[:, k * cols : (k + 1) * cols]


def product(near, hidden, downs, lines, flops, after=()):
    (mixed,) = call(
        functools.partial(product_kernel, len(downs), near),
        [((lines, hidden.shape[1] // 2 // lines, len(downs) * downs[0].shape[2]), BF16)],
        [VMEM] * (1 + len(downs)) + [ANY] * len(after),
        (hidden, *downs, *after),
        flops,
        2 * len(downs) * downs[0].size,
    )
    return mixed


def tensor_sum_pieces(mine, theirs):
    lines = mine.shape[0]
    my_line = lax.axis_index("tensor") // 2
    pair = mine.astype(F32) + swap(theirs, "tensor", 1).astype(F32)
    pair = pair.astype(BF16)
    pieces = [lax.dynamic_index_in_dim(pair, my_line ^ k, 0, keepdims=False) for k in range(lines)]
    return [pieces[0]] + [swap(pieces[k], "tensor", 2 * k) for k in range(1, lines)]


def on_device(tokens, gate_weight, up_weight, down_weight, router_weight, carry_mean):
    dp = lax.axis_size("dp")
    tensor = lax.axis_size("tensor")
    lines = tensor // 2
    my_dp = lax.axis_index("dp").reshape(1)
    core = (lax.axis_index("tensor") % 2).reshape(1)
    own_rows, width = tokens.shape
    own_segs = own_rows // SEG
    assert own_segs == 1
    rows = own_rows // tensor
    experts, depth, hidden_count = gate_weight.shape
    cols = down_weight.shape[2]
    segs = dp * own_segs

    extra = -(-(own_segs + 1) // 16) * 16
    quarter = own_rows // 4
    own, *sends = call(
        functools.partial(prepare_kernel, dp, own_segs, rows),
        [((own_rows, depth), BF16)]
        + [((quarter + extra, depth), BF16)] * (dp - 1)
        + [((quarter, depth), BF16)] * (dp - 1),
        [SMEM, SMEM, HBM, HBM, HBM],
        (my_dp, core, *map(in_hbm, (tokens, router_weight.T, carry_mean.reshape(1, width)))),
        2 * extra * own_rows * width,
        4 * own_rows * width,
        [
            pltpu.VMEM((dp, own_rows, depth), BF16),
            pltpu.VMEM((experts, width), F32),
            pltpu.VMEM((1, width), F32),
            pltpu.SemaphoreType.DMA((dp + 2,)),
        ],
    )
    firsts = [swap(sends[k - 1], "dp", k) for k in range(1, dp)]
    seconds = [swap(sends[dp + k - 2], "dp", k) for k in range(1, dp)]
    (down,) = load((down_weight,), own)
    block = 32 if hidden_count % 32 == 0 else 16
    (mix,) = call(
        functools.partial(route_kernel, dp, own_segs, block),
        [((segs * block, experts * block), BF16)],
        [SMEM] + [VMEM] * dp + [ANY],
        (my_dp, sends[0], *firsts, down),
        0,
        2 * own_rows * depth,
    )
    merged_down = merge(mix, dp, own_segs, (down,), 2 * mix.size * down.size // experts // block)
    downs = [block if k == 0 else swap(block, "dp", k) for k, block in enumerate(merged_down)]
    gate_t, up_t = load(
        (jnp.swapaxes(gate_weight, 1, 2), jnp.swapaxes(up_weight, 1, 2)), merged_down[0]
    )
    (stacked,) = call(
        functools.partial(stack_kernel, dp),
        [((dp - 1, own_rows // 2, depth), BF16)],
        [VMEM] * (2 * dp - 2) + [ANY],
        (*firsts, *seconds, up_t),
        0,
        2 * own_rows * width,
    )
    other = swap(stacked, "tensor", 1)
    merged = merge(mix, dp, own_segs, (gate_t, up_t), BESIDE)
    partial_pre = preact(own, stacked, other, merged)
    parts = [partial_pre[0]] + [swap(partial_pre[k], "dp", k) for k in range(1, dp)]

    early, late = tuple(range(dp - 1)), (dp - 1,)
    downs_early, downs_late = [downs[k] for k in early], [downs[k] for k in late]
    hidden, theirs = call(
        functools.partial(hidden_kernel, dp),
        [((hidden_count, SEG), BF16), ((lines, rows, len(early) * cols), BF16)],
        [VMEM] * (dp + len(early)),
        (*parts, *downs_early),
        own_rows * hidden_count * cols * len(early),
        2 * (own_rows * hidden_count * dp * 2 + hidden_count * cols * len(early)),
    )
    mine = product(True, hidden, downs_early, lines, BESIDE)
    early_pieces = tensor_sum_pieces(mine, theirs)
    flops = own_rows * hidden_count * cols
    theirs = product(False, hidden, downs_late, lines, flops, early_pieces[1:])
    mine = product(True, hidden, downs_late, lines, BESIDE)
    late_pieces = tensor_sum_pieces(mine, theirs)
    (out,) = call(
        functools.partial(finish_kernel, (early, late), lines),
        [((rows, width), BF16)],
        [SMEM] + [VMEM] * (2 * lines),
        (my_dp, *early_pieces, *late_pieces),
        rows * width * lines,
        2 * rows * width * (lines + 1),
    )
    return out


def solution(mesh):
    placed = (
        P("dp", None),
        P(None, "dp", "tensor"),
        P(None, "dp", "tensor"),
        P(None, "tensor", "dp"),
        P(),
        P(),
    )
    return jax.shard_map(
        on_device, mesh=mesh, in_specs=placed, out_specs=P(("dp", "tensor"), None), check_vma=False
    )
```

```python
import functools

import jax
import jax.numpy as jnp
from jax import lax
from jax.experimental import pallas as pl
from jax.experimental.pallas import tpu as pltpu
from jax.sharding import PartitionSpec as P

SEG = 256
SOFT_CAP = 8.0
VMEM = pl.BlockSpec(memory_space=pltpu.VMEM)
SMEM = pl.BlockSpec(memory_space=pltpu.SMEM)
F32 = jnp.float32
BF16 = jnp.bfloat16
LANES = 128
BESIDE = 10**10
HBM = pl.BlockSpec(memory_space=pltpu.HBM)
ANY = pl.BlockSpec(memory_space=pl.ANY)


def swap(value, axis, step):
    count = lax.axis_size(axis)
    return lax.ppermute(value, axis, [(i, i ^ step) for i in range(count)])


def in_hbm(value):
    return pltpu.with_memory_space_constraint(value, pltpu.HBM)


def call(kernel, outs, in_specs, args, flops, moved, scratch=()):
    return pl.pallas_call(
        kernel,
        out_shape=[jax.ShapeDtypeStruct(shape, dtype) for shape, dtype in outs],
        in_specs=in_specs,
        out_specs=[VMEM] * len(outs),
        scratch_shapes=list(scratch),
        compiler_params=pltpu.CompilerParams(vmem_limit_bytes=24 * 2**20),
        cost_estimate=pl.CostEstimate(flops=flops, bytes_accessed=moved, transcendentals=0),
    )(*args)


def prepare_kernel(dp, own_segs, my_dp, core, tokens, router, carry, own, *refs):
    firsts, seconds = refs[: dp - 1], refs[dp - 1 : 2 * dp - 2]
    blocks, routers, carries, sems = refs[2 * dp - 2 :]
    rows, depth = own.shape
    half = rows // 2
    quarter = half // 2
    extra = firsts[0].shape[0] - quarter
    experts = router.shape[0]
    columns = [pl.multiple_of((my_dp[0] ^ k) * depth, depth) for k in range(dp)]
    copies = [
        pltpu.make_async_copy(
            tokens.at[:, pl.ds(columns[k], depth)],
            own if k == 0 else blocks.at[k - 1],
            sems.at[k],
        )
        for k in range(dp)
    ]
    copies.append(pltpu.make_async_copy(router, routers, sems.at[dp]))
    copies.append(pltpu.make_async_copy(carry, carries, sems.at[dp + 1]))
    for copy in copies[dp:] + copies[:dp]:
        copy.start()
    member = lax.broadcasted_iota(jnp.int32, (extra, rows), 1) // SEG
    ones = member == lax.broadcasted_iota(jnp.int32, (extra, rows), 0)
    ones = jnp.where(ones, 1.0, 0.0).astype(BF16)
    start = pl.multiple_of(core[0] * half, quarter)
    for copy in copies:
        copy.wait()
    totals = [jnp.zeros((experts, depth), F32)] * (own_segs + 1)
    for k in range(dp):
        block = own[...] if k == 0 else blocks[k - 1]
        weight = routers[:, pl.ds(columns[k], depth)]
        means = jnp.dot(ones, block, preferred_element_type=F32) / SEG
        for j in range(own_segs):
            totals[j] += means[j : j + 1, :] * weight
        totals[own_segs] += carries[:, pl.ds(columns[k], depth)] * weight
        if k > 0:
            firsts[k - 1][:quarter] = blocks[k - 1, pl.ds(start, quarter), :]
            seconds[k - 1][...] = blocks[k - 1, pl.ds(start + quarter, quarter), :]
    lane = lax.broadcasted_iota(jnp.int32, (experts, LANES), 1)
    place = lane % experts == lax.broadcasted_iota(jnp.int32, (experts, LANES), 0)
    row = lax.broadcasted_iota(jnp.int32, (extra, LANES), 0)
    lane = lax.broadcasted_iota(jnp.int32, (extra, LANES), 1)
    logits = jnp.zeros((extra, LANES), F32)
    for j, total in enumerate(totals):
        column = jnp.sum(total, axis=1, keepdims=True)
        spread = jnp.sum(jnp.where(place, column, 0.0), axis=0, keepdims=True)
        logits = jnp.where(row == j, spread, logits)
    high = logits.astype(BF16).astype(F32)
    middle = (logits - high).astype(BF16).astype(F32)
    low = logits - high - middle
    terms = jnp.where(lane < experts, high, jnp.where(lane < 2 * experts, middle, low))
    terms = jnp.where(lane < 3 * experts, terms, 0.0).astype(BF16)
    for first in firsts:
        first[quarter:] = jnp.zeros((extra, depth), BF16)
        first[quarter:, :LANES] = terms


def load_kernel(count, *refs):
    sources, targets, sems = refs[:count], refs[-count - 1 : -1], refs[-1]
    copies = [
        pltpu.make_async_copy(source, target, sems.at[i])
        for i, (source, target) in enumerate(zip(sources, targets))
    ]
    for copy in copies:
        copy.start()
    for copy in copies:
        copy.wait()


def read_table(piece, tokens, experts):
    lane = lax.broadcasted_iota(jnp.int32, (LANES, experts), 0)
    summed = lane % experts == lax.broadcasted_iota(jnp.int32, (LANES, experts), 1)
    summed = jnp.where(summed & (lane < 3 * experts), 1.0, 0.0).astype(BF16)
    return jnp.dot(piece[tokens:, :LANES], summed, preferred_element_type=F32)


def load(weights, after):
    count = len(weights)
    return call(
        functools.partial(load_kernel, count),
        [(weight.shape, BF16) for weight in weights],
        [HBM] * count + [ANY],
        (*map(in_hbm, weights), after),
        0,
        4 * count * weights[0].size,
        [pltpu.SemaphoreType.DMA((count,))],
    )


def spread_probs(my_dp, tables, own_segs, experts, steps, block):
    raws = []
    for k in steps:
        for j in range(own_segs):
            prior = (my_dp ^ k) * own_segs + j - 1
            raw = tables[0][own_segs : own_segs + 1, :]
            for q, table in enumerate(tables):
                for i in range(own_segs):
                    here = (my_dp ^ q) * own_segs + i == prior
                    raw = jnp.where(here, table[i : i + 1, :], raw)
            raws.append(raw)
    logits = SOFT_CAP * jnp.tanh(jnp.concatenate(raws, axis=0) / SOFT_CAP)
    scores = jnp.exp(logits)
    probs = (scores / jnp.sum(scores, axis=1, keepdims=True)).astype(BF16).astype(F32)
    shape = (experts, experts * block)
    ahead = lax.broadcasted_iota(jnp.int32, shape, 1) // block
    spread = jnp.where(ahead == lax.broadcasted_iota(jnp.int32, shape, 0), 1.0, 0.0)
    wide = jnp.dot(probs, spread, preferred_element_type=F32)
    shape = (block, experts * block)
    diagonal = lax.broadcasted_iota(jnp.int32, shape, 1) % block == lax.broadcasted_iota(
        jnp.int32, shape, 0
    )
    return jnp.concatenate(
        [jnp.where(diagonal, wide[s : s + 1, :], 0.0) for s in range(len(raws))], axis=0
    ).astype(BF16)


def route_kernel(dp, own_segs, block, my_dp, *refs):
    pieces, mix = refs[:dp], refs[-1]
    experts = mix.shape[1] // block
    tables = [read_table(piece, own_segs * SEG // 4, experts) for piece in pieces]
    mix[...] = spread_probs(my_dp[0], tables, own_segs, experts, tuple(range(dp)), block)


def stack_kernel(dp, *refs):
    firsts, seconds, stacked = refs[: dp - 1], refs[dp - 1 : 2 * dp - 2], refs[-1]
    quarter = seconds[0].shape[0]
    for k in range(dp - 1):
        stacked[k, :quarter] = firsts[k][:quarter]
        stacked[k, quarter:] = seconds[k][...]


def merge_kernel(own_segs, mix, *refs):
    weights, outs = refs
    experts, rows, cols = weights[0].shape
    block = mix.shape[1] // experts
    for w, weight in enumerate(weights):
        for start in range(0, rows, block):
            tile = weight[:, start : start + block, :].reshape(experts * block, cols)
            out = jnp.dot(mix[...], tile, preferred_element_type=F32).astype(BF16)
            out = out.reshape(len(outs), own_segs, block, cols)
            at = w * rows + start
            for k in range(len(outs)):
                outs[k][:, at : at + block, :] = out[k]


def merge(mix, dp, own_segs, weights, flops):
    experts, rows, cols = weights[0].shape
    total = rows * len(weights)
    count = len(weights)

    def kernel(mix_ref, *refs):
        merge_kernel(own_segs, mix_ref, refs[:count], refs[-dp:])

    return call(
        kernel,
        [((own_segs, total, cols), BF16)] * dp,
        [VMEM] * (1 + count),
        (mix, *weights),
        flops,
        2 * total * cols * (experts + dp * own_segs),
    )


def preact_kernel(dp, core, own, brought, other, *refs):
    merged, outs, whole = refs[:dp], refs[dp : 2 * dp], refs[-1]
    half = own.shape[0] // 2
    near = pl.multiple_of(core[0] * half, half)
    far = pl.multiple_of((1 - core[0]) * half, half)
    for k in range(dp - 1, -1, -1):
        if k > 0:
            whole[k - 1, pl.ds(near, half), :] = brought[k - 1]
            whole[k - 1, pl.ds(far, half), :] = other[k - 1]
        for j in range(merged[k].shape[0]):
            rows = slice(j * SEG, (j + 1) * SEG)
            outs[k][j] = lax.dot_general(
                merged[k][j],
                own[rows, :] if k == 0 else whole[k - 1, rows, :],
                (((1,), (1,)), ((), ())),
                preferred_element_type=F32,
            ).astype(BF16)


def preact(core, own, brought, other, merged):
    dp = len(merged)
    own_segs, total, depth = merged[0].shape
    segs = dp * own_segs
    return call(
        functools.partial(preact_kernel, dp),
        [((own_segs, total, SEG), BF16)] * dp,
        [SMEM] + [VMEM] * (dp + 3),
        (core, own, brought, other, *merged),
        2 * segs * total * SEG * depth,
        2 * segs * (total * depth + SEG * depth + total * SEG),
        [pltpu.VMEM((dp - 1, own_segs * SEG, depth), BF16)],
    )


def down_columns(core, hidden, downs, mixed):
    cols = downs[0].shape[2]
    rows = mixed.shape[2]
    for j, part in enumerate(hidden):
        for k, down in enumerate(downs):
            out = lax.dot_general(
                part, down[j], (((0,), (0,)), ((), ())), preferred_element_type=F32
            ).astype(BF16)
            for i in range(SEG // rows):
                at = j * (SEG // rows) + i
                mixed[(at % 2) ^ core, at // 2, :, k * cols : (k + 1) * cols] = out[
                    i * rows : (i + 1) * rows
                ]


def first_kernel(dp, core, *refs):
    parts, downs, hidden, mixed = refs[:dp], refs[dp:-2], refs[-2], refs[-1]
    half = hidden.shape[1]
    kept = []
    for j in range(hidden.shape[0]):
        total = parts[0][j].astype(F32)
        for part in parts[1:]:
            total += part[j].astype(F32)
        gate, up = total[:half], total[half:]
        kept.append((gate / (1.0 + jnp.exp(-gate)) * up).astype(BF16))
        hidden[j] = kept[j]
    down_columns(core[0], kept, downs, mixed)


def second_kernel(count, core, hidden, *refs):
    kept = [hidden[j] for j in range(hidden.shape[0])]
    down_columns(core[0], kept, refs[:count], refs[-1])


def finish_kernel(groups, lines, my_dp, *refs):
    out = refs[-1]
    for g, steps in enumerate(groups):
        pieces = refs[g * lines : (g + 1) * lines]
        cols = pieces[0].shape[1] // len(steps)
        total = pieces[0][...].astype(F32)
        for piece in pieces[1:]:
            total += piece[...].astype(F32)
        total = total.astype(BF16)
        for k, step in enumerate(steps):
            at = pl.multiple_of((my_dp[0] ^ step) * cols, cols)
            out[:, pl.ds(at, cols)] = total[:, k * cols : (k + 1) * cols]


def tensor_sum_pieces(mixed, lines):
    my_line = lax.axis_index("tensor") // 2
    pair = mixed[0].astype(F32) + swap(mixed[1], "tensor", 1).astype(F32)
    pair = pair.astype(BF16)
    pieces = [lax.dynamic_index_in_dim(pair, my_line ^ k, 0, keepdims=False) for k in range(lines)]
    return [swap(pieces[k], "tensor", 2 * k) for k in range(lines - 1, 0, -1)] + [pieces[0]]


def on_device(tokens, gate_weight, up_weight, down_weight, router_weight, carry_mean):
    dp = lax.axis_size("dp")
    tensor = lax.axis_size("tensor")
    lines = tensor // 2
    my_dp = lax.axis_index("dp").reshape(1)
    core = (lax.axis_index("tensor") % 2).reshape(1)
    own_rows, width = tokens.shape
    own_segs = own_rows // SEG
    experts, depth, hidden_count = gate_weight.shape
    cols = down_weight.shape[2]
    segs = dp * own_segs

    extra = -(-(own_segs + 1) // 16) * 16
    quarter = own_rows // 4
    own, *sends = call(
        functools.partial(prepare_kernel, dp, own_segs),
        [((own_rows, depth), BF16)]
        + [((quarter + extra, depth), BF16)] * (dp - 1)
        + [((quarter, depth), BF16)] * (dp - 1),
        [SMEM, SMEM, HBM, HBM, HBM],
        (my_dp, core, *map(in_hbm, (tokens, router_weight.T, carry_mean.reshape(1, width)))),
        2 * extra * own_rows * width,
        4 * own_rows * width,
        [
            pltpu.VMEM((dp - 1, own_rows, depth), BF16),
            pltpu.VMEM((experts, width), F32),
            pltpu.VMEM((1, width), F32),
            pltpu.SemaphoreType.DMA((dp + 2,)),
        ],
    )
    firsts = [swap(sends[k - 1], "dp", k) for k in range(1, dp)]
    seconds = [swap(sends[dp + k - 2], "dp", k) for k in range(1, dp)]
    (down,) = load((down_weight,), own)
    block = 32 if hidden_count % 32 == 0 else 16
    (mix,) = call(
        functools.partial(route_kernel, dp, own_segs, block),
        [((segs * block, experts * block), BF16)],
        [SMEM] + [VMEM] * dp + [ANY],
        (my_dp, sends[0], *firsts, down),
        0,
        2 * own_rows * depth,
    )
    merged_down = merge(mix, dp, own_segs, (down,), 2 * mix.size * down.size // experts // block)
    downs = [block if k == 0 else swap(block, "dp", k) for k, block in enumerate(merged_down)]
    gate_up = (jnp.swapaxes(gate_weight, 1, 2), jnp.swapaxes(up_weight, 1, 2))
    (stacked,) = call(
        functools.partial(stack_kernel, dp),
        [((dp - 1, own_rows // 2, depth), BF16)],
        [VMEM] * (2 * dp - 2) + [ANY],
        (*firsts, *seconds, merged_down[0]),
        0,
        2 * own_rows * width,
    )
    other = swap(stacked, "tensor", 1)
    merged = merge(mix, dp, own_segs, gate_up, BESIDE)
    partial_pre = preact(core, own, stacked, other, merged)
    parts = [partial_pre[0]] + [swap(partial_pre[k], "dp", k) for k in range(1, dp)]

    rows = own_rows // tensor
    early, late = tuple(range(dp - 1)), (dp - 1,)
    flops = 2 * own_rows * hidden_count * cols
    hidden, mixed = call(
        functools.partial(first_kernel, dp),
        [((own_segs, hidden_count, SEG), BF16), ((2, lines, rows, len(early) * cols), BF16)],
        [SMEM] + [VMEM] * (dp + len(early)),
        (core, *parts, *[downs[k] for k in early]),
        flops * len(early),
        2 * (own_rows * hidden_count * dp * 2 + hidden_count * cols * len(early)),
    )
    early_pieces = tensor_sum_pieces(mixed, lines)
    (mixed,) = call(
        functools.partial(second_kernel, len(late)),
        [((2, lines, rows, len(late) * cols), BF16)],
        [SMEM] + [VMEM] * (1 + len(late)) + [ANY] * lines,
        (core, hidden, *[downs[k] for k in late], *early_pieces),
        flops * len(late),
        2 * (own_rows * hidden_count + hidden_count * cols * len(late)),
    )
    late_pieces = tensor_sum_pieces(mixed, lines)
    (out,) = call(
        functools.partial(finish_kernel, (early, late), lines),
        [((rows, width), BF16)],
        [SMEM] + [VMEM] * (2 * lines),
        (my_dp, *early_pieces, *late_pieces),
        rows * width * lines,
        2 * rows * width * (lines + 1),
    )
    return out


def solution(mesh):
    placed = (
        P("dp", None),
        P(None, "dp", "tensor"),
        P(None, "dp", "tensor"),
        P(None, "tensor", "dp"),
        P(),
        P(),
    )
    return jax.shard_map(
        on_device, mesh=mesh, in_specs=placed, out_specs=P(("dp", "tensor"), None), check_vma=False
    )
```

```python
import functools

import jax
import jax.numpy as jnp
from jax import lax
from jax.experimental import pallas as pl
from jax.experimental.pallas import tpu as pltpu
from jax.sharding import PartitionSpec as P

SEG = 256
SOFT_CAP = 8.0
VMEM = pl.BlockSpec(memory_space=pltpu.VMEM)
SMEM = pl.BlockSpec(memory_space=pltpu.SMEM)
F32 = jnp.float32
BF16 = jnp.bfloat16
LANES = 128
BESIDE = 10**10
HBM = pl.BlockSpec(memory_space=pltpu.HBM)
ANY = pl.BlockSpec(memory_space=pl.ANY)


def swap(value, axis, step):
    count = lax.axis_size(axis)
    return lax.ppermute(value, axis, [(i, i ^ step) for i in range(count)])


def in_hbm(value):
    return pltpu.with_memory_space_constraint(value, pltpu.HBM)


def call(kernel, outs, in_specs, args, flops, moved, scratch=()):
    return pl.pallas_call(
        kernel,
        out_shape=[jax.ShapeDtypeStruct(shape, dtype) for shape, dtype in outs],
        in_specs=in_specs,
        out_specs=[VMEM] * len(outs),
        scratch_shapes=list(scratch),
        compiler_params=pltpu.CompilerParams(vmem_limit_bytes=24 * 2**20),
        cost_estimate=pl.CostEstimate(flops=flops, bytes_accessed=moved, transcendentals=0),
    )(*args)


def prepare_kernel(dp, own_segs, my_dp, core, tokens, router, carry, own, *refs):
    firsts, seconds = refs[: dp - 1], refs[dp - 1 : 2 * dp - 2]
    blocks, routers, carries, sems = refs[2 * dp - 2 :]
    rows, depth = own.shape
    half = rows // 2
    quarter = half // 2
    extra = firsts[0].shape[0] - quarter
    experts = router.shape[0]
    columns = [pl.multiple_of((my_dp[0] ^ k) * depth, depth) for k in range(dp)]
    copies = [
        pltpu.make_async_copy(
            tokens.at[:, pl.ds(columns[k], depth)],
            own if k == 0 else blocks.at[k - 1],
            sems.at[k],
        )
        for k in range(dp)
    ]
    copies.append(pltpu.make_async_copy(router, routers, sems.at[dp]))
    copies.append(pltpu.make_async_copy(carry, carries, sems.at[dp + 1]))
    for copy in copies[dp:] + copies[:dp]:
        copy.start()
    member = lax.broadcasted_iota(jnp.int32, (extra, rows), 1) // SEG
    ones = member == lax.broadcasted_iota(jnp.int32, (extra, rows), 0)
    ones = jnp.where(ones, 1.0, 0.0).astype(BF16)
    start = pl.multiple_of(core[0] * half, quarter)
    for copy in copies:
        copy.wait()
    totals = [jnp.zeros((experts, depth), F32)] * (own_segs + 1)
    for k in range(dp):
        block = own[...] if k == 0 else blocks[k - 1]
        weight = routers[:, pl.ds(columns[k], depth)]
        means = jnp.dot(ones, block, preferred_element_type=F32) / SEG
        for j in range(own_segs):
            totals[j] += means[j : j + 1, :] * weight
        totals[own_segs] += carries[:, pl.ds(columns[k], depth)] * weight
        if k > 0:
            firsts[k - 1][:quarter] = blocks[k - 1, pl.ds(start, quarter), :]
            seconds[k - 1][...] = blocks[k - 1, pl.ds(start + quarter, quarter), :]
    lane = lax.broadcasted_iota(jnp.int32, (experts, LANES), 1)
    place = lane % experts == lax.broadcasted_iota(jnp.int32, (experts, LANES), 0)
    row = lax.broadcasted_iota(jnp.int32, (extra, LANES), 0)
    lane = lax.broadcasted_iota(jnp.int32, (extra, LANES), 1)
    logits = jnp.zeros((extra, LANES), F32)
    for j, total in enumerate(totals):
        column = jnp.sum(total, axis=1, keepdims=True)
        spread = jnp.sum(jnp.where(place, column, 0.0), axis=0, keepdims=True)
        logits = jnp.where(row == j, spread, logits)
    high = logits.astype(BF16).astype(F32)
    middle = (logits - high).astype(BF16).astype(F32)
    low = logits - high - middle
    terms = jnp.where(lane < experts, high, jnp.where(lane < 2 * experts, middle, low))
    terms = jnp.where(lane < 3 * experts, terms, 0.0).astype(BF16)
    for first in firsts:
        first[quarter:] = jnp.zeros((extra, depth), BF16)
        first[quarter:, :LANES] = terms


def read_table(piece, tokens, experts):
    lane = lax.broadcasted_iota(jnp.int32, (LANES, experts), 0)
    summed = lane % experts == lax.broadcasted_iota(jnp.int32, (LANES, experts), 1)
    summed = jnp.where(summed & (lane < 3 * experts), 1.0, 0.0).astype(BF16)
    return jnp.dot(piece[tokens:, :LANES], summed, preferred_element_type=F32)


def spread_probs(my_dp, tables, own_segs, experts, steps, block):
    raws = []
    for k in steps:
        for j in range(own_segs):
            prior = (my_dp ^ k) * own_segs + j - 1
            raw = tables[0][own_segs : own_segs + 1, :]
            for q, table in enumerate(tables):
                for i in range(own_segs):
                    here = (my_dp ^ q) * own_segs + i == prior
                    raw = jnp.where(here, table[i : i + 1, :], raw)
            raws.append(raw)
    logits = SOFT_CAP * jnp.tanh(jnp.concatenate(raws, axis=0) / SOFT_CAP)
    scores = jnp.exp(logits)
    probs = (scores / jnp.sum(scores, axis=1, keepdims=True)).astype(BF16).astype(F32)
    shape = (experts, experts * block)
    ahead = lax.broadcasted_iota(jnp.int32, shape, 1) // block
    spread = jnp.where(ahead == lax.broadcasted_iota(jnp.int32, shape, 0), 1.0, 0.0)
    wide = jnp.dot(probs, spread, preferred_element_type=F32)
    shape = (block, experts * block)
    diagonal = lax.broadcasted_iota(jnp.int32, shape, 1) % block == lax.broadcasted_iota(
        jnp.int32, shape, 0
    )
    return jnp.concatenate(
        [jnp.where(diagonal, wide[s : s + 1, :], 0.0) for s in range(len(raws))], axis=0
    ).astype(BF16)


def route_kernel(dp, own_segs, block, my_dp, *refs):
    pieces, mix = refs[:dp], refs[-1]
    experts = mix.shape[1] // block
    tables = [read_table(piece, own_segs * SEG // 4, experts) for piece in pieces]
    mix[...] = spread_probs(my_dp[0], tables, own_segs, experts, tuple(range(dp)), block)


def stack_kernel(dp, *refs):
    firsts, seconds, stacked = refs[: dp - 1], refs[dp - 1 : 2 * dp - 2], refs[-1]
    quarter = seconds[0].shape[0]
    for k in range(dp - 1):
        stacked[k, :quarter] = firsts[k][:quarter]
        stacked[k, quarter:] = seconds[k][...]


def merge_kernel(own_segs, mix, *refs):
    weights, outs = refs
    experts, rows, cols = weights[0].shape
    block = mix.shape[1] // experts
    for w, weight in enumerate(weights):
        for start in range(0, rows, block):
            tile = weight[:, start : start + block, :].reshape(experts * block, cols)
            out = jnp.dot(mix[...], tile, preferred_element_type=F32).astype(BF16)
            out = out.reshape(len(outs), own_segs, block, cols)
            at = w * rows + start
            for k in range(len(outs)):
                outs[k][:, at : at + block, :] = out[k]


def merge(mix, dp, own_segs, weights, flops):
    experts, rows, cols = weights[0].shape
    total = rows * len(weights)
    count = len(weights)

    def kernel(mix_ref, *refs):
        merge_kernel(own_segs, mix_ref, refs[:count], refs[-dp:])

    return call(
        kernel,
        [((own_segs, total, cols), BF16)] * dp,
        [VMEM] * (1 + count),
        (mix, *weights),
        flops,
        2 * total * cols * (experts + dp * own_segs),
    )


def preact_kernel(dp, core, own, brought, other, *refs):
    merged, outs, whole = refs[:dp], refs[dp : 2 * dp], refs[-1]
    half = own.shape[0] // 2
    near = pl.multiple_of(core[0] * half, half)
    far = pl.multiple_of((1 - core[0]) * half, half)
    for k in range(dp - 1, -1, -1):
        if k > 0:
            whole[k - 1, pl.ds(near, half), :] = brought[k - 1]
            whole[k - 1, pl.ds(far, half), :] = other[k - 1]
        for j in range(merged[k].shape[0]):
            rows = slice(j * SEG, (j + 1) * SEG)
            outs[k][j] = lax.dot_general(
                merged[k][j],
                own[rows, :] if k == 0 else whole[k - 1, rows, :],
                (((1,), (1,)), ((), ())),
                preferred_element_type=F32,
            ).astype(BF16)


def preact(core, own, brought, other, merged):
    dp = len(merged)
    own_segs, total, depth = merged[0].shape
    segs = dp * own_segs
    return call(
        functools.partial(preact_kernel, dp),
        [((own_segs, total, SEG), BF16)] * dp,
        [SMEM] + [VMEM] * (dp + 3),
        (core, own, brought, other, *merged),
        2 * segs * total * SEG * depth,
        2 * segs * (total * depth + SEG * depth + total * SEG),
        [pltpu.VMEM((dp - 1, own_segs * SEG, depth), BF16)],
    )


def down_columns(core, hidden, downs, mixed):
    cols = downs[0].shape[2]
    rows = mixed.shape[2]
    for j, part in enumerate(hidden):
        for k, down in enumerate(downs):
            out = lax.dot_general(
                part, down[j], (((0,), (0,)), ((), ())), preferred_element_type=F32
            ).astype(BF16)
            for i in range(SEG // rows):
                at = j * (SEG // rows) + i
                mixed[(at % 2) ^ core, at // 2, :, k * cols : (k + 1) * cols] = out[
                    i * rows : (i + 1) * rows
                ]


def first_kernel(dp, core, *refs):
    parts, downs, hidden, mixed = refs[:dp], refs[dp:-2], refs[-2], refs[-1]
    half = hidden.shape[1]
    kept = []
    for j in range(hidden.shape[0]):
        total = parts[0][j].astype(F32)
        for part in parts[1:]:
            total += part[j].astype(F32)
        gate, up = total[:half], total[half:]
        kept.append((gate / (1.0 + jnp.exp(-gate)) * up).astype(BF16))
        hidden[j] = kept[j]
    down_columns(core[0], kept, downs, mixed)


def second_kernel(count, core, hidden, *refs):
    kept = [hidden[j] for j in range(hidden.shape[0])]
    down_columns(core[0], kept, refs[:count], refs[-1])


def finish_kernel(groups, lines, my_dp, *refs):
    out = refs[-1]
    for g, steps in enumerate(groups):
        pieces = refs[g * lines : (g + 1) * lines]
        cols = pieces[0].shape[1] // len(steps)
        total = pieces[0][...].astype(F32)
        for piece in pieces[1:]:
            total += piece[...].astype(F32)
        total = total.astype(BF16)
        for k, step in enumerate(steps):
            at = pl.multiple_of((my_dp[0] ^ step) * cols, cols)
            out[:, pl.ds(at, cols)] = total[:, k * cols : (k + 1) * cols]


def tensor_sum_pieces(mixed, lines):
    my_line = lax.axis_index("tensor") // 2
    pair = mixed[0].astype(F32) + swap(mixed[1], "tensor", 1).astype(F32)
    pair = pair.astype(BF16)
    pieces = [lax.dynamic_index_in_dim(pair, my_line ^ k, 0, keepdims=False) for k in range(lines)]
    return [swap(pieces[k], "tensor", 2 * k) for k in range(lines - 1, 0, -1)] + [pieces[0]]


def on_device(tokens, gate_weight, up_weight, down_weight, router_weight, carry_mean):
    dp = lax.axis_size("dp")
    tensor = lax.axis_size("tensor")
    lines = tensor // 2
    my_dp = lax.axis_index("dp").reshape(1)
    core = (lax.axis_index("tensor") % 2).reshape(1)
    own_rows, width = tokens.shape
    own_segs = own_rows // SEG
    experts, depth, hidden_count = gate_weight.shape
    cols = down_weight.shape[2]
    segs = dp * own_segs

    extra = -(-(own_segs + 1) // 16) * 16
    quarter = own_rows // 4
    own, *sends = call(
        functools.partial(prepare_kernel, dp, own_segs),
        [((own_rows, depth), BF16)]
        + [((quarter + extra, depth), BF16)] * (dp - 1)
        + [((quarter, depth), BF16)] * (dp - 1),
        [SMEM, SMEM, HBM, HBM, HBM],
        (my_dp, core, *map(in_hbm, (tokens, router_weight.T, carry_mean.reshape(1, width)))),
        BESIDE,
        4 * own_rows * width,
        [
            pltpu.VMEM((dp - 1, own_rows, depth), BF16),
            pltpu.VMEM((experts, width), F32),
            pltpu.VMEM((1, width), F32),
            pltpu.SemaphoreType.DMA((dp + 2,)),
        ],
    )
    firsts = [swap(sends[k - 1], "dp", k) for k in range(1, dp)]
    seconds = [swap(sends[dp + k - 2], "dp", k) for k in range(1, dp)]
    block = 32 if hidden_count % 32 == 0 else 16
    (mix,) = call(
        functools.partial(route_kernel, dp, own_segs, block),
        [((segs * block, experts * block), BF16)],
        [SMEM] + [VMEM] * dp,
        (my_dp, sends[0], *firsts),
        0,
        2 * own_rows * depth,
    )
    merged_down = merge(mix, dp, own_segs, (down_weight,), 2 * mix.size * down_weight.size // experts // block)
    downs = [block if k == 0 else swap(block, "dp", k) for k, block in enumerate(merged_down)]
    gate_up = (jnp.swapaxes(gate_weight, 1, 2), jnp.swapaxes(up_weight, 1, 2))
    (stacked,) = call(
        functools.partial(stack_kernel, dp),
        [((dp - 1, own_rows // 2, depth), BF16)],
        [VMEM] * (2 * dp - 2) + [ANY],
        (*firsts, *seconds, merged_down[0]),
        0,
        2 * own_rows * width,
    )
    other = swap(stacked, "tensor", 1)
    merged = merge(mix, dp, own_segs, gate_up, BESIDE)
    partial_pre = preact(core, own, stacked, other, merged)
    parts = [partial_pre[0]] + [swap(partial_pre[k], "dp", k) for k in range(1, dp)]

    rows = own_rows // tensor
    early, late = tuple(range(dp - 1)), (dp - 1,)
    flops = 2 * own_rows * hidden_count * cols
    hidden, mixed = call(
        functools.partial(first_kernel, dp),
        [((own_segs, hidden_count, SEG), BF16), ((2, lines, rows, len(early) * cols), BF16)],
        [SMEM] + [VMEM] * (dp + len(early)),
        (core, *parts, *[downs[k] for k in early]),
        flops * len(early),
        2 * (own_rows * hidden_count * dp * 2 + hidden_count * cols * len(early)),
    )
    early_pieces = tensor_sum_pieces(mixed, lines)
    (mixed,) = call(
        functools.partial(second_kernel, len(late)),
        [((2, lines, rows, len(late) * cols), BF16)],
        [SMEM] + [VMEM] * (1 + len(late)) + [ANY] * lines,
        (core, hidden, *[downs[k] for k in late], *early_pieces),
        flops * len(late),
        2 * (own_rows * hidden_count + hidden_count * cols * len(late)),
    )
    late_pieces = tensor_sum_pieces(mixed, lines)
    (out,) = call(
        functools.partial(finish_kernel, (early, late), lines),
        [((rows, width), BF16)],
        [SMEM] + [VMEM] * (2 * lines),
        (my_dp, *early_pieces, *late_pieces),
        rows * width * lines,
        2 * rows * width * (lines + 1),
    )
    return out


def solution(mesh):
    placed = (
        P("dp", None),
        P(None, "dp", "tensor"),
        P(None, "dp", "tensor"),
        P(None, "tensor", "dp"),
        P(),
        P(),
    )
    return jax.shard_map(
        on_device, mesh=mesh, in_specs=placed, out_specs=P(("dp", "tensor"), None), check_vma=False
    )
```

```python
import functools

import jax
import jax.numpy as jnp
from jax import lax
from jax.experimental import pallas as pl
from jax.experimental.pallas import tpu as pltpu
from jax.sharding import PartitionSpec as P

SEG = 256
SOFT_CAP = 8.0
VMEM = pl.BlockSpec(memory_space=pltpu.VMEM)
SMEM = pl.BlockSpec(memory_space=pltpu.SMEM)
F32 = jnp.float32
BF16 = jnp.bfloat16
LANES = 128
BESIDE = 10**10
HBM = pl.BlockSpec(memory_space=pltpu.HBM)
ANY = pl.BlockSpec(memory_space=pl.ANY)


def swap(value, axis, step):
    count = lax.axis_size(axis)
    return lax.ppermute(value, axis, [(i, i ^ step) for i in range(count)])


def in_hbm(value):
    return pltpu.with_memory_space_constraint(value, pltpu.HBM)


def call(kernel, outs, in_specs, args, flops, moved, scratch=()):
    return pl.pallas_call(
        kernel,
        out_shape=[jax.ShapeDtypeStruct(shape, dtype) for shape, dtype in outs],
        in_specs=in_specs,
        out_specs=[VMEM] * len(outs),
        scratch_shapes=list(scratch),
        compiler_params=pltpu.CompilerParams(vmem_limit_bytes=24 * 2**20),
        cost_estimate=pl.CostEstimate(flops=flops, bytes_accessed=moved, transcendentals=0),
    )(*args)


def prepare_kernel(dp, own_segs, my_dp, core, tokens, router, carry, own, *refs):
    firsts, seconds = refs[: dp - 1], refs[dp - 1 : 2 * dp - 2]
    blocks, routers, carries, sems = refs[2 * dp - 2 :]
    rows, depth = own.shape
    half = rows // 2
    quarter = half // 2
    extra = firsts[0].shape[0] - quarter
    experts = router.shape[0]
    columns = [pl.multiple_of((my_dp[0] ^ k) * depth, depth) for k in range(dp)]
    copies = [
        pltpu.make_async_copy(
            tokens.at[:, pl.ds(columns[k], depth)],
            own if k == 0 else blocks.at[k - 1],
            sems.at[k],
        )
        for k in range(dp)
    ]
    copies.append(pltpu.make_async_copy(router, routers, sems.at[dp]))
    copies.append(pltpu.make_async_copy(carry, carries, sems.at[dp + 1]))
    for copy in copies[dp:] + copies[:dp]:
        copy.start()
    member = lax.broadcasted_iota(jnp.int32, (extra, rows), 1) // SEG
    ones = member == lax.broadcasted_iota(jnp.int32, (extra, rows), 0)
    ones = jnp.where(ones, 1.0, 0.0).astype(BF16)
    start = pl.multiple_of(core[0] * half, quarter)
    for copy in copies:
        copy.wait()
    totals = [jnp.zeros((experts, depth), F32)] * (own_segs + 1)
    for k in range(dp):
        block = own[...] if k == 0 else blocks[k - 1]
        weight = routers[:, pl.ds(columns[k], depth)]
        means = jnp.dot(ones, block, preferred_element_type=F32) / SEG
        for j in range(own_segs):
            totals[j] += means[j : j + 1, :] * weight
        totals[own_segs] += carries[:, pl.ds(columns[k], depth)] * weight
        if k > 0:
            firsts[k - 1][:quarter] = blocks[k - 1, pl.ds(start, quarter), :]
            seconds[k - 1][...] = blocks[k - 1, pl.ds(start + quarter, quarter), :]
    lane = lax.broadcasted_iota(jnp.int32, (experts, LANES), 1)
    place = lane % experts == lax.broadcasted_iota(jnp.int32, (experts, LANES), 0)
    row = lax.broadcasted_iota(jnp.int32, (extra, LANES), 0)
    lane = lax.broadcasted_iota(jnp.int32, (extra, LANES), 1)
    logits = jnp.zeros((extra, LANES), F32)
    for j, total in enumerate(totals):
        column = jnp.sum(total, axis=1, keepdims=True)
        spread = jnp.sum(jnp.where(place, column, 0.0), axis=0, keepdims=True)
        logits = jnp.where(row == j, spread, logits)
    high = logits.astype(BF16).astype(F32)
    middle = (logits - high).astype(BF16).astype(F32)
    low = logits - high - middle
    terms = jnp.where(lane < experts, high, jnp.where(lane < 2 * experts, middle, low))
    terms = jnp.where(lane < 3 * experts, terms, 0.0).astype(BF16)
    for first in firsts:
        first[quarter:] = jnp.zeros((extra, depth), BF16)
        first[quarter:, :LANES] = terms


def read_table(piece, tokens, experts):
    lane = lax.broadcasted_iota(jnp.int32, (LANES, experts), 0)
    summed = lane % experts == lax.broadcasted_iota(jnp.int32, (LANES, experts), 1)
    summed = jnp.where(summed & (lane < 3 * experts), 1.0, 0.0).astype(BF16)
    return jnp.dot(piece[tokens:, :LANES], summed, preferred_element_type=F32)


def spread_probs(my_dp, tables, own_segs, experts, steps, block):
    raws = []
    for k in steps:
        for j in range(own_segs):
            prior = (my_dp ^ k) * own_segs + j - 1
            raw = tables[0][own_segs : own_segs + 1, :]
            for q, table in enumerate(tables):
                for i in range(own_segs):
                    here = (my_dp ^ q) * own_segs + i == prior
                    raw = jnp.where(here, table[i : i + 1, :], raw)
            raws.append(raw)
    logits = SOFT_CAP * jnp.tanh(jnp.concatenate(raws, axis=0) / SOFT_CAP)
    scores = jnp.exp(logits)
    probs = (scores / jnp.sum(scores, axis=1, keepdims=True)).astype(BF16).astype(F32)
    shape = (experts, experts * block)
    ahead = lax.broadcasted_iota(jnp.int32, shape, 1) // block
    spread = jnp.where(ahead == lax.broadcasted_iota(jnp.int32, shape, 0), 1.0, 0.0)
    wide = jnp.dot(probs, spread, preferred_element_type=F32)
    shape = (block, experts * block)
    diagonal = lax.broadcasted_iota(jnp.int32, shape, 1) % block == lax.broadcasted_iota(
        jnp.int32, shape, 0
    )
    return jnp.concatenate(
        [jnp.where(diagonal, wide[s : s + 1, :], 0.0) for s in range(len(raws))], axis=0
    ).astype(BF16)


def route_kernel(dp, own_segs, block, my_dp, *refs):
    pieces, mix = refs[:dp], refs[-1]
    experts = mix.shape[1] // block
    tables = [read_table(piece, own_segs * SEG // 4, experts) for piece in pieces]
    mix[...] = spread_probs(my_dp[0], tables, own_segs, experts, tuple(range(dp)), block)


def stack_kernel(dp, *refs):
    firsts, seconds, stacked = refs[: dp - 1], refs[dp - 1 : 2 * dp - 2], refs[-1]
    quarter = seconds[0].shape[0]
    for k in range(dp - 1):
        stacked[k, :quarter] = firsts[k][:quarter]
        stacked[k, quarter:] = seconds[k][...]


def merge_kernel(own_segs, mix, *refs):
    weights, outs = refs
    experts, rows, cols = weights[0].shape
    block = mix.shape[1] // experts
    for w, weight in enumerate(weights):
        for start in range(0, rows, block):
            tile = weight[:, start : start + block, :].reshape(experts * block, cols)
            out = jnp.dot(mix[...], tile, preferred_element_type=F32).astype(BF16)
            out = out.reshape(len(outs), own_segs, block, cols)
            at = w * rows + start
            for k in range(len(outs)):
                outs[k][:, at : at + block, :] = out[k]


def merge(mix, dp, own_segs, weights, flops):
    experts, rows, cols = weights[0].shape
    total = rows * len(weights)
    count = len(weights)

    def kernel(mix_ref, *refs):
        merge_kernel(own_segs, mix_ref, refs[:count], refs[-dp:])

    return call(
        kernel,
        [((own_segs, total, cols), BF16)] * dp,
        [VMEM] * (1 + count),
        (mix, *weights),
        flops,
        2 * total * cols * (experts + dp * own_segs),
    )


def preact_kernel(dp, core, own, brought, other, *refs):
    merged, outs, whole = refs[:dp], refs[dp : 2 * dp], refs[-1]
    half = own.shape[0] // 2
    near = pl.multiple_of(core[0] * half, half)
    far = pl.multiple_of((1 - core[0]) * half, half)
    for k in range(dp - 1, -1, -1):
        if k > 0:
            whole[k - 1, pl.ds(near, half), :] = brought[k - 1]
            whole[k - 1, pl.ds(far, half), :] = other[k - 1]
        for j in range(merged[k].shape[0]):
            rows = slice(j * SEG, (j + 1) * SEG)
            outs[k][j] = lax.dot_general(
                merged[k][j],
                own[rows, :] if k == 0 else whole[k - 1, rows, :],
                (((1,), (1,)), ((), ())),
                preferred_element_type=F32,
            ).astype(BF16)


def preact(core, own, brought, other, merged):
    dp = len(merged)
    own_segs, total, depth = merged[0].shape
    segs = dp * own_segs
    return call(
        functools.partial(preact_kernel, dp),
        [((own_segs, total, SEG), BF16)] * dp,
        [SMEM] + [VMEM] * (dp + 3),
        (core, own, brought, other, *merged),
        2 * segs * total * SEG * depth,
        2 * segs * (total * depth + SEG * depth + total * SEG),
        [pltpu.VMEM((dp - 1, own_segs * SEG, depth), BF16)],
    )


def down_columns(core, hidden, downs, mixed):
    cols = downs[0].shape[2]
    rows = mixed.shape[2]
    for j, part in enumerate(hidden):
        for k, down in enumerate(downs):
            out = lax.dot_general(
                part, down[j], (((0,), (0,)), ((), ())), preferred_element_type=F32
            ).astype(BF16)
            for i in range(SEG // rows):
                at = j * (SEG // rows) + i
                mixed[(at % 2) ^ core, at // 2, :, k * cols : (k + 1) * cols] = out[
                    i * rows : (i + 1) * rows
                ]


def first_kernel(dp, core, *refs):
    parts, downs, hidden, mixed = refs[:dp], refs[dp:-2], refs[-2], refs[-1]
    half = hidden.shape[1]
    kept = []
    for j in range(hidden.shape[0]):
        total = parts[0][j].astype(F32)
        for part in parts[1:]:
            total += part[j].astype(F32)
        gate, up = total[:half], total[half:]
        kept.append((gate / (1.0 + jnp.exp(-gate)) * up).astype(BF16))
        hidden[j] = kept[j]
    down_columns(core[0], kept, downs, mixed)


def second_kernel(count, core, hidden, *refs):
    kept = [hidden[j] for j in range(hidden.shape[0])]
    down_columns(core[0], kept, refs[:count], refs[-1])


def sum_kernel(*refs):
    total = refs[0][...].astype(F32)
    for piece in refs[1:-1]:
        total += piece[...].astype(F32)
    refs[-1][...] = total.astype(BF16)


def copy_kernel(source, target):
    target[...] = source[0]


def finish_kernel(groups, my_dp, early, *refs):
    out = refs[-1]
    total = refs[0][...].astype(F32)
    for piece in refs[1:-1]:
        total += piece[...].astype(F32)
    for value, steps in zip((early[...], total.astype(BF16)), groups):
        cols = value.shape[1] // len(steps)
        for k, step in enumerate(steps):
            at = pl.multiple_of((my_dp[0] ^ step) * cols, cols)
            out[:, pl.ds(at, cols)] = value[:, k * cols : (k + 1) * cols]


def tensor_sum_pieces(mixed, lines, beside):
    my_line = lax.axis_index("tensor") // 2
    mine = mixed[0]
    if beside:
        (mine,) = call(copy_kernel, [(mine.shape, BF16)], [VMEM], (mixed,), BESIDE, 0)
    pair = mine.astype(F32) + swap(mixed[1], "tensor", 1).astype(F32)
    pair = pair.astype(BF16)
    pieces = [lax.dynamic_index_in_dim(pair, my_line ^ k, 0, keepdims=False) for k in range(lines)]
    return [swap(pieces[k], "tensor", 2 * k) for k in range(lines - 1, 0, -1)] + [pieces[0]]


def on_device(tokens, gate_weight, up_weight, down_weight, router_weight, carry_mean):
    dp = lax.axis_size("dp")
    tensor = lax.axis_size("tensor")
    lines = tensor // 2
    my_dp = lax.axis_index("dp").reshape(1)
    core = (lax.axis_index("tensor") % 2).reshape(1)
    own_rows, width = tokens.shape
    own_segs = own_rows // SEG
    experts, depth, hidden_count = gate_weight.shape
    cols = down_weight.shape[2]
    segs = dp * own_segs

    extra = -(-(own_segs + 1) // 16) * 16
    quarter = own_rows // 4
    own, *sends = call(
        functools.partial(prepare_kernel, dp, own_segs),
        [((own_rows, depth), BF16)]
        + [((quarter + extra, depth), BF16)] * (dp - 1)
        + [((quarter, depth), BF16)] * (dp - 1),
        [SMEM, SMEM, HBM, HBM, HBM],
        (my_dp, core, *map(in_hbm, (tokens, router_weight.T, carry_mean.reshape(1, width)))),
        BESIDE,
        4 * own_rows * width,
        [
            pltpu.VMEM((dp - 1, own_rows, depth), BF16),
            pltpu.VMEM((experts, width), F32),
            pltpu.VMEM((1, width), F32),
            pltpu.SemaphoreType.DMA((dp + 2,)),
        ],
    )
    firsts = [swap(sends[k - 1], "dp", k) for k in range(1, dp)]
    seconds = [swap(sends[dp + k - 2], "dp", k) for k in range(1, dp)]
    block = 32 if hidden_count % 32 == 0 else 16
    (mix,) = call(
        functools.partial(route_kernel, dp, own_segs, block),
        [((segs * block, experts * block), BF16)],
        [SMEM] + [VMEM] * dp,
        (my_dp, sends[0], *firsts),
        0,
        2 * own_rows * depth,
    )
    merged_down = merge(mix, dp, own_segs, (down_weight,), 2 * mix.size * down_weight.size // experts // block)
    downs = [block if k == 0 else swap(block, "dp", k) for k, block in enumerate(merged_down)]
    gate_up = (jnp.swapaxes(gate_weight, 1, 2), jnp.swapaxes(up_weight, 1, 2))
    (stacked,) = call(
        functools.partial(stack_kernel, dp),
        [((dp - 1, own_rows // 2, depth), BF16)],
        [VMEM] * (2 * dp - 2) + [ANY],
        (*firsts, *seconds, merged_down[0]),
        0,
        2 * own_rows * width,
    )
    other = swap(stacked, "tensor", 1)
    merged = merge(mix, dp, own_segs, gate_up, BESIDE)
    partial_pre = preact(core, own, stacked, other, merged)
    parts = [partial_pre[0]] + [swap(partial_pre[k], "dp", k) for k in range(1, dp)]

    rows = own_rows // tensor
    early, late = tuple(range(dp - 1)), (dp - 1,)
    flops = 2 * own_rows * hidden_count * cols
    hidden, mixed = call(
        functools.partial(first_kernel, dp),
        [((own_segs, hidden_count, SEG), BF16), ((2, lines, rows, len(early) * cols), BF16)],
        [SMEM] + [VMEM] * (dp + len(early)),
        (core, *parts, *[downs[k] for k in early]),
        flops * len(early),
        2 * (own_rows * hidden_count * dp * 2 + hidden_count * cols * len(early)),
    )
    early_pieces = tensor_sum_pieces(mixed, lines, False)
    (mixed,) = call(
        functools.partial(second_kernel, len(late)),
        [((2, lines, rows, len(late) * cols), BF16)],
        [SMEM] + [VMEM] * (1 + len(late)) + [ANY],
        (core, hidden, *[downs[k] for k in late], early_pieces[0]),
        flops * len(late),
        2 * (own_rows * hidden_count + hidden_count * cols * len(late)),
    )
    late_pieces = tensor_sum_pieces(mixed, lines, True)
    (early_sum,) = call(
        sum_kernel,
        [(early_pieces[0].shape, BF16)],
        [VMEM] * lines,
        early_pieces,
        BESIDE,
        2 * rows * width * lines,
    )
    (out,) = call(
        functools.partial(finish_kernel, (early, late)),
        [((rows, width), BF16)],
        [SMEM] + [VMEM] * (1 + lines),
        (my_dp, early_sum, *late_pieces),
        rows * width * lines,
        2 * rows * width * (lines + 1),
    )
    return out


def solution(mesh):
    placed = (
        P("dp", None),
        P(None, "dp", "tensor"),
        P(None, "dp", "tensor"),
        P(None, "tensor", "dp"),
        P(),
        P(),
    )
    return jax.shard_map(
        on_device, mesh=mesh, in_specs=placed, out_specs=P(("dp", "tensor"), None), check_vma=False
    )
```

```python
import functools

import jax
import jax.numpy as jnp
from jax import lax
from jax.experimental import pallas as pl
from jax.experimental.pallas import tpu as pltpu
from jax.sharding import PartitionSpec as P

SEG = 256
SOFT_CAP = 8.0
VMEM = pl.BlockSpec(memory_space=pltpu.VMEM)
SMEM = pl.BlockSpec(memory_space=pltpu.SMEM)
F32 = jnp.float32
BF16 = jnp.bfloat16
LANES = 128
BESIDE = 10**10
HBM = pl.BlockSpec(memory_space=pltpu.HBM)
ANY = pl.BlockSpec(memory_space=pl.ANY)


def swap(value, axis, step):
    count = lax.axis_size(axis)
    return lax.ppermute(value, axis, [(i, i ^ step) for i in range(count)])


def in_hbm(value):
    return pltpu.with_memory_space_constraint(value, pltpu.HBM)


def call(kernel, outs, in_specs, args, flops, moved, scratch=()):
    return pl.pallas_call(
        kernel,
        out_shape=[jax.ShapeDtypeStruct(shape, dtype) for shape, dtype in outs],
        in_specs=in_specs,
        out_specs=[VMEM] * len(outs),
        scratch_shapes=list(scratch),
        compiler_params=pltpu.CompilerParams(vmem_limit_bytes=24 * 2**20),
        cost_estimate=pl.CostEstimate(flops=flops, bytes_accessed=moved, transcendentals=0),
    )(*args)


def prepare_kernel(dp, own_segs, my_dp, core, tokens, router, carry, own, *refs):
    firsts, seconds = refs[: dp - 1], refs[dp - 1 : 2 * dp - 2]
    blocks, routers, carries, sems = refs[2 * dp - 2 :]
    rows, depth = own.shape
    half = rows // 2
    quarter = half // 2
    extra = firsts[0].shape[0] - quarter
    experts = router.shape[0]
    columns = [pl.multiple_of((my_dp[0] ^ k) * depth, depth) for k in range(dp)]
    copies = [
        pltpu.make_async_copy(
            tokens.at[:, pl.ds(columns[k], depth)],
            own if k == 0 else blocks.at[k - 1],
            sems.at[k],
        )
        for k in range(dp)
    ]
    copies.append(pltpu.make_async_copy(router, routers, sems.at[dp]))
    copies.append(pltpu.make_async_copy(carry, carries, sems.at[dp + 1]))
    for copy in copies[dp:] + copies[:dp]:
        copy.start()
    member = lax.broadcasted_iota(jnp.int32, (extra, rows), 1) // SEG
    ones = member == lax.broadcasted_iota(jnp.int32, (extra, rows), 0)
    ones = jnp.where(ones, 1.0, 0.0).astype(BF16)
    start = pl.multiple_of(core[0] * half, quarter)
    for copy in copies:
        copy.wait()
    totals = [jnp.zeros((experts, depth), F32)] * (own_segs + 1)
    for k in range(dp):
        block = own[...] if k == 0 else blocks[k - 1]
        weight = routers[:, pl.ds(columns[k], depth)]
        means = jnp.dot(ones, block, preferred_element_type=F32) / SEG
        for j in range(own_segs):
            totals[j] += means[j : j + 1, :] * weight
        totals[own_segs] += carries[:, pl.ds(columns[k], depth)] * weight
        if k > 0:
            firsts[k - 1][:quarter] = blocks[k - 1, pl.ds(start, quarter), :]
            seconds[k - 1][...] = blocks[k - 1, pl.ds(start + quarter, quarter), :]
    lane = lax.broadcasted_iota(jnp.int32, (experts, LANES), 1)
    place = lane % experts == lax.broadcasted_iota(jnp.int32, (experts, LANES), 0)
    row = lax.broadcasted_iota(jnp.int32, (extra, LANES), 0)
    lane = lax.broadcasted_iota(jnp.int32, (extra, LANES), 1)
    logits = jnp.zeros((extra, LANES), F32)
    for j, total in enumerate(totals):
        column = jnp.sum(total, axis=1, keepdims=True)
        spread = jnp.sum(jnp.where(place, column, 0.0), axis=0, keepdims=True)
        logits = jnp.where(row == j, spread, logits)
    high = logits.astype(BF16).astype(F32)
    middle = (logits - high).astype(BF16).astype(F32)
    low = logits - high - middle
    terms = jnp.where(lane < experts, high, jnp.where(lane < 2 * experts, middle, low))
    terms = jnp.where(lane < 3 * experts, terms, 0.0).astype(BF16)
    for first in firsts:
        first[quarter:] = jnp.zeros((extra, depth), BF16)
        first[quarter:, :LANES] = terms


def read_table(piece, tokens, experts):
    lane = lax.broadcasted_iota(jnp.int32, (LANES, experts), 0)
    summed = lane % experts == lax.broadcasted_iota(jnp.int32, (LANES, experts), 1)
    summed = jnp.where(summed & (lane < 3 * experts), 1.0, 0.0).astype(BF16)
    return jnp.dot(piece[tokens:, :LANES], summed, preferred_element_type=F32)


def spread_probs(my_dp, tables, own_segs, experts, steps, block):
    raws = []
    for k in steps:
        for j in range(own_segs):
            prior = (my_dp ^ k) * own_segs + j - 1
            raw = tables[0][own_segs : own_segs + 1, :]
            for q, table in enumerate(tables):
                for i in range(own_segs):
                    here = (my_dp ^ q) * own_segs + i == prior
                    raw = jnp.where(here, table[i : i + 1, :], raw)
            raws.append(raw)
    logits = SOFT_CAP * jnp.tanh(jnp.concatenate(raws, axis=0) / SOFT_CAP)
    scores = jnp.exp(logits)
    probs = (scores / jnp.sum(scores, axis=1, keepdims=True)).astype(BF16).astype(F32)
    shape = (experts, experts * block)
    ahead = lax.broadcasted_iota(jnp.int32, shape, 1) // block
    spread = jnp.where(ahead == lax.broadcasted_iota(jnp.int32, shape, 0), 1.0, 0.0)
    wide = jnp.dot(probs, spread, preferred_element_type=F32)
    shape = (block, experts * block)
    diagonal = lax.broadcasted_iota(jnp.int32, shape, 1) % block == lax.broadcasted_iota(
        jnp.int32, shape, 0
    )
    return jnp.concatenate(
        [jnp.where(diagonal, wide[s : s + 1, :], 0.0) for s in range(len(raws))], axis=0
    ).astype(BF16)


def route_kernel(dp, own_segs, block, my_dp, *refs):
    pieces, mix = refs[:dp], refs[-1]
    experts = mix.shape[1] // block
    tables = [read_table(piece, own_segs * SEG // 4, experts) for piece in pieces]
    mix[...] = spread_probs(my_dp[0], tables, own_segs, experts, tuple(range(dp)), block)


def stack_kernel(dp, *refs):
    firsts, seconds, stacked = refs[: dp - 1], refs[dp - 1 : 2 * dp - 2], refs[-1]
    quarter = seconds[0].shape[0]
    for k in range(dp - 1):
        stacked[k, :quarter] = firsts[k][:quarter]
        stacked[k, quarter:] = seconds[k][...]


def merge_kernel(own_segs, steps, mix, *refs):
    weights, outs = refs
    experts, rows, cols = weights[0].shape
    block = mix.shape[1] // experts
    size = own_segs * block
    rows_of = mix[steps[0] * size : (steps[-1] + 1) * size, :]
    for w, weight in enumerate(weights):
        for start in range(0, rows, block):
            tile = weight[:, start : start + block, :].reshape(experts * block, cols)
            out = jnp.dot(rows_of, tile, preferred_element_type=F32).astype(BF16)
            out = out.reshape(len(outs), own_segs, block, cols)
            at = w * rows + start
            for k in range(len(outs)):
                outs[k][:, at : at + block, :] = out[k]


def merge(mix, steps, own_segs, weights, flops, after=()):
    experts, rows, cols = weights[0].shape
    total = rows * len(weights)
    count = len(weights)

    def kernel(mix_ref, *refs):
        outs = refs[-len(steps) :]
        merge_kernel(own_segs, steps, mix_ref, refs[:count], outs)

    return call(
        kernel,
        [((own_segs, total, cols), BF16)] * len(steps),
        [VMEM] * (1 + count) + [ANY] * len(after),
        (mix, *weights, *after),
        flops,
        2 * total * cols * (experts + len(steps) * own_segs),
    )


def preact_kernel(dp, core, own, brought, other, *refs):
    merged, outs, whole = refs[:dp], refs[dp : 2 * dp], refs[-1]
    half = own.shape[0] // 2
    near = pl.multiple_of(core[0] * half, half)
    far = pl.multiple_of((1 - core[0]) * half, half)
    for k in range(dp - 1, -1, -1):
        if k > 0:
            whole[k - 1, pl.ds(near, half), :] = brought[k - 1]
            whole[k - 1, pl.ds(far, half), :] = other[k - 1]
        for j in range(merged[k].shape[0]):
            rows = slice(j * SEG, (j + 1) * SEG)
            outs[k][j] = lax.dot_general(
                merged[k][j],
                own[rows, :] if k == 0 else whole[k - 1, rows, :],
                (((1,), (1,)), ((), ())),
                preferred_element_type=F32,
            ).astype(BF16)


def preact(core, own, brought, other, merged):
    dp = len(merged)
    own_segs, total, depth = merged[0].shape
    segs = dp * own_segs
    return call(
        functools.partial(preact_kernel, dp),
        [((own_segs, total, SEG), BF16)] * dp,
        [SMEM] + [VMEM] * (dp + 3),
        (core, own, brought, other, *merged),
        2 * segs * total * SEG * depth,
        2 * segs * (total * depth + SEG * depth + total * SEG),
        [pltpu.VMEM((dp - 1, own_segs * SEG, depth), BF16)],
    )


def down_columns(core, hidden, downs, mixed):
    cols = downs[0].shape[2]
    rows = mixed.shape[2]
    for j, part in enumerate(hidden):
        for k, down in enumerate(downs):
            out = lax.dot_general(
                part, down[j], (((0,), (0,)), ((), ())), preferred_element_type=F32
            ).astype(BF16)
            for i in range(SEG // rows):
                at = j * (SEG // rows) + i
                mixed[(at % 2) ^ core, at // 2, :, k * cols : (k + 1) * cols] = out[
                    i * rows : (i + 1) * rows
                ]


def first_kernel(dp, core, *refs):
    parts, downs, hidden, mixed = refs[:dp], refs[dp:-3], refs[-2], refs[-1]
    half = hidden.shape[1]
    kept = []
    for j in range(hidden.shape[0]):
        total = parts[0][j].astype(F32)
        for part in parts[1:]:
            total += part[j].astype(F32)
        gate, up = total[:half], total[half:]
        kept.append((gate / (1.0 + jnp.exp(-gate)) * up).astype(BF16))
        hidden[j] = kept[j]
    down_columns(core[0], kept, downs, mixed)


def second_kernel(count, core, hidden, *refs):
    kept = [hidden[j] for j in range(hidden.shape[0])]
    down_columns(core[0], kept, refs[:count], refs[-1])


def sum_kernel(*refs):
    total = refs[0][...].astype(F32)
    for piece in refs[1:-1]:
        total += piece[...].astype(F32)
    refs[-1][...] = total.astype(BF16)


def copy_kernel(source, target):
    target[...] = source[0]


def finish_kernel(groups, my_dp, early, *refs):
    out = refs[-1]
    total = refs[0][...].astype(F32)
    for piece in refs[1:-1]:
        total += piece[...].astype(F32)
    for value, steps in zip((early[...], total.astype(BF16)), groups):
        cols = value.shape[1] // len(steps)
        for k, step in enumerate(steps):
            at = pl.multiple_of((my_dp[0] ^ step) * cols, cols)
            out[:, pl.ds(at, cols)] = value[:, k * cols : (k + 1) * cols]


def tensor_sum_pieces(mixed, lines, beside):
    my_line = lax.axis_index("tensor") // 2
    mine = mixed[0]
    if beside:
        (mine,) = call(copy_kernel, [(mine.shape, BF16)], [VMEM], (mixed,), BESIDE, 0)
    pair = mine.astype(F32) + swap(mixed[1], "tensor", 1).astype(F32)
    pair = pair.astype(BF16)
    pieces = [lax.dynamic_index_in_dim(pair, my_line ^ k, 0, keepdims=False) for k in range(lines)]
    return [swap(pieces[k], "tensor", 2 * k) for k in range(lines - 1, 0, -1)] + [pieces[0]]


def on_device(tokens, gate_weight, up_weight, down_weight, router_weight, carry_mean):
    dp = lax.axis_size("dp")
    tensor = lax.axis_size("tensor")
    lines = tensor // 2
    my_dp = lax.axis_index("dp").reshape(1)
    core = (lax.axis_index("tensor") % 2).reshape(1)
    own_rows, width = tokens.shape
    own_segs = own_rows // SEG
    experts, depth, hidden_count = gate_weight.shape
    cols = down_weight.shape[2]
    segs = dp * own_segs

    extra = -(-(own_segs + 1) // 16) * 16
    quarter = own_rows // 4
    own, *sends = call(
        functools.partial(prepare_kernel, dp, own_segs),
        [((own_rows, depth), BF16)]
        + [((quarter + extra, depth), BF16)] * (dp - 1)
        + [((quarter, depth), BF16)] * (dp - 1),
        [SMEM, SMEM, HBM, HBM, HBM],
        (my_dp, core, *map(in_hbm, (tokens, router_weight.T, carry_mean.reshape(1, width)))),
        BESIDE,
        4 * own_rows * width,
        [
            pltpu.VMEM((dp - 1, own_rows, depth), BF16),
            pltpu.VMEM((experts, width), F32),
            pltpu.VMEM((1, width), F32),
            pltpu.SemaphoreType.DMA((dp + 2,)),
        ],
    )
    firsts = [swap(sends[k - 1], "dp", k) for k in range(1, dp)]
    seconds = [swap(sends[dp + k - 2], "dp", k) for k in range(1, dp)]
    block = 32 if hidden_count % 32 == 0 else 16
    (mix,) = call(
        functools.partial(route_kernel, dp, own_segs, block),
        [((segs * block, experts * block), BF16)],
        [SMEM] + [VMEM] * dp,
        (my_dp, sends[0], *firsts),
        0,
        2 * own_rows * depth,
    )
    flops = 2 * mix.size * down_weight.size // experts // block
    merged_down = merge(mix, tuple(range(dp - 1)), own_segs, (down_weight,), flops)
    downs = [down if k == 0 else swap(down, "dp", k) for k, down in enumerate(merged_down)]
    gate_up = (jnp.swapaxes(gate_weight, 1, 2), jnp.swapaxes(up_weight, 1, 2))
    (stacked,) = call(
        functools.partial(stack_kernel, dp),
        [((dp - 1, own_rows // 2, depth), BF16)],
        [VMEM] * (2 * dp - 2) + [ANY],
        (*firsts, *seconds, merged_down[0]),
        0,
        2 * own_rows * width,
    )
    other = swap(stacked, "tensor", 1)
    merged = merge(mix, tuple(range(dp)), own_segs, gate_up, BESIDE)
    partial_pre = preact(core, own, stacked, other, merged)
    parts = [partial_pre[0]] + [swap(partial_pre[k], "dp", k) for k in range(1, dp)]

    rows = own_rows // tensor
    last = (dp - 1,)
    (down,) = merge(mix, last, own_segs, (down_weight,), flops // dp, (parts[1], *downs[1:]))
    downs.append(swap(down, "dp", dp - 1))
    early, late = tuple(range(dp - 1)), (dp - 1,)
    flops = 2 * own_rows * hidden_count * cols
    hidden, mixed = call(
        functools.partial(first_kernel, dp),
        [((own_segs, hidden_count, SEG), BF16), ((2, lines, rows, len(early) * cols), BF16)],
        [SMEM] + [VMEM] * (dp + len(early)) + [ANY],
        (core, *parts, *[downs[k] for k in early], down),
        flops * len(early),
        2 * (own_rows * hidden_count * dp * 2 + hidden_count * cols * len(early)),
    )
    early_pieces = tensor_sum_pieces(mixed, lines, True)
    (mixed,) = call(
        functools.partial(second_kernel, len(late)),
        [((2, lines, rows, len(late) * cols), BF16)],
        [SMEM] + [VMEM] * (1 + len(late)) + [ANY],
        (core, hidden, *[downs[k] for k in late], early_pieces[0]),
        flops * len(late),
        2 * (own_rows * hidden_count + hidden_count * cols * len(late)),
    )
    late_pieces = tensor_sum_pieces(mixed, lines, True)
    (early_sum,) = call(
        sum_kernel,
        [(early_pieces[0].shape, BF16)],
        [VMEM] * lines,
        early_pieces,
        BESIDE,
        2 * rows * width * lines,
    )
    (out,) = call(
        functools.partial(finish_kernel, (early, late)),
        [((rows, width), BF16)],
        [SMEM] + [VMEM] * (1 + lines),
        (my_dp, early_sum, *late_pieces),
        rows * width * lines,
        2 * rows * width * (lines + 1),
    )
    return out


def solution(mesh):
    placed = (
        P("dp", None),
        P(None, "dp", "tensor"),
        P(None, "dp", "tensor"),
        P(None, "tensor", "dp"),
        P(),
        P(),
    )
    return jax.shard_map(
        on_device, mesh=mesh, in_specs=placed, out_specs=P(("dp", "tensor"), None), check_vma=False
    )
```

```python
import functools

import jax
import jax.numpy as jnp
from jax import lax
from jax.experimental import pallas as pl
from jax.experimental.pallas import tpu as pltpu
from jax.sharding import PartitionSpec as P

SEG = 256
SOFT_CAP = 8.0
VMEM = pl.BlockSpec(memory_space=pltpu.VMEM)
SMEM = pl.BlockSpec(memory_space=pltpu.SMEM)
F32 = jnp.float32
BF16 = jnp.bfloat16
LANES = 128
BESIDE = 10**10
HBM = pl.BlockSpec(memory_space=pltpu.HBM)
ANY = pl.BlockSpec(memory_space=pl.ANY)


def swap(value, axis, step):
    count = lax.axis_size(axis)
    return lax.ppermute(value, axis, [(i, i ^ step) for i in range(count)])


def in_hbm(value):
    return pltpu.with_memory_space_constraint(value, pltpu.HBM)


def call(kernel, outs, in_specs, args, flops, moved, scratch=()):
    return pl.pallas_call(
        kernel,
        out_shape=[jax.ShapeDtypeStruct(shape, dtype) for shape, dtype in outs],
        in_specs=in_specs,
        out_specs=[VMEM] * len(outs),
        scratch_shapes=list(scratch),
        compiler_params=pltpu.CompilerParams(vmem_limit_bytes=24 * 2**20),
        cost_estimate=pl.CostEstimate(flops=flops, bytes_accessed=moved, transcendentals=0),
    )(*args)


def prepare_kernel(dp, own_segs, my_dp, core, tokens, router, carry, own, *refs):
    firsts, seconds = refs[: dp - 1], refs[dp - 1 : 2 * dp - 2]
    blocks, routers, carries, sems = refs[2 * dp - 2 :]
    rows, depth = own.shape
    half = rows // 2
    quarter = half // 2
    extra = firsts[0].shape[0] - quarter
    experts = router.shape[0]
    columns = [pl.multiple_of((my_dp[0] ^ k) * depth, depth) for k in range(dp)]
    copies = [
        pltpu.make_async_copy(
            tokens.at[:, pl.ds(columns[k], depth)],
            own if k == 0 else blocks.at[k - 1],
            sems.at[k],
        )
        for k in range(dp)
    ]
    copies.append(pltpu.make_async_copy(router, routers, sems.at[dp]))
    copies.append(pltpu.make_async_copy(carry, carries, sems.at[dp + 1]))
    for copy in copies[dp:] + copies[:dp]:
        copy.start()
    member = lax.broadcasted_iota(jnp.int32, (extra, rows), 1) // SEG
    ones = member == lax.broadcasted_iota(jnp.int32, (extra, rows), 0)
    ones = jnp.where(ones, 1.0, 0.0).astype(BF16)
    start = pl.multiple_of(core[0] * half, quarter)
    for copy in copies:
        copy.wait()
    totals = [jnp.zeros((experts, depth), F32)] * (own_segs + 1)
    for k in range(dp):
        block = own[...] if k == 0 else blocks[k - 1]
        weight = routers[:, pl.ds(columns[k], depth)]
        means = jnp.dot(ones, block, preferred_element_type=F32) / SEG
        for j in range(own_segs):
            totals[j] += means[j : j + 1, :] * weight
        totals[own_segs] += carries[:, pl.ds(columns[k], depth)] * weight
        if k > 0:
            firsts[k - 1][:quarter] = blocks[k - 1, pl.ds(start, quarter), :]
            seconds[k - 1][...] = blocks[k - 1, pl.ds(start + quarter, quarter), :]
    lane = lax.broadcasted_iota(jnp.int32, (experts, LANES), 1)
    place = lane % experts == lax.broadcasted_iota(jnp.int32, (experts, LANES), 0)
    row = lax.broadcasted_iota(jnp.int32, (extra, LANES), 0)
    lane = lax.broadcasted_iota(jnp.int32, (extra, LANES), 1)
    logits = jnp.zeros((extra, LANES), F32)
    for j, total in enumerate(totals):
        column = jnp.sum(total, axis=1, keepdims=True)
        spread = jnp.sum(jnp.where(place, column, 0.0), axis=0, keepdims=True)
        logits = jnp.where(row == j, spread, logits)
    high = logits.astype(BF16).astype(F32)
    middle = (logits - high).astype(BF16).astype(F32)
    low = logits - high - middle
    terms = jnp.where(lane < experts, high, jnp.where(lane < 2 * experts, middle, low))
    terms = jnp.where(lane < 3 * experts, terms, 0.0).astype(BF16)
    for first in firsts:
        first[quarter:] = jnp.zeros((extra, depth), BF16)
        first[quarter:, :LANES] = terms


def read_table(piece, tokens, experts):
    lane = lax.broadcasted_iota(jnp.int32, (LANES, experts), 0)
    summed = lane % experts == lax.broadcasted_iota(jnp.int32, (LANES, experts), 1)
    summed = jnp.where(summed & (lane < 3 * experts), 1.0, 0.0).astype(BF16)
    return jnp.dot(piece[tokens:, :LANES], summed, preferred_element_type=F32)


def spread_probs(my_dp, tables, own_segs, experts, steps, block):
    raws = []
    for k in steps:
        for j in range(own_segs):
            prior = (my_dp ^ k) * own_segs + j - 1
            raw = tables[0][own_segs : own_segs + 1, :]
            for q, table in enumerate(tables):
                for i in range(own_segs):
                    here = (my_dp ^ q) * own_segs + i == prior
                    raw = jnp.where(here, table[i : i + 1, :], raw)
            raws.append(raw)
    logits = SOFT_CAP * jnp.tanh(jnp.concatenate(raws, axis=0) / SOFT_CAP)
    scores = jnp.exp(logits)
    probs = (scores / jnp.sum(scores, axis=1, keepdims=True)).astype(BF16).astype(F32)
    shape = (experts, experts * block)
    ahead = lax.broadcasted_iota(jnp.int32, shape, 1) // block
    spread = jnp.where(ahead == lax.broadcasted_iota(jnp.int32, shape, 0), 1.0, 0.0)
    wide = jnp.dot(probs, spread, preferred_element_type=F32)
    shape = (block, experts * block)
    diagonal = lax.broadcasted_iota(jnp.int32, shape, 1) % block == lax.broadcasted_iota(
        jnp.int32, shape, 0
    )
    return jnp.concatenate(
        [jnp.where(diagonal, wide[s : s + 1, :], 0.0) for s in range(len(raws))], axis=0
    ).astype(BF16)


def route_kernel(dp, own_segs, block, my_dp, *refs):
    pieces, mix = refs[:dp], refs[-1]
    experts = mix.shape[1] // block
    tables = [read_table(piece, own_segs * SEG // 4, experts) for piece in pieces]
    mix[...] = spread_probs(my_dp[0], tables, own_segs, experts, tuple(range(dp)), block)


def stack_kernel(dp, *refs):
    firsts, seconds, stacked = refs[: dp - 1], refs[dp - 1 : 2 * dp - 2], refs[-1]
    quarter = seconds[0].shape[0]
    for k in range(dp - 1):
        stacked[k, :quarter] = firsts[k][:quarter]
        stacked[k, quarter:] = seconds[k][...]


def merge_kernel(own_segs, mix, *refs):
    weights, outs = refs
    experts, rows, cols = weights[0].shape
    block = mix.shape[1] // experts
    for w, weight in enumerate(weights):
        for start in range(0, rows, block):
            tile = weight[:, start : start + block, :].reshape(experts * block, cols)
            out = jnp.dot(mix[...], tile, preferred_element_type=F32).astype(BF16)
            out = out.reshape(len(outs), own_segs, block, cols)
            at = w * rows + start
            for k in range(len(outs)):
                outs[k][:, at : at + block, :] = out[k]


def merge(mix, dp, own_segs, weights, flops):
    experts, rows, cols = weights[0].shape
    total = rows * len(weights)
    count = len(weights)

    def kernel(mix_ref, *refs):
        merge_kernel(own_segs, mix_ref, refs[:count], refs[-dp:])

    return call(
        kernel,
        [((own_segs, total, cols), BF16)] * dp,
        [VMEM] * (1 + count),
        (mix, *weights),
        flops,
        2 * total * cols * (experts + dp * own_segs),
    )


def preact_kernel(dp, core, own, brought, other, *refs):
    merged, outs, whole = refs[:dp], refs[dp : 2 * dp], refs[-1]
    half = own.shape[0] // 2
    near = pl.multiple_of(core[0] * half, half)
    far = pl.multiple_of((1 - core[0]) * half, half)
    for k in range(dp - 1, -1, -1):
        if k > 0:
            whole[k - 1, pl.ds(near, half), :] = brought[k - 1]
            whole[k - 1, pl.ds(far, half), :] = other[k - 1]
        for j in range(merged[k].shape[0]):
            rows = slice(j * SEG, (j + 1) * SEG)
            outs[k][j] = lax.dot_general(
                merged[k][j],
                own[rows, :] if k == 0 else whole[k - 1, rows, :],
                (((1,), (1,)), ((), ())),
                preferred_element_type=F32,
            ).astype(BF16)


def preact(core, own, brought, other, merged):
    dp = len(merged)
    own_segs, total, depth = merged[0].shape
    segs = dp * own_segs
    return call(
        functools.partial(preact_kernel, dp),
        [((own_segs, total, SEG), BF16)] * dp,
        [SMEM] + [VMEM] * (dp + 3),
        (core, own, brought, other, *merged),
        2 * segs * total * SEG * depth,
        2 * segs * (total * depth + SEG * depth + total * SEG),
        [pltpu.VMEM((dp - 1, own_segs * SEG, depth), BF16)],
    )


def down_columns(core, hidden, downs, mixed):
    cols = downs[0].shape[2]
    rows = mixed.shape[2]
    for j, part in enumerate(hidden):
        for k, down in enumerate(downs):
            out = lax.dot_general(
                part, down[j], (((0,), (0,)), ((), ())), preferred_element_type=F32
            ).astype(BF16)
            for i in range(SEG // rows):
                at = j * (SEG // rows) + i
                mixed[(at % 2) ^ core, at // 2, :, k * cols : (k + 1) * cols] = out[
                    i * rows : (i + 1) * rows
                ]


def first_kernel(dp, core, *refs):
    parts, downs, hidden, mixed = refs[:dp], refs[dp:-2], refs[-2], refs[-1]
    half = hidden.shape[1]
    kept = []
    for j in range(hidden.shape[0]):
        total = parts[0][j].astype(F32)
        for part in parts[1:]:
            total += part[j].astype(F32)
        gate, up = total[:half], total[half:]
        kept.append((gate / (1.0 + jnp.exp(-gate)) * up).astype(BF16))
        hidden[j] = kept[j]
    down_columns(core[0], kept, downs, mixed)


def second_kernel(count, core, hidden, *refs):
    kept = [hidden[j] for j in range(hidden.shape[0])]
    down_columns(core[0], kept, refs[:count], refs[-1])


def sum_kernel(*refs):
    total = refs[0][...].astype(F32)
    for piece in refs[1:-1]:
        total += piece[...].astype(F32)
    refs[-1][...] = total.astype(BF16)


def copy_kernel(source, target):
    target[...] = source[0]


def finish_kernel(groups, my_dp, early, *refs):
    out = refs[-1]
    total = refs[0][...].astype(F32)
    for piece in refs[1:-1]:
        total += piece[...].astype(F32)
    for value, steps in zip((early[...], total.astype(BF16)), groups):
        cols = value.shape[1] // len(steps)
        for k, step in enumerate(steps):
            at = pl.multiple_of((my_dp[0] ^ step) * cols, cols)
            out[:, pl.ds(at, cols)] = value[:, k * cols : (k + 1) * cols]


def tensor_sum_pieces(mixed, lines, beside):
    my_line = lax.axis_index("tensor") // 2
    mine = mixed[0]
    if beside:
        (mine,) = call(copy_kernel, [(mine.shape, BF16)], [VMEM], (mixed,), BESIDE, 0)
    pair = mine.astype(F32) + swap(mixed[1], "tensor", 1).astype(F32)
    pair = pair.astype(BF16)
    pieces = [lax.dynamic_index_in_dim(pair, my_line ^ k, 0, keepdims=False) for k in range(lines)]
    return [swap(pieces[k], "tensor", 2 * k) for k in range(lines - 1, 0, -1)] + [pieces[0]]


def on_device(tokens, gate_weight, up_weight, down_weight, router_weight, carry_mean):
    dp = lax.axis_size("dp")
    tensor = lax.axis_size("tensor")
    lines = tensor // 2
    my_dp = lax.axis_index("dp").reshape(1)
    core = (lax.axis_index("tensor") % 2).reshape(1)
    own_rows, width = tokens.shape
    own_segs = own_rows // SEG
    experts, depth, hidden_count = gate_weight.shape
    cols = down_weight.shape[2]
    segs = dp * own_segs

    extra = -(-(own_segs + 1) // 16) * 16
    quarter = own_rows // 4
    own, *sends = call(
        functools.partial(prepare_kernel, dp, own_segs),
        [((own_rows, depth), BF16)]
        + [((quarter + extra, depth), BF16)] * (dp - 1)
        + [((quarter, depth), BF16)] * (dp - 1),
        [SMEM, SMEM, HBM, HBM, HBM],
        (my_dp, core, *map(in_hbm, (tokens, router_weight.T, carry_mean.reshape(1, width)))),
        BESIDE,
        4 * own_rows * width,
        [
            pltpu.VMEM((dp - 1, own_rows, depth), BF16),
            pltpu.VMEM((experts, width), F32),
            pltpu.VMEM((1, width), F32),
            pltpu.SemaphoreType.DMA((dp + 2,)),
        ],
    )
    firsts = [swap(sends[k - 1], "dp", k) for k in range(1, dp)]
    seconds = [swap(sends[dp + k - 2], "dp", k) for k in range(1, dp)]
    block = 32 if hidden_count % 32 == 0 else 16
    (mix,) = call(
        functools.partial(route_kernel, dp, own_segs, block),
        [((segs * block, experts * block), BF16)],
        [SMEM] + [VMEM] * dp,
        (my_dp, sends[0], *firsts),
        0,
        2 * own_rows * depth,
    )
    merged_down = merge(mix, dp, own_segs, (down_weight,), 2 * mix.size * down_weight.size // experts // block)
    downs = [block if k == 0 else swap(block, "dp", k) for k, block in enumerate(merged_down)]
    gate_up = (jnp.swapaxes(gate_weight, 1, 2), jnp.swapaxes(up_weight, 1, 2))
    (stacked,) = call(
        functools.partial(stack_kernel, dp),
        [((dp - 1, own_rows // 2, depth), BF16)],
        [VMEM] * (2 * dp - 2) + [ANY],
        (*firsts, *seconds, merged_down[0]),
        0,
        2 * own_rows * width,
    )
    other = swap(stacked, "tensor", 1)
    merged = merge(mix, dp, own_segs, gate_up, BESIDE)
    partial_pre = preact(core, own, stacked, other, merged)
    parts = [partial_pre[0]] + [swap(partial_pre[k], "dp", k) for k in range(1, dp)]

    rows = own_rows // tensor
    early, late = tuple(range(dp - 1)), (dp - 1,)
    flops = 2 * own_rows * hidden_count * cols
    hidden, mixed = call(
        functools.partial(first_kernel, dp),
        [((own_segs, hidden_count, SEG), BF16), ((2, lines, rows, len(early) * cols), BF16)],
        [SMEM] + [VMEM] * (dp + len(early)),
        (core, *parts, *[downs[k] for k in early]),
        flops * len(early),
        2 * (own_rows * hidden_count * dp * 2 + hidden_count * cols * len(early)),
    )
    early_pieces = tensor_sum_pieces(mixed, lines, False)
    (mixed,) = call(
        functools.partial(second_kernel, len(late)),
        [((2, lines, rows, len(late) * cols), BF16)],
        [SMEM] + [VMEM] * (1 + len(late)) + [ANY],
        (core, hidden, *[downs[k] for k in late], early_pieces[-2]),
        flops * len(late),
        2 * (own_rows * hidden_count + hidden_count * cols * len(late)),
    )
    late_pieces = tensor_sum_pieces(mixed, lines, True)
    (early_sum,) = call(
        sum_kernel,
        [(early_pieces[0].shape, BF16)],
        [VMEM] * lines,
        early_pieces,
        BESIDE,
        2 * rows * width * lines,
    )
    (out,) = call(
        functools.partial(finish_kernel, (early, late)),
        [((rows, width), BF16)],
        [SMEM] + [VMEM] * (1 + lines),
        (my_dp, early_sum, *late_pieces),
        rows * width * lines,
        2 * rows * width * (lines + 1),
    )
    return out


def solution(mesh):
    placed = (
        P("dp", None),
        P(None, "dp", "tensor"),
        P(None, "dp", "tensor"),
        P(None, "tensor", "dp"),
        P(),
        P(),
    )
    return jax.shard_map(
        on_device, mesh=mesh, in_specs=placed, out_specs=P(("dp", "tensor"), None), check_vma=False
    )
```

```python
import functools

import jax
import jax.numpy as jnp
from jax import lax
from jax.experimental import pallas as pl
from jax.experimental.pallas import tpu as pltpu
from jax.sharding import PartitionSpec as P

SEG = 256
SOFT_CAP = 8.0
VMEM = pl.BlockSpec(memory_space=pltpu.VMEM)
SMEM = pl.BlockSpec(memory_space=pltpu.SMEM)
F32 = jnp.float32
BF16 = jnp.bfloat16
LANES = 128
BESIDE = 10**10
HBM = pl.BlockSpec(memory_space=pltpu.HBM)
ANY = pl.BlockSpec(memory_space=pl.ANY)


def swap(value, axis, step):
    count = lax.axis_size(axis)
    return lax.ppermute(value, axis, [(i, i ^ step) for i in range(count)])


def in_hbm(value):
    return pltpu.with_memory_space_constraint(value, pltpu.HBM)


def call(kernel, outs, in_specs, args, flops, moved, scratch=()):
    return pl.pallas_call(
        kernel,
        out_shape=[jax.ShapeDtypeStruct(shape, dtype) for shape, dtype in outs],
        in_specs=in_specs,
        out_specs=[VMEM] * len(outs),
        scratch_shapes=list(scratch),
        compiler_params=pltpu.CompilerParams(vmem_limit_bytes=24 * 2**20),
        cost_estimate=pl.CostEstimate(flops=flops, bytes_accessed=moved, transcendentals=0),
    )(*args)


def prepare_kernel(dp, own_segs, my_dp, core, tokens, router, carry, own, *refs):
    firsts, seconds = refs[: dp - 1], refs[dp - 1 : 2 * dp - 2]
    blocks, routers, carries, sems = refs[2 * dp - 2 :]
    rows, depth = own.shape
    half = rows // 2
    quarter = half // 2
    extra = firsts[0].shape[0] - quarter
    experts = router.shape[0]
    columns = [pl.multiple_of((my_dp[0] ^ k) * depth, depth) for k in range(dp)]
    copies = [
        pltpu.make_async_copy(
            tokens.at[:, pl.ds(columns[k], depth)],
            own if k == 0 else blocks.at[k - 1],
            sems.at[k],
        )
        for k in range(dp)
    ]
    copies.append(pltpu.make_async_copy(router, routers, sems.at[dp]))
    copies.append(pltpu.make_async_copy(carry, carries, sems.at[dp + 1]))
    for copy in copies[dp:] + copies[:dp]:
        copy.start()
    member = lax.broadcasted_iota(jnp.int32, (extra, rows), 1) // SEG
    ones = member == lax.broadcasted_iota(jnp.int32, (extra, rows), 0)
    ones = jnp.where(ones, 1.0, 0.0).astype(BF16)
    start = pl.multiple_of(core[0] * half, quarter)
    for copy in copies:
        copy.wait()
    totals = [jnp.zeros((experts, depth), F32)] * (own_segs + 1)
    for k in range(dp):
        block = own[...] if k == 0 else blocks[k - 1]
        weight = routers[:, pl.ds(columns[k], depth)]
        means = jnp.dot(ones, block, preferred_element_type=F32) / SEG
        for j in range(own_segs):
            totals[j] += means[j : j + 1, :] * weight
        totals[own_segs] += carries[:, pl.ds(columns[k], depth)] * weight
        if k > 0:
            firsts[k - 1][:quarter] = blocks[k - 1, pl.ds(start, quarter), :]
            seconds[k - 1][...] = blocks[k - 1, pl.ds(start + quarter, quarter), :]
    lane = lax.broadcasted_iota(jnp.int32, (experts, LANES), 1)
    place = lane % experts == lax.broadcasted_iota(jnp.int32, (experts, LANES), 0)
    row = lax.broadcasted_iota(jnp.int32, (extra, LANES), 0)
    lane = lax.broadcasted_iota(jnp.int32, (extra, LANES), 1)
    logits = jnp.zeros((extra, LANES), F32)
    for j, total in enumerate(totals):
        column = jnp.sum(total, axis=1, keepdims=True)
        spread = jnp.sum(jnp.where(place, column, 0.0), axis=0, keepdims=True)
        logits = jnp.where(row == j, spread, logits)
    high = logits.astype(BF16).astype(F32)
    middle = (logits - high).astype(BF16).astype(F32)
    low = logits - high - middle
    terms = jnp.where(lane < experts, high, jnp.where(lane < 2 * experts, middle, low))
    terms = jnp.where(lane < 3 * experts, terms, 0.0).astype(BF16)
    for first in firsts:
        first[quarter:] = jnp.zeros((extra, depth), BF16)
        first[quarter:, :LANES] = terms


def read_table(piece, tokens, experts):
    lane = lax.broadcasted_iota(jnp.int32, (LANES, experts), 0)
    summed = lane % experts == lax.broadcasted_iota(jnp.int32, (LANES, experts), 1)
    summed = jnp.where(summed & (lane < 3 * experts), 1.0, 0.0).astype(BF16)
    return jnp.dot(piece[tokens:, :LANES], summed, preferred_element_type=F32)


def spread_probs(my_dp, tables, own_segs, experts, steps, block):
    raws = []
    for k in steps:
        for j in range(own_segs):
            prior = (my_dp ^ k) * own_segs + j - 1
            raw = tables[0][own_segs : own_segs + 1, :]
            for q, table in enumerate(tables):
                for i in range(own_segs):
                    here = (my_dp ^ q) * own_segs + i == prior
                    raw = jnp.where(here, table[i : i + 1, :], raw)
            raws.append(raw)
    logits = SOFT_CAP * jnp.tanh(jnp.concatenate(raws, axis=0) / SOFT_CAP)
    scores = jnp.exp(logits)
    probs = (scores / jnp.sum(scores, axis=1, keepdims=True)).astype(BF16).astype(F32)
    shape = (experts, experts * block)
    ahead = lax.broadcasted_iota(jnp.int32, shape, 1) // block
    spread = jnp.where(ahead == lax.broadcasted_iota(jnp.int32, shape, 0), 1.0, 0.0)
    wide = jnp.dot(probs, spread, preferred_element_type=F32)
    shape = (block, experts * block)
    diagonal = lax.broadcasted_iota(jnp.int32, shape, 1) % block == lax.broadcasted_iota(
        jnp.int32, shape, 0
    )
    return jnp.concatenate(
        [jnp.where(diagonal, wide[s : s + 1, :], 0.0) for s in range(len(raws))], axis=0
    ).astype(BF16)


def route_kernel(dp, own_segs, block, my_dp, *refs):
    pieces, mix = refs[:dp], refs[-1]
    experts = mix.shape[1] // block
    tables = [read_table(piece, own_segs * SEG // 4, experts) for piece in pieces]
    mix[...] = spread_probs(my_dp[0], tables, own_segs, experts, tuple(range(dp)), block)


def stack_kernel(dp, *refs):
    firsts, seconds, stacked = refs[: dp - 1], refs[dp - 1 : 2 * dp - 2], refs[-1]
    quarter = seconds[0].shape[0]
    for k in range(dp - 1):
        stacked[k, :quarter] = firsts[k][:quarter]
        stacked[k, quarter:] = seconds[k][...]


def merge_kernel(own_segs, mix, *refs):
    weights, outs = refs
    experts, rows, cols = weights[0].shape
    block = mix.shape[1] // experts
    for w, weight in enumerate(weights):
        for start in range(0, rows, block):
            tile = weight[:, start : start + block, :].reshape(experts * block, cols)
            out = jnp.dot(mix[...], tile, preferred_element_type=F32).astype(BF16)
            out = out.reshape(len(outs), own_segs, block, cols)
            at = w * rows + start
            for k in range(len(outs)):
                outs[k][:, at : at + block, :] = out[k]


def merge(mix, dp, own_segs, weights, flops):
    experts, rows, cols = weights[0].shape
    total = rows * len(weights)
    count = len(weights)

    def kernel(mix_ref, *refs):
        merge_kernel(own_segs, mix_ref, refs[:count], refs[-dp:])

    return call(
        kernel,
        [((own_segs, total, cols), BF16)] * dp,
        [VMEM] * (1 + count),
        (mix, *weights),
        flops,
        2 * total * cols * (experts + dp * own_segs),
    )


def preact_kernel(dp, core, own, brought, other, *refs):
    merged, outs, whole = refs[:dp], refs[dp : 2 * dp], refs[-1]
    half = own.shape[0] // 2
    near = pl.multiple_of(core[0] * half, half)
    far = pl.multiple_of((1 - core[0]) * half, half)
    for k in range(dp - 1, -1, -1):
        if k > 0:
            whole[k - 1, pl.ds(near, half), :] = brought[k - 1]
            whole[k - 1, pl.ds(far, half), :] = other[k - 1]
        for j in range(merged[k].shape[0]):
            rows = slice(j * SEG, (j + 1) * SEG)
            outs[k][j] = lax.dot_general(
                merged[k][j],
                own[rows, :] if k == 0 else whole[k - 1, rows, :],
                (((1,), (1,)), ((), ())),
                preferred_element_type=F32,
            ).astype(BF16)


def preact(core, own, brought, other, merged):
    dp = len(merged)
    own_segs, total, depth = merged[0].shape
    segs = dp * own_segs
    return call(
        functools.partial(preact_kernel, dp),
        [((own_segs, total, SEG), BF16)] * dp,
        [SMEM] + [VMEM] * (dp + 3),
        (core, own, brought, other, *merged),
        2 * segs * total * SEG * depth,
        2 * segs * (total * depth + SEG * depth + total * SEG),
        [pltpu.VMEM((dp - 1, own_segs * SEG, depth), BF16)],
    )


def down_columns(core, hidden, downs, mixed):
    cols = downs[0].shape[2]
    rows = mixed.shape[2]
    for j, part in enumerate(hidden):
        for k, down in enumerate(downs):
            out = lax.dot_general(
                part, down[j], (((0,), (0,)), ((), ())), preferred_element_type=F32
            ).astype(BF16)
            for i in range(SEG // rows):
                at = j * (SEG // rows) + i
                mixed[(at % 2) ^ core, at // 2, :, k * cols : (k + 1) * cols] = out[
                    i * rows : (i + 1) * rows
                ]


def first_kernel(dp, core, *refs):
    parts, downs, hidden, mixed = refs[:dp], refs[dp:-2], refs[-2], refs[-1]
    half = hidden.shape[1]
    kept = []
    for j in range(hidden.shape[0]):
        total = parts[0][j].astype(F32)
        for part in parts[1:]:
            total += part[j].astype(F32)
        gate, up = total[:half], total[half:]
        kept.append((gate / (1.0 + jnp.exp(-gate)) * up).astype(BF16))
        hidden[j] = kept[j]
    down_columns(core[0], kept, downs, mixed)


def second_kernel(count, core, hidden, *refs):
    kept = [hidden[j] for j in range(hidden.shape[0])]
    down_columns(core[0], kept, refs[:count], refs[-1])


def sum_kernel(*refs):
    total = refs[0][...].astype(F32)
    for piece in refs[1:-1]:
        total += piece[...].astype(F32)
    refs[-1][...] = total.astype(BF16)


def copy_kernel(source, target):
    target[...] = source[...]


def finish_kernel(groups, my_dp, early, *refs):
    out = refs[-1]
    total = refs[0][...].astype(F32)
    for piece in refs[1:-1]:
        total += piece[...].astype(F32)
    for value, steps in zip((early[...], total.astype(BF16)), groups):
        cols = value.shape[1] // len(steps)
        for k, step in enumerate(steps):
            at = pl.multiple_of((my_dp[0] ^ step) * cols, cols)
            out[:, pl.ds(at, cols)] = value[:, k * cols : (k + 1) * cols]


def tensor_sum_pieces(mixed, lines):
    my_line = lax.axis_index("tensor") // 2
    pair = mixed[0].astype(F32) + swap(mixed[1], "tensor", 1).astype(F32)
    pair = pair.astype(BF16)
    pieces = [lax.dynamic_index_in_dim(pair, my_line ^ k, 0, keepdims=False) for k in range(lines)]
    return [swap(pieces[k], "tensor", 2 * k) for k in range(lines - 1, 0, -1)] + [pieces[0]]


def keep(value):
    return call(copy_kernel, [(value.shape, BF16)], [VMEM], (value,), BESIDE, 0)[0]


def tensor_halve(mixed):
    mine, theirs = keep(mixed[0]), mixed[1]
    step, my_line = 1, lax.axis_index("tensor") // 2
    while mine.shape[0] > 1:
        total = mine.astype(F32) + swap(theirs, "tensor", step).astype(F32)
        total = total.astype(BF16).reshape(-1, 2, *mine.shape[1:])
        side = my_line % 2
        mine = lax.dynamic_index_in_dim(total, side, 1, keepdims=False)
        mine = keep(mine) if mine.shape[0] > 1 else mine
        theirs = lax.dynamic_index_in_dim(total, 1 - side, 1, keepdims=False)
        step, my_line = 2 * step, my_line // 2
    return [mine[0], swap(theirs[0], "tensor", step)]


def on_device(tokens, gate_weight, up_weight, down_weight, router_weight, carry_mean):
    dp = lax.axis_size("dp")
    tensor = lax.axis_size("tensor")
    lines = tensor // 2
    my_dp = lax.axis_index("dp").reshape(1)
    core = (lax.axis_index("tensor") % 2).reshape(1)
    own_rows, width = tokens.shape
    own_segs = own_rows // SEG
    experts, depth, hidden_count = gate_weight.shape
    cols = down_weight.shape[2]
    segs = dp * own_segs

    extra = -(-(own_segs + 1) // 16) * 16
    quarter = own_rows // 4
    own, *sends = call(
        functools.partial(prepare_kernel, dp, own_segs),
        [((own_rows, depth), BF16)]
        + [((quarter + extra, depth), BF16)] * (dp - 1)
        + [((quarter, depth), BF16)] * (dp - 1),
        [SMEM, SMEM, HBM, HBM, HBM],
        (my_dp, core, *map(in_hbm, (tokens, router_weight.T, carry_mean.reshape(1, width)))),
        BESIDE,
        4 * own_rows * width,
        [
            pltpu.VMEM((dp - 1, own_rows, depth), BF16),
            pltpu.VMEM((experts, width), F32),
            pltpu.VMEM((1, width), F32),
            pltpu.SemaphoreType.DMA((dp + 2,)),
        ],
    )
    firsts = [swap(sends[k - 1], "dp", k) for k in range(1, dp)]
    seconds = [swap(sends[dp + k - 2], "dp", k) for k in range(1, dp)]
    block = 32 if hidden_count % 32 == 0 else 16
    (mix,) = call(
        functools.partial(route_kernel, dp, own_segs, block),
        [((segs * block, experts * block), BF16)],
        [SMEM] + [VMEM] * dp,
        (my_dp, sends[0], *firsts),
        0,
        2 * own_rows * depth,
    )
    merged_down = merge(mix, dp, own_segs, (down_weight,), 2 * mix.size * down_weight.size // experts // block)
    downs = [block if k == 0 else swap(block, "dp", k) for k, block in enumerate(merged_down)]
    gate_up = (jnp.swapaxes(gate_weight, 1, 2), jnp.swapaxes(up_weight, 1, 2))
    (stacked,) = call(
        functools.partial(stack_kernel, dp),
        [((dp - 1, own_rows // 2, depth), BF16)],
        [VMEM] * (2 * dp - 2) + [ANY],
        (*firsts, *seconds, merged_down[0]),
        0,
        2 * own_rows * width,
    )
    other = swap(stacked, "tensor", 1)
    merged = merge(mix, dp, own_segs, gate_up, BESIDE)
    partial_pre = preact(core, own, stacked, other, merged)
    parts = [partial_pre[0]] + [swap(partial_pre[k], "dp", k) for k in range(1, dp)]

    rows = own_rows // tensor
    early, late = tuple(range(dp - 1)), (dp - 1,)
    flops = 2 * own_rows * hidden_count * cols
    hidden, mixed = call(
        functools.partial(first_kernel, dp),
        [((own_segs, hidden_count, SEG), BF16), ((2, lines, rows, len(early) * cols), BF16)],
        [SMEM] + [VMEM] * (dp + len(early)),
        (core, *parts, *[downs[k] for k in early]),
        flops * len(early),
        2 * (own_rows * hidden_count * dp * 2 + hidden_count * cols * len(early)),
    )
    early_pieces = tensor_sum_pieces(mixed, lines)
    (mixed,) = call(
        functools.partial(second_kernel, len(late)),
        [((2, lines, rows, len(late) * cols), BF16)],
        [SMEM] + [VMEM] * (1 + len(late)) + [ANY],
        (core, hidden, *[downs[k] for k in late], early_pieces[0]),
        flops * len(late),
        2 * (own_rows * hidden_count + hidden_count * cols * len(late)),
    )
    late_pieces = tensor_halve(mixed)
    (early_sum,) = call(
        sum_kernel,
        [(early_pieces[0].shape, BF16)],
        [VMEM] * lines,
        early_pieces,
        BESIDE,
        2 * rows * width * lines,
    )
    (out,) = call(
        functools.partial(finish_kernel, (early, late)),
        [((rows, width), BF16)],
        [SMEM] + [VMEM] * (1 + len(late_pieces)),
        (my_dp, early_sum, *late_pieces),
        rows * width * lines,
        2 * rows * width * (lines + 1),
    )
    return out


def solution(mesh):
    placed = (
        P("dp", None),
        P(None, "dp", "tensor"),
        P(None, "dp", "tensor"),
        P(None, "tensor", "dp"),
        P(),
        P(),
    )
    return jax.shard_map(
        on_device, mesh=mesh, in_specs=placed, out_specs=P(("dp", "tensor"), None), check_vma=False
    )
```

```python
import functools

import jax
import jax.numpy as jnp
from jax import lax
from jax.experimental import pallas as pl
from jax.experimental.pallas import tpu as pltpu
from jax.sharding import PartitionSpec as P

SEG = 256
SOFT_CAP = 8.0
VMEM = pl.BlockSpec(memory_space=pltpu.VMEM)
SMEM = pl.BlockSpec(memory_space=pltpu.SMEM)
F32 = jnp.float32
BF16 = jnp.bfloat16
LANES = 128
BESIDE = 10**10
HBM = pl.BlockSpec(memory_space=pltpu.HBM)
ANY = pl.BlockSpec(memory_space=pl.ANY)


def swap(value, axis, step):
    count = lax.axis_size(axis)
    return lax.ppermute(value, axis, [(i, i ^ step) for i in range(count)])


def in_hbm(value):
    return pltpu.with_memory_space_constraint(value, pltpu.HBM)


def call(kernel, outs, in_specs, args, flops, moved, scratch=()):
    return pl.pallas_call(
        kernel,
        out_shape=[jax.ShapeDtypeStruct(shape, dtype) for shape, dtype in outs],
        in_specs=in_specs,
        out_specs=[VMEM] * len(outs),
        scratch_shapes=list(scratch),
        compiler_params=pltpu.CompilerParams(vmem_limit_bytes=24 * 2**20),
        cost_estimate=pl.CostEstimate(flops=flops, bytes_accessed=moved, transcendentals=0),
    )(*args)


def prepare_kernel(dp, own_segs, my_dp, core, tokens, router, carry, own, *refs):
    firsts, seconds = refs[: dp - 1], refs[dp - 1 : 2 * dp - 2]
    blocks, routers, carries, sems = refs[2 * dp - 2 :]
    rows, depth = own.shape
    half = rows // 2
    quarter = half // 2
    extra = firsts[0].shape[0] - quarter
    experts = router.shape[0]
    columns = [pl.multiple_of((my_dp[0] ^ k) * depth, depth) for k in range(dp)]
    copies = [
        pltpu.make_async_copy(
            tokens.at[:, pl.ds(columns[k], depth)],
            own if k == 0 else blocks.at[k - 1],
            sems.at[k],
        )
        for k in range(dp)
    ]
    copies.append(pltpu.make_async_copy(router, routers, sems.at[dp]))
    copies.append(pltpu.make_async_copy(carry, carries, sems.at[dp + 1]))
    for copy in copies[dp:] + copies[:dp]:
        copy.start()
    member = lax.broadcasted_iota(jnp.int32, (extra, rows), 1) // SEG
    ones = member == lax.broadcasted_iota(jnp.int32, (extra, rows), 0)
    ones = jnp.where(ones, 1.0, 0.0).astype(BF16)
    start = pl.multiple_of(core[0] * half, quarter)
    for copy in copies:
        copy.wait()
    totals = [jnp.zeros((experts, depth), F32)] * (own_segs + 1)
    for k in range(dp):
        block = own[...] if k == 0 else blocks[k - 1]
        weight = routers[:, pl.ds(columns[k], depth)]
        means = jnp.dot(ones, block, preferred_element_type=F32) / SEG
        for j in range(own_segs):
            totals[j] += means[j : j + 1, :] * weight
        totals[own_segs] += carries[:, pl.ds(columns[k], depth)] * weight
        if k > 0:
            firsts[k - 1][:quarter] = blocks[k - 1, pl.ds(start, quarter), :]
            seconds[k - 1][...] = blocks[k - 1, pl.ds(start + quarter, quarter), :]
    lane = lax.broadcasted_iota(jnp.int32, (experts, LANES), 1)
    place = lane % experts == lax.broadcasted_iota(jnp.int32, (experts, LANES), 0)
    row = lax.broadcasted_iota(jnp.int32, (extra, LANES), 0)
    lane = lax.broadcasted_iota(jnp.int32, (extra, LANES), 1)
    logits = jnp.zeros((extra, LANES), F32)
    for j, total in enumerate(totals):
        column = jnp.sum(total, axis=1, keepdims=True)
        spread = jnp.sum(jnp.where(place, column, 0.0), axis=0, keepdims=True)
        logits = jnp.where(row == j, spread, logits)
    high = logits.astype(BF16).astype(F32)
    middle = (logits - high).astype(BF16).astype(F32)
    low = logits - high - middle
    terms = jnp.where(lane < experts, high, jnp.where(lane < 2 * experts, middle, low))
    terms = jnp.where(lane < 3 * experts, terms, 0.0).astype(BF16)
    for first in firsts:
        first[quarter:] = jnp.zeros((extra, depth), BF16)
        first[quarter:, :LANES] = terms


def read_table(piece, tokens, experts):
    lane = lax.broadcasted_iota(jnp.int32, (LANES, experts), 0)
    summed = lane % experts == lax.broadcasted_iota(jnp.int32, (LANES, experts), 1)
    summed = jnp.where(summed & (lane < 3 * experts), 1.0, 0.0).astype(BF16)
    return jnp.dot(piece[tokens:, :LANES], summed, preferred_element_type=F32)


def spread_probs(my_dp, tables, own_segs, experts, steps, block):
    raws = []
    for k in steps:
        for j in range(own_segs):
            prior = (my_dp ^ k) * own_segs + j - 1
            raw = tables[0][own_segs : own_segs + 1, :]
            for q, table in enumerate(tables):
                for i in range(own_segs):
                    here = (my_dp ^ q) * own_segs + i == prior
                    raw = jnp.where(here, table[i : i + 1, :], raw)
            raws.append(raw)
    logits = SOFT_CAP * jnp.tanh(jnp.concatenate(raws, axis=0) / SOFT_CAP)
    scores = jnp.exp(logits)
    probs = (scores / jnp.sum(scores, axis=1, keepdims=True)).astype(BF16).astype(F32)
    shape = (experts, experts * block)
    ahead = lax.broadcasted_iota(jnp.int32, shape, 1) // block
    spread = jnp.where(ahead == lax.broadcasted_iota(jnp.int32, shape, 0), 1.0, 0.0)
    wide = jnp.dot(probs, spread, preferred_element_type=F32)
    shape = (block, experts * block)
    diagonal = lax.broadcasted_iota(jnp.int32, shape, 1) % block == lax.broadcasted_iota(
        jnp.int32, shape, 0
    )
    return jnp.concatenate(
        [jnp.where(diagonal, wide[s : s + 1, :], 0.0) for s in range(len(raws))], axis=0
    ).astype(BF16)


def route_kernel(dp, own_segs, block, my_dp, *refs):
    pieces, mix = refs[:dp], refs[-1]
    experts = mix.shape[1] // block
    tables = [read_table(piece, own_segs * SEG // 4, experts) for piece in pieces]
    mix[...] = spread_probs(my_dp[0], tables, own_segs, experts, tuple(range(dp)), block)


def stack_kernel(dp, *refs):
    firsts, seconds, stacked = refs[: dp - 1], refs[dp - 1 : 2 * dp - 2], refs[-1]
    quarter = seconds[0].shape[0]
    for k in range(dp - 1):
        stacked[k, :quarter] = firsts[k][:quarter]
        stacked[k, quarter:] = seconds[k][...]


def merge_kernel(own_segs, mix, *refs):
    weights, outs = refs
    experts, rows, cols = weights[0].shape
    block = mix.shape[1] // experts
    for w, weight in enumerate(weights):
        for start in range(0, rows, block):
            tile = weight[:, start : start + block, :].reshape(experts * block, cols)
            out = jnp.dot(mix[...], tile, preferred_element_type=F32).astype(BF16)
            out = out.reshape(len(outs), own_segs, block, cols)
            at = w * rows + start
            for k in range(len(outs)):
                outs[k][:, at : at + block, :] = out[k]


def merge(mix, dp, own_segs, weights, flops):
    experts, rows, cols = weights[0].shape
    total = rows * len(weights)
    count = len(weights)

    def kernel(mix_ref, *refs):
        merge_kernel(own_segs, mix_ref, refs[:count], refs[-dp:])

    return call(
        kernel,
        [((own_segs, total, cols), BF16)] * dp,
        [VMEM] * (1 + count),
        (mix, *weights),
        flops,
        2 * total * cols * (experts + dp * own_segs),
    )


def preact_kernel(dp, core, own, brought, other, *refs):
    merged, outs, whole = refs[:dp], refs[dp : 2 * dp], refs[-1]
    half = own.shape[0] // 2
    near = pl.multiple_of(core[0] * half, half)
    far = pl.multiple_of((1 - core[0]) * half, half)
    for k in range(dp - 1, -1, -1):
        if k > 0:
            whole[k - 1, pl.ds(near, half), :] = brought[k - 1]
            whole[k - 1, pl.ds(far, half), :] = other[k - 1]
        for j in range(merged[k].shape[0]):
            rows = slice(j * SEG, (j + 1) * SEG)
            outs[k][j] = lax.dot_general(
                merged[k][j],
                own[rows, :] if k == 0 else whole[k - 1, rows, :],
                (((1,), (1,)), ((), ())),
                preferred_element_type=F32,
            ).astype(BF16)


def preact(core, own, brought, other, merged):
    dp = len(merged)
    own_segs, total, depth = merged[0].shape
    segs = dp * own_segs
    return call(
        functools.partial(preact_kernel, dp),
        [((own_segs, total, SEG), BF16)] * dp,
        [SMEM] + [VMEM] * (dp + 3),
        (core, own, brought, other, *merged),
        2 * segs * total * SEG * depth,
        2 * segs * (total * depth + SEG * depth + total * SEG),
        [pltpu.VMEM((dp - 1, own_segs * SEG, depth), BF16)],
    )


def down_columns(core, hidden, downs, mixed):
    cols = downs[0].shape[2]
    rows = mixed.shape[2]
    for j, part in enumerate(hidden):
        for k, down in enumerate(downs):
            out = lax.dot_general(
                part, down[j], (((0,), (0,)), ((), ())), preferred_element_type=F32
            ).astype(BF16)
            for i in range(SEG // rows):
                at = j * (SEG // rows) + i
                mixed[(at % 2) ^ core, at // 2, :, k * cols : (k + 1) * cols] = out[
                    i * rows : (i + 1) * rows
                ]


def first_kernel(dp, core, *refs):
    parts, downs, hidden, mixed = refs[:dp], refs[dp:-2], refs[-2], refs[-1]
    half = hidden.shape[1]
    kept = []
    for j in range(hidden.shape[0]):
        total = parts[0][j].astype(F32)
        for part in parts[1:]:
            total += part[j].astype(F32)
        gate, up = total[:half], total[half:]
        kept.append((gate / (1.0 + jnp.exp(-gate)) * up).astype(BF16))
        hidden[j] = kept[j]
    down_columns(core[0], kept, downs, mixed)


def second_kernel(count, core, hidden, *refs):
    kept = [hidden[j] for j in range(hidden.shape[0])]
    down_columns(core[0], kept, refs[:count], refs[-1])


def sum_kernel(*refs):
    total = refs[0][...].astype(F32)
    for piece in refs[1:-1]:
        total += piece[...].astype(F32)
    refs[-1][...] = total.astype(BF16)


def copy_kernel(source, target):
    target[...] = source[...]


def finish_kernel(groups, my_dp, early, *refs):
    out = refs[-1]
    total = refs[0][...].astype(F32)
    for piece in refs[1:-1]:
        total += piece[...].astype(F32)
    for value, steps in zip((early[...], total.astype(BF16)), groups):
        cols = value.shape[1] // len(steps)
        for k, step in enumerate(steps):
            at = pl.multiple_of((my_dp[0] ^ step) * cols, cols)
            out[:, pl.ds(at, cols)] = value[:, k * cols : (k + 1) * cols]


def tensor_sum_pieces(mixed, lines):
    my_line = lax.axis_index("tensor") // 2
    pair = mixed[0].astype(F32) + swap(mixed[1], "tensor", 1).astype(F32)
    pair = pair.astype(BF16)
    pieces = [lax.dynamic_index_in_dim(pair, my_line ^ k, 0, keepdims=False) for k in range(lines)]
    return [swap(pieces[k], "tensor", 2 * k) for k in range(lines - 1, 0, -1)] + [pieces[0]]


def keep(value):
    return call(copy_kernel, [(value.shape, BF16)], [VMEM], (value,), BESIDE, 0)[0]


def tensor_halve(mixed):
    mine, theirs = keep(mixed[0]), mixed[1]
    step, my_line = 1, lax.axis_index("tensor") // 2
    while mine.shape[0] > 1:
        total = mine.astype(F32) + swap(theirs, "tensor", step).astype(F32)
        total = total.astype(BF16).reshape(-1, 2, *mine.shape[1:])
        side = my_line % 2
        mine = lax.dynamic_index_in_dim(total, side, 1, keepdims=False)
        mine = keep(mine) if mine.shape[0] > 1 else mine
        theirs = lax.dynamic_index_in_dim(total, 1 - side, 1, keepdims=False)
        step, my_line = 2 * step, my_line // 2
    return [mine[0], swap(theirs[0], "tensor", step)]


def on_device(tokens, gate_weight, up_weight, down_weight, router_weight, carry_mean):
    dp = lax.axis_size("dp")
    tensor = lax.axis_size("tensor")
    lines = tensor // 2
    my_dp = lax.axis_index("dp").reshape(1)
    core = (lax.axis_index("tensor") % 2).reshape(1)
    own_rows, width = tokens.shape
    own_segs = own_rows // SEG
    experts, depth, hidden_count = gate_weight.shape
    cols = down_weight.shape[2]
    segs = dp * own_segs

    extra = -(-(own_segs + 1) // 16) * 16
    quarter = own_rows // 4
    own, *sends = call(
        functools.partial(prepare_kernel, dp, own_segs),
        [((own_rows, depth), BF16)]
        + [((quarter + extra, depth), BF16)] * (dp - 1)
        + [((quarter, depth), BF16)] * (dp - 1),
        [SMEM, SMEM, HBM, HBM, HBM],
        (my_dp, core, *map(in_hbm, (tokens, router_weight.T, carry_mean.reshape(1, width)))),
        BESIDE,
        4 * own_rows * width,
        [
            pltpu.VMEM((dp - 1, own_rows, depth), BF16),
            pltpu.VMEM((experts, width), F32),
            pltpu.VMEM((1, width), F32),
            pltpu.SemaphoreType.DMA((dp + 2,)),
        ],
    )
    firsts = [swap(sends[k - 1], "dp", k) for k in range(1, dp)]
    seconds = [swap(sends[dp + k - 2], "dp", k) for k in range(1, dp)]
    block = 32 if hidden_count % 32 == 0 else 16
    (mix,) = call(
        functools.partial(route_kernel, dp, own_segs, block),
        [((segs * block, experts * block), BF16)],
        [SMEM] + [VMEM] * dp,
        (my_dp, sends[0], *firsts),
        0,
        2 * own_rows * depth,
    )
    merged_down = merge(mix, dp, own_segs, (down_weight,), 2 * mix.size * down_weight.size // experts // block)
    downs = [block if k == 0 else swap(block, "dp", k) for k, block in enumerate(merged_down)]
    gate_up = (jnp.swapaxes(gate_weight, 1, 2), jnp.swapaxes(up_weight, 1, 2))
    (stacked,) = call(
        functools.partial(stack_kernel, dp),
        [((dp - 1, own_rows // 2, depth), BF16)],
        [VMEM] * (2 * dp - 2) + [ANY],
        (*firsts, *seconds, merged_down[1]),
        0,
        2 * own_rows * width,
    )
    other = swap(stacked, "tensor", 1)
    merged = merge(mix, dp, own_segs, gate_up, BESIDE)
    partial_pre = preact(core, own, stacked, other, merged)
    parts = [partial_pre[0]] + [swap(partial_pre[k], "dp", k) for k in range(1, dp)]

    rows = own_rows // tensor
    early, late = tuple(range(dp - 1)), (dp - 1,)
    flops = 2 * own_rows * hidden_count * cols
    hidden, mixed = call(
        functools.partial(first_kernel, dp),
        [((own_segs, hidden_count, SEG), BF16), ((2, lines, rows, len(early) * cols), BF16)],
        [SMEM] + [VMEM] * (dp + len(early)),
        (core, *parts, *[downs[k] for k in early]),
        flops * len(early),
        2 * (own_rows * hidden_count * dp * 2 + hidden_count * cols * len(early)),
    )
    early_pieces = tensor_sum_pieces(mixed, lines)
    (mixed,) = call(
        functools.partial(second_kernel, len(late)),
        [((2, lines, rows, len(late) * cols), BF16)],
        [SMEM] + [VMEM] * (1 + len(late)) + [ANY],
        (core, hidden, *[downs[k] for k in late], early_pieces[0]),
        flops * len(late),
        2 * (own_rows * hidden_count + hidden_count * cols * len(late)),
    )
    late_pieces = tensor_halve(mixed)
    (early_sum,) = call(
        sum_kernel,
        [(early_pieces[0].shape, BF16)],
        [VMEM] * lines,
        early_pieces,
        BESIDE,
        2 * rows * width * lines,
    )
    (out,) = call(
        functools.partial(finish_kernel, (early, late)),
        [((rows, width), BF16)],
        [SMEM] + [VMEM] * (1 + len(late_pieces)),
        (my_dp, early_sum, *late_pieces),
        rows * width * lines,
        2 * rows * width * (lines + 1),
    )
    return out


def solution(mesh):
    placed = (
        P("dp", None),
        P(None, "dp", "tensor"),
        P(None, "dp", "tensor"),
        P(None, "tensor", "dp"),
        P(),
        P(),
    )
    return jax.shard_map(
        on_device, mesh=mesh, in_specs=placed, out_specs=P(("dp", "tensor"), None), check_vma=False
    )
```

```python
import functools

import jax
import jax.numpy as jnp
from jax import lax
from jax.experimental import pallas as pl
from jax.experimental.pallas import tpu as pltpu
from jax.sharding import PartitionSpec as P

SEG = 256
SOFT_CAP = 8.0
VMEM = pl.BlockSpec(memory_space=pltpu.VMEM)
SMEM = pl.BlockSpec(memory_space=pltpu.SMEM)
F32 = jnp.float32
BF16 = jnp.bfloat16
LANES = 128
BESIDE = 10**10
HBM = pl.BlockSpec(memory_space=pltpu.HBM)
ANY = pl.BlockSpec(memory_space=pl.ANY)


def swap(value, axis, step):
    count = lax.axis_size(axis)
    return lax.ppermute(value, axis, [(i, i ^ step) for i in range(count)])


def in_hbm(value):
    return pltpu.with_memory_space_constraint(value, pltpu.HBM)


def call(kernel, outs, in_specs, args, flops, moved, scratch=()):
    return pl.pallas_call(
        kernel,
        out_shape=[jax.ShapeDtypeStruct(shape, dtype) for shape, dtype in outs],
        in_specs=in_specs,
        out_specs=[VMEM] * len(outs),
        scratch_shapes=list(scratch),
        compiler_params=pltpu.CompilerParams(vmem_limit_bytes=24 * 2**20),
        cost_estimate=pl.CostEstimate(flops=flops, bytes_accessed=moved, transcendentals=0),
    )(*args)


def prepare_kernel(dp, own_segs, my_dp, core, tokens, router, carry, own, *refs):
    firsts, seconds = refs[: dp - 1], refs[dp - 1 : 2 * dp - 2]
    blocks, routers, carries, sems = refs[2 * dp - 2 :]
    rows, depth = own.shape
    half = rows // 2
    quarter = half // 2
    extra = firsts[0].shape[0] - quarter
    experts = router.shape[0]
    columns = [pl.multiple_of((my_dp[0] ^ k) * depth, depth) for k in range(dp)]
    copies = [
        pltpu.make_async_copy(
            tokens.at[:, pl.ds(columns[k], depth)],
            own if k == 0 else blocks.at[k - 1],
            sems.at[k],
        )
        for k in range(dp)
    ]
    copies.append(pltpu.make_async_copy(router, routers, sems.at[dp]))
    copies.append(pltpu.make_async_copy(carry, carries, sems.at[dp + 1]))
    for copy in copies[dp:] + copies[:dp]:
        copy.start()
    member = lax.broadcasted_iota(jnp.int32, (extra, rows), 1) // SEG
    ones = member == lax.broadcasted_iota(jnp.int32, (extra, rows), 0)
    ones = jnp.where(ones, 1.0, 0.0).astype(BF16)
    start = pl.multiple_of(core[0] * half, quarter)
    for copy in copies:
        copy.wait()
    totals = [jnp.zeros((experts, depth), F32)] * (own_segs + 1)
    for k in range(dp):
        block = own[...] if k == 0 else blocks[k - 1]
        weight = routers[:, pl.ds(columns[k], depth)]
        means = jnp.dot(ones, block, preferred_element_type=F32) / SEG
        for j in range(own_segs):
            totals[j] += means[j : j + 1, :] * weight
        totals[own_segs] += carries[:, pl.ds(columns[k], depth)] * weight
        if k > 0:
            firsts[k - 1][:quarter] = blocks[k - 1, pl.ds(start, quarter), :]
            seconds[k - 1][...] = blocks[k - 1, pl.ds(start + quarter, quarter), :]
    lane = lax.broadcasted_iota(jnp.int32, (experts, LANES), 1)
    place = lane % experts == lax.broadcasted_iota(jnp.int32, (experts, LANES), 0)
    row = lax.broadcasted_iota(jnp.int32, (extra, LANES), 0)
    lane = lax.broadcasted_iota(jnp.int32, (extra, LANES), 1)
    logits = jnp.zeros((extra, LANES), F32)
    for j, total in enumerate(totals):
        column = jnp.sum(total, axis=1, keepdims=True)
        spread = jnp.sum(jnp.where(place, column, 0.0), axis=0, keepdims=True)
        logits = jnp.where(row == j, spread, logits)
    high = logits.astype(BF16).astype(F32)
    middle = (logits - high).astype(BF16).astype(F32)
    low = logits - high - middle
    terms = jnp.where(lane < experts, high, jnp.where(lane < 2 * experts, middle, low))
    terms = jnp.where(lane < 3 * experts, terms, 0.0).astype(BF16)
    for first in firsts:
        first[quarter:] = jnp.zeros((extra, depth), BF16)
        first[quarter:, :LANES] = terms


def read_table(piece, tokens, experts):
    lane = lax.broadcasted_iota(jnp.int32, (LANES, experts), 0)
    summed = lane % experts == lax.broadcasted_iota(jnp.int32, (LANES, experts), 1)
    summed = jnp.where(summed & (lane < 3 * experts), 1.0, 0.0).astype(BF16)
    return jnp.dot(piece[tokens:, :LANES], summed, preferred_element_type=F32)


def spread_probs(my_dp, tables, own_segs, experts, steps, block):
    raws = []
    for k in steps:
        for j in range(own_segs):
            prior = (my_dp ^ k) * own_segs + j - 1
            raw = tables[0][own_segs : own_segs + 1, :]
            for q, table in enumerate(tables):
                for i in range(own_segs):
                    here = (my_dp ^ q) * own_segs + i == prior
                    raw = jnp.where(here, table[i : i + 1, :], raw)
            raws.append(raw)
    logits = SOFT_CAP * jnp.tanh(jnp.concatenate(raws, axis=0) / SOFT_CAP)
    scores = jnp.exp(logits)
    probs = (scores / jnp.sum(scores, axis=1, keepdims=True)).astype(BF16).astype(F32)
    shape = (experts, experts * block)
    ahead = lax.broadcasted_iota(jnp.int32, shape, 1) // block
    spread = jnp.where(ahead == lax.broadcasted_iota(jnp.int32, shape, 0), 1.0, 0.0)
    wide = jnp.dot(probs, spread, preferred_element_type=F32)
    shape = (block, experts * block)
    diagonal = lax.broadcasted_iota(jnp.int32, shape, 1) % block == lax.broadcasted_iota(
        jnp.int32, shape, 0
    )
    return jnp.concatenate(
        [jnp.where(diagonal, wide[s : s + 1, :], 0.0) for s in range(len(raws))], axis=0
    ).astype(BF16)


def route_kernel(dp, own_segs, block, my_dp, *refs):
    pieces, mix = refs[:dp], refs[-1]
    experts = mix.shape[1] // block
    tables = [read_table(piece, own_segs * SEG // 4, experts) for piece in pieces]
    mix[...] = spread_probs(my_dp[0], tables, own_segs, experts, tuple(range(dp)), block)


def stack_kernel(dp, *refs):
    firsts, seconds, stacked = refs[: dp - 1], refs[dp - 1 : 2 * dp - 2], refs[-1]
    quarter = seconds[0].shape[0]
    for k in range(dp - 1):
        stacked[k, :quarter] = firsts[k][:quarter]
        stacked[k, quarter:] = seconds[k][...]


def merge_kernel(own_segs, mix, *refs):
    weights, outs = refs
    experts, rows, cols = weights[0].shape
    block = mix.shape[1] // experts
    for w, weight in enumerate(weights):
        for start in range(0, rows, block):
            tile = weight[:, start : start + block, :].reshape(experts * block, cols)
            out = jnp.dot(mix[...], tile, preferred_element_type=F32).astype(BF16)
            out = out.reshape(len(outs), own_segs, block, cols)
            at = w * rows + start
            for k in range(len(outs)):
                outs[k][:, at : at + block, :] = out[k]


def merge(mix, dp, own_segs, weights, flops):
    experts, rows, cols = weights[0].shape
    total = rows * len(weights)
    count = len(weights)

    def kernel(mix_ref, *refs):
        merge_kernel(own_segs, mix_ref, refs[:count], refs[-dp:])

    return call(
        kernel,
        [((own_segs, total, cols), BF16)] * dp,
        [VMEM] * (1 + count),
        (mix, *weights),
        flops,
        2 * total * cols * (experts + dp * own_segs),
    )


def preact_kernel(dp, core, own, brought, other, *refs):
    merged, outs, whole = refs[:dp], refs[dp : 2 * dp], refs[-1]
    half = own.shape[0] // 2
    near = pl.multiple_of(core[0] * half, half)
    far = pl.multiple_of((1 - core[0]) * half, half)
    for k in range(dp - 1, -1, -1):
        if k > 0:
            whole[k - 1, pl.ds(near, half), :] = brought[k - 1]
            whole[k - 1, pl.ds(far, half), :] = other[k - 1]
        for j in range(merged[k].shape[0]):
            rows = slice(j * SEG, (j + 1) * SEG)
            outs[k][j] = lax.dot_general(
                merged[k][j],
                own[rows, :] if k == 0 else whole[k - 1, rows, :],
                (((1,), (1,)), ((), ())),
                preferred_element_type=F32,
            ).astype(BF16)


def preact(core, own, brought, other, merged):
    dp = len(merged)
    own_segs, total, depth = merged[0].shape
    segs = dp * own_segs
    return call(
        functools.partial(preact_kernel, dp),
        [((own_segs, total, SEG), BF16)] * dp,
        [SMEM] + [VMEM] * (dp + 3),
        (core, own, brought, other, *merged),
        2 * segs * total * SEG * depth,
        2 * segs * (total * depth + SEG * depth + total * SEG),
        [pltpu.VMEM((dp - 1, own_segs * SEG, depth), BF16)],
    )


def down_columns(core, hidden, downs, mixed):
    cols = downs[0].shape[2]
    rows = mixed.shape[2]
    for j, part in enumerate(hidden):
        for k, down in enumerate(downs):
            out = lax.dot_general(
                part, down[j], (((0,), (0,)), ((), ())), preferred_element_type=F32
            ).astype(BF16)
            for i in range(SEG // rows):
                at = j * (SEG // rows) + i
                mixed[(at % 2) ^ core, at // 2, :, k * cols : (k + 1) * cols] = out[
                    i * rows : (i + 1) * rows
                ]


def first_kernel(dp, core, *refs):
    parts, downs, hidden, mixed = refs[:dp], refs[dp:-2], refs[-2], refs[-1]
    half = hidden.shape[1]
    kept = []
    for j in range(hidden.shape[0]):
        total = parts[0][j].astype(F32)
        for part in parts[1:]:
            total += part[j].astype(F32)
        gate, up = total[:half], total[half:]
        kept.append((gate / (1.0 + jnp.exp(-gate)) * up).astype(BF16))
        hidden[j] = kept[j]
    down_columns(core[0], kept, downs, mixed)


def second_kernel(count, core, hidden, *refs):
    kept = [hidden[j] for j in range(hidden.shape[0])]
    down_columns(core[0], kept, refs[:count], refs[-1])


def sum_kernel(*refs):
    total = refs[0][...].astype(F32)
    for piece in refs[1:-1]:
        total += piece[...].astype(F32)
    refs[-1][...] = total.astype(BF16)


def copy_kernel(source, target):
    target[...] = source[...]


def finish_kernel(groups, my_dp, early, *refs):
    out = refs[-1]
    total = refs[0][...].astype(F32)
    for piece in refs[1:-1]:
        total += piece[...].astype(F32)
    for value, steps in zip((early[...], total.astype(BF16)), groups):
        cols = value.shape[1] // len(steps)
        for k, step in enumerate(steps):
            at = pl.multiple_of((my_dp[0] ^ step) * cols, cols)
            out[:, pl.ds(at, cols)] = value[:, k * cols : (k + 1) * cols]


def tensor_sum_pieces(mixed, lines):
    my_line = lax.axis_index("tensor") // 2
    pair = mixed[0].astype(F32) + swap(mixed[1], "tensor", 1).astype(F32)
    pair = pair.astype(BF16)
    pieces = [lax.dynamic_index_in_dim(pair, my_line ^ k, 0, keepdims=False) for k in range(lines)]
    return [swap(pieces[k], "tensor", 2 * k) for k in range(lines - 1, 0, -1)] + [pieces[0]]


def keep(value):
    return call(copy_kernel, [(value.shape, BF16)], [VMEM], (value,), BESIDE, 0)[0]


def tensor_halve(mixed):
    mine, theirs = keep(mixed[0]), mixed[1]
    step, my_line = 1, lax.axis_index("tensor") // 2
    while mine.shape[0] > 1:
        total = mine.astype(F32) + swap(theirs, "tensor", step).astype(F32)
        total = total.astype(BF16).reshape(-1, 2, *mine.shape[1:])
        side = my_line % 2
        mine = lax.dynamic_index_in_dim(total, side, 1, keepdims=False)
        mine = keep(mine) if mine.shape[0] > 1 else mine
        theirs = lax.dynamic_index_in_dim(total, 1 - side, 1, keepdims=False)
        step, my_line = 2 * step, my_line // 2
    return [mine[0], swap(theirs[0], "tensor", step)]


def on_device(tokens, gate_weight, up_weight, down_weight, router_weight, carry_mean):
    dp = lax.axis_size("dp")
    tensor = lax.axis_size("tensor")
    lines = tensor // 2
    my_dp = lax.axis_index("dp").reshape(1)
    core = (lax.axis_index("tensor") % 2).reshape(1)
    own_rows, width = tokens.shape
    own_segs = own_rows // SEG
    experts, depth, hidden_count = gate_weight.shape
    cols = down_weight.shape[2]
    segs = dp * own_segs

    extra = -(-(own_segs + 1) // 16) * 16
    quarter = own_rows // 4
    own, *sends = call(
        functools.partial(prepare_kernel, dp, own_segs),
        [((own_rows, depth), BF16)]
        + [((quarter + extra, depth), BF16)] * (dp - 1)
        + [((quarter, depth), BF16)] * (dp - 1),
        [SMEM, SMEM, HBM, HBM, HBM],
        (my_dp, core, *map(in_hbm, (tokens, router_weight.T, carry_mean.reshape(1, width)))),
        BESIDE,
        4 * own_rows * width,
        [
            pltpu.VMEM((dp - 1, own_rows, depth), BF16),
            pltpu.VMEM((experts, width), F32),
            pltpu.VMEM((1, width), F32),
            pltpu.SemaphoreType.DMA((dp + 2,)),
        ],
    )
    firsts = [swap(sends[k - 1], "dp", k) for k in range(1, dp)]
    seconds = [swap(sends[dp + k - 2], "dp", k) for k in range(1, dp)]
    block = 32 if hidden_count % 32 == 0 else 16
    (mix,) = call(
        functools.partial(route_kernel, dp, own_segs, block),
        [((segs * block, experts * block), BF16)],
        [SMEM] + [VMEM] * dp,
        (my_dp, sends[0], *firsts),
        0,
        2 * own_rows * depth,
    )
    merged_down = merge(mix, dp, own_segs, (down_weight,), 2 * mix.size * down_weight.size // experts // block)
    downs = [block if k == 0 else swap(block, "dp", k) for k, block in enumerate(merged_down)]
    gate_up = (jnp.swapaxes(gate_weight, 1, 2), jnp.swapaxes(up_weight, 1, 2))
    (stacked,) = call(
        functools.partial(stack_kernel, dp),
        [((dp - 1, own_rows // 2, depth), BF16)],
        [VMEM] * (2 * dp - 2) + [ANY] * (dp - 2),
        (*firsts, *seconds, *merged_down[1:-1]),
        0,
        2 * own_rows * width,
    )
    other = swap(stacked, "tensor", 1)
    merged = merge(mix, dp, own_segs, gate_up, BESIDE)
    partial_pre = preact(core, own, stacked, other, merged)
    parts = [partial_pre[0]] + [swap(partial_pre[k], "dp", k) for k in range(1, dp)]

    rows = own_rows // tensor
    early, late = tuple(range(dp - 1)), (dp - 1,)
    flops = 2 * own_rows * hidden_count * cols
    hidden, mixed = call(
        functools.partial(first_kernel, dp),
        [((own_segs, hidden_count, SEG), BF16), ((2, lines, rows, len(early) * cols), BF16)],
        [SMEM] + [VMEM] * (dp + len(early)),
        (core, *parts, *[downs[k] for k in early]),
        flops * len(early),
        2 * (own_rows * hidden_count * dp * 2 + hidden_count * cols * len(early)),
    )
    early_pieces = tensor_sum_pieces(mixed, lines)
    (mixed,) = call(
        functools.partial(second_kernel, len(late)),
        [((2, lines, rows, len(late) * cols), BF16)],
        [SMEM] + [VMEM] * (1 + len(late)) + [ANY],
        (core, hidden, *[downs[k] for k in late], early_pieces[0]),
        flops * len(late),
        2 * (own_rows * hidden_count + hidden_count * cols * len(late)),
    )
    late_pieces = tensor_halve(mixed)
    (early_sum,) = call(
        sum_kernel,
        [(early_pieces[0].shape, BF16)],
        [VMEM] * lines,
        early_pieces,
        BESIDE,
        2 * rows * width * lines,
    )
    (out,) = call(
        functools.partial(finish_kernel, (early, late)),
        [((rows, width), BF16)],
        [SMEM] + [VMEM] * (1 + len(late_pieces)),
        (my_dp, early_sum, *late_pieces),
        rows * width * lines,
        2 * rows * width * (lines + 1),
    )
    return out


def solution(mesh):
    placed = (
        P("dp", None),
        P(None, "dp", "tensor"),
        P(None, "dp", "tensor"),
        P(None, "tensor", "dp"),
        P(),
        P(),
    )
    return jax.shard_map(
        on_device, mesh=mesh, in_specs=placed, out_specs=P(("dp", "tensor"), None), check_vma=False
    )
```
